32 devices in a mesh: dp: 16 (over z, y, core), mlp: 2 (over x).
Axes of the slice: x: 2, y: 2, z: 4, core: 2. Of those that a mesh axis runs over, the one named last changes fastest.
Arguments:
- tokens: bfloat16 [125440, 768], P(('dp', 'mlp')), may hold values from -6 to 6
- window_extent: int32 [640, 2], P(('dp', 'mlp')), may hold values from 0 to 14, as said below
- ln1_gain: float32 [768], replicated, may hold values from 0.5 to 1.5
- ln1_bias: float32 [768], replicated, may hold values from -3 to 3
- qkv_weight: bfloat16 [768, 2304], replicated, may hold values from -0.21875 to 0.21875
- query_bias: float32 [768], replicated, may hold values from -3 to 3
- value_bias: float32 [768], replicated, may hold values from -3 to 3
- rel_h: float32 [27, 64], replicated, may hold values from -0.6 to 0.6
- rel_w: float32 [27, 64], replicated, may hold values from -0.6 to 0.6
- proj_weight: bfloat16 [768, 768], replicated, may hold values from -0.875 to 0.875
- proj_bias: float32 [768], replicated, may hold values from -3 to 3
- ln2_gain: float32 [768], replicated, may hold values from 0.5 to 1.5
- ln2_bias: float32 [768], replicated, may hold values from -3 to 3
- up_weight: bfloat16 [768, 3072], P(None, 'mlp'), may hold values from -0.21875 to 0.21875
- up_bias: float32 [3072], P('mlp'), may hold values from -3 to 3
- down_weight: bfloat16 [768, 3072], P(None, 'mlp'), may hold values from -0.109375 to 0.109375
- down_bias: float32 [768], replicated, may hold values from -3 to 3
- grad_out: bfloat16 [125440, 768], P(('dp', 'mlp')), may hold values from -6 to 6
Outputs:
- output: bfloat16 [125440, 768], P(('dp', 'mlp'))
- grad_tokens: bfloat16 [125440, 768], P(('dp', 'mlp'))
- grad_ln1_gain: float32 [768], replicated
- grad_ln1_bias: float32 [768], replicated
- grad_qkv_weight: float32 [768, 2304], P('dp', 'mlp')
- grad_query_bias: float32 [768], replicated
- grad_value_bias: float32 [768], replicated
- grad_rel_h: float32 [27, 64], replicated
- grad_rel_w: float32 [27, 64], replicated
- grad_proj_weight: float32 [768, 768], P('dp', 'mlp')
- grad_proj_bias: float32 [768], replicated
- grad_ln2_gain: float32 [768], replicated
- grad_ln2_bias: float32 [768], replicated
- grad_up_weight: float32 [768, 3072], P('dp', 'mlp')
- grad_up_bias: float32 [3072], replicated
- grad_down_weight: float32 [768, 3072], P('dp', 'mlp')
- grad_down_bias: float32 [768], replicated
The draws below stay inside these ranges and needn't reach their ends.
Inputs may be any that keep to these rules, and one draw needn't show every extreme that they name: `window_extent`: each aligned group of 40 window slots (one index of dp) holds whole images placed in order from its first slot; an image of 48, 64 or 80 patches a side takes 16, 25 or 36 slots in row-major window order, with extents 14 except in its last window row or column (6, 8 or 10); slots after the group's last image have extents 0 and 0.
All inputs are finite; a program needn't handle non-finite values.
Results may differ from the reference program's by a relative error of at most 0.018.
Values may be sent and summed in bfloat16 or wider, within the bound.
No kernel may reach another device: no remote copies, remote signals or barrier semaphores. Data moves between devices by JAX's collectives and lax.ppermute only.
A program may use at most 960 MiB of HBM per device.

```python
import jax
import jax.numpy as jnp
from jax import lax

D = 768
HEADS = 12
HEAD_DIM = 64
FF = 3072
WIN = 14
GROUP_WIN = 40
WINDOWS = 640
TOKENS = 125440


def draw_window_extent(key, part):
    groups = WINDOWS // GROUP_WIN
    candidates = GROUP_WIN // 16 + 1
    image_kind = jax.random.randint(key, (groups, candidates), 0, 3)
    grid_side = 48 + 16 * image_kind
    window_side = 4 + image_kind
    window_total = window_side * window_side
    ending = jnp.cumsum(window_total, axis=1)
    beginning = ending - window_total
    placed = ending <= GROUP_WIN
    slots = jnp.arange(GROUP_WIN)
    inside = placed[:, None, :] & (beginning[:, None, :] <= slots[None, :, None]) & (slots[None, :, None] < ending[:, None, :])
    inside_int = inside.astype(jnp.int32)
    occupied = jnp.sum(inside_int, axis=2)
    local_slot = jnp.sum(inside_int * (slots[None, :, None] - beginning[:, None, :]), axis=2)
    grid_here = jnp.sum(inside_int * grid_side[:, None, :], axis=2)
    side_here = jnp.maximum(jnp.sum(inside_int * window_side[:, None, :], axis=2), 1)
    window_row = local_slot // side_here
    window_col = local_slot % side_here
    extent_rows = jnp.where(occupied > 0, jnp.minimum(WIN, grid_here - WIN * window_row), 0)
    extent_cols = jnp.where(occupied > 0, jnp.minimum(WIN, grid_here - WIN * window_col), 0)
    return jnp.stack([extent_rows, extent_cols], axis=-1).reshape(WINDOWS, 2).astype(jnp.int32)


def levels(own_key, shape, split, least, high):
    def one(axis_at, parts):
        heights = jax.random.uniform(jax.random.fold_in(jax.random.fold_in(own_key, 6), axis_at), (parts,), jnp.float32, least / len(split), high / len(split))
        return jnp.repeat(jnp.exp(heights), shape[axis_at] // parts).reshape((-1,) + (1,) * (len(shape) - axis_at - 1))

    factor_of = one(*split[0])
    for cut in split[1:]:
        factor_of = factor_of * one(*cut)
    return factor_of


def bell_draw(key, shape, scale, limit, pieces=(), kind=jnp.bfloat16):
    level = levels(key, shape, pieces, -0.22, 0.18) if pieces else 1.0
    values = jax.random.normal(key, shape, jnp.float32) * scale * level
    return jnp.minimum(jnp.maximum(values, -limit), limit).astype(kind)


def setup_inputs(seed: int = 0) -> dict:
    seeds = jax.random.split(jax.random.key(seed), 19)
    return {
        "tokens": bell_draw(seeds[0], (TOKENS, D), 1.0, 6.0, ((0, 32),)),
        "window_extent": draw_window_extent(jax.random.fold_in(seeds[18], 71), 0),
        "ln1_gain": jnp.clip(1.0 + 0.1 * jax.random.normal(seeds[2], (D,), jnp.float32), 0.5, 1.5),
        "ln1_bias": bell_draw(seeds[3], (D,), 0.5, 3.0, (), jnp.float32),
        "qkv_weight": bell_draw(seeds[4], (D, 3 * D), D ** -0.5, 0.21875),
        "query_bias": bell_draw(seeds[5], (D,), 0.5, 3.0, (), jnp.float32),
        "value_bias": bell_draw(seeds[6], (D,), 0.5, 3.0, (), jnp.float32),
        "rel_h": bell_draw(seeds[7], (2 * WIN - 1, HEAD_DIM), 0.1, 0.6, (), jnp.float32),
        "rel_w": bell_draw(seeds[8], (2 * WIN - 1, HEAD_DIM), 0.1, 0.6, (), jnp.float32),
        "proj_weight": bell_draw(seeds[9], (D, D), (D // 16) ** -0.5, 0.875),
        "proj_bias": bell_draw(seeds[10], (D,), 0.5, 3.0, (), jnp.float32),
        "ln2_gain": jnp.clip(1.0 + 0.1 * jax.random.normal(seeds[11], (D,), jnp.float32), 0.5, 1.5),
        "ln2_bias": bell_draw(seeds[12], (D,), 0.5, 3.0, (), jnp.float32),
        "up_weight": bell_draw(seeds[13], (D, FF), D ** -0.5, 0.21875, ((1, 2),)),
        "up_bias": bell_draw(seeds[14], (FF,), 0.5, 3.0, ((0, 2),), jnp.float32),
        "down_weight": bell_draw(seeds[15], (D, FF), FF ** -0.5, 0.109375, ((1, 2),)),
        "down_bias": bell_draw(seeds[16], (D,), 0.5, 3.0, (), jnp.float32),
        "grad_out": bell_draw(seeds[17], (TOKENS, D), 1.0, 6.0, ((0, 32),)),
    }


@jax.custom_vjp
def low(v):
    return lax.optimization_barrier(v.astype(jnp.bfloat16)).astype(jnp.float32)

@jax.custom_vjp
def low_back(v):
    return v

def low_keep(v):
    return (low(v), None)

def low_pass(kept, grad):
    return (grad,)

def back_keep(v):
    return (v, None)

def back_low(kept, grad):
    return (low(grad),)
low.defvjp(low_keep, low_pass)
low_back.defvjp(back_keep, back_low)
NEGATIVE = -1e+30
EPSILON = 1e-06
HIGHEST = lax.Precision.HIGHEST

def layer_norm(values, scale_vec, offset_vec):
    centre = lax.optimization_barrier(jnp.mean(values, axis=-1, keepdims=True))
    centred = values - centre
    second = lax.optimization_barrier(jnp.mean(centred * centred, axis=-1, keepdims=True))
    return centred * lax.rsqrt(second + EPSILON) * scale_vec + offset_vec

def gelu_exact(values):
    return jax.nn.gelu(values, approximate=False)

def offset_picks(table_rows):
    places = jnp.arange(WIN)
    target = places[:, None] - places[None, :] + WIN - 1
    return (target[:, :, None] == jnp.arange(table_rows)[None, None, :]).astype(jnp.float32)

def window_valid(extent):
    places = jnp.arange(WIN * WIN)
    row_index = places // WIN
    col_index = places % WIN
    return (row_index[None, :] < extent[:, 0:1]) & (col_index[None, :] < extent[:, 1:2])

def block_forward(params, tokens_blk, extent_blk):
    ln1_gain, ln1_bias, qkv_weight, query_bias, value_bias, rel_h, rel_w, proj_weight, proj_bias, ln2_gain, ln2_bias, up_weight, up_bias, down_weight, down_bias = params
    window_count = extent_blk.shape[0]
    window_area = WIN * WIN
    usable = window_valid(extent_blk)
    normed = layer_norm(tokens_blk, ln1_gain, ln1_bias)
    projected = jnp.dot(low(normed), qkv_weight, precision=HIGHEST)
    queries = low(low_back(projected[:, :D] + query_bias))
    key_rows = low(low_back(projected[:, D:2 * D]))
    value_rows = low(low_back(projected[:, 2 * D:] + value_bias))
    queries_split = queries.reshape(window_count, window_area, HEADS, HEAD_DIM)
    keys_split = key_rows.reshape(window_count, window_area, HEADS, HEAD_DIM)
    values_split = value_rows.reshape(window_count, window_area, HEADS, HEAD_DIM)
    scores = jnp.einsum('wqhd,wkhd->whqk', queries_split, keys_split, precision=HIGHEST) * HEAD_DIM ** (-0.5)
    selector = offset_picks(2 * WIN - 1)
    table_h = jnp.einsum('rkj,jd->rkd', selector, rel_h, precision=HIGHEST)
    table_w = jnp.einsum('rkj,jd->rkd', selector, rel_w, precision=HIGHEST)
    queries_grid = queries.reshape(window_count, WIN, WIN, HEADS, HEAD_DIM)
    along_h = jnp.einsum('wrchd,rkd->whrck', queries_grid, table_h, precision=HIGHEST)
    along_w = jnp.einsum('wrchd,ckd->whrck', queries_grid, table_w, precision=HIGHEST)
    scores = scores.reshape(window_count, HEADS, WIN, WIN, WIN, WIN) + along_h[..., :, None] + along_w[..., None, :]
    scores = low_back(scores.reshape(window_count, HEADS, window_area, window_area))
    scores = jnp.where(usable[:, None, None, :], scores, NEGATIVE)
    row_top = lax.optimization_barrier(jnp.max(scores, axis=-1, keepdims=True))
    raised = jnp.exp(scores - row_top)
    weights = raised / lax.optimization_barrier(jnp.sum(raised, axis=-1, keepdims=True))
    attended = jnp.einsum('whqk,wkhd->wqhd', low(weights), values_split, precision=HIGHEST)
    attended = low(low_back(attended.reshape(window_count * window_area, D)))
    branch = low_back(jnp.dot(attended, proj_weight, precision=HIGHEST) + proj_bias)
    middle = tokens_blk + branch
    mlp_input = low(layer_norm(middle, ln2_gain, ln2_bias))
    hidden_pre = low_back(jnp.dot(mlp_input, up_weight, precision=HIGHEST) + up_bias)
    hidden_low = low(gelu_exact(hidden_pre))
    mlp_out = low_back(jnp.dot(hidden_low, down_weight.T, precision=HIGHEST) + down_bias)
    row_mask = usable.reshape(window_count * window_area, 1).astype(jnp.float32)
    return row_mask * (middle + mlp_out)

def reference(tokens, window_extent, ln1_gain, ln1_bias, qkv_weight, query_bias, value_bias, rel_h, rel_w, proj_weight, proj_bias, ln2_gain, ln2_bias, up_weight, up_bias, down_weight, down_bias, grad_out):
    params = tuple((member.astype(jnp.float32) for member in (ln1_gain, ln1_bias, qkv_weight, query_bias, value_bias, rel_h, rel_w, proj_weight, proj_bias, ln2_gain, ln2_bias, up_weight, up_bias, down_weight, down_bias)))
    block_count = WINDOWS // 20
    block_rows = 20 * WIN * WIN
    token_blocks = tokens.astype(jnp.float32).reshape(block_count, block_rows, D)
    extent_blocks = window_extent.reshape(block_count, 20, 2)
    checked = jax.checkpoint(block_forward)

    def whole_layer(token_all, params_all):
        return lax.map(lambda block_pair: checked(params_all, block_pair[0], block_pair[1]), (token_all, extent_blocks))
    result, pullback = jax.vjp(whole_layer, token_blocks, params)
    grad_blocks, grad_params = pullback(grad_out.astype(jnp.float32).reshape(block_count, block_rows, D))
    output = result.reshape(TOKENS, D).astype(jnp.bfloat16)
    grad_tokens = grad_blocks.reshape(TOKENS, D).astype(jnp.bfloat16)
    return (output, grad_tokens, grad_params[0], grad_params[1], grad_params[2], grad_params[3], grad_params[4], grad_params[5], grad_params[6], grad_params[7], grad_params[8], grad_params[9], grad_params[10], grad_params[11], grad_params[12], grad_params[13], grad_params[14])
```

```python
import functools
import jax
import jax.numpy as jnp
from jax import lax
from jax.experimental import pallas as pl
from jax.experimental.pallas import tpu as pltpu
from jax.sharding import PartitionSpec as P

HEADS = 12
HEAD_DIM = 64
WIN = 14
AREA = WIN * WIN
PADDED = 208
PAIRS = HEADS // 2
MODEL = HEADS * HEAD_DIM
EPSILON = 1e-6
NEGATIVE = -1e30
SCALE = HEAD_DIM ** -0.5
F32 = jnp.float32
BF16 = jnp.bfloat16
NN = (((1,), (0,)), ((), ()))
NT = (((1,), (1,)), ((), ()))
TN = (((0,), (0,)), ((), ()))
VMEM_LIMIT = 60 * 1024 * 1024


def mm(a, b, dims=NN):
    return lax.dot_general(a, b, dims, preferred_element_type=F32)


def fold8(v):
    return jnp.sum(v.reshape(v.shape[0] // 8, 8, v.shape[1]), axis=0)


def norm(v):
    mu = jnp.mean(v, axis=-1, keepdims=True)
    c = v - mu
    return c, lax.rsqrt(jnp.mean(c * c, axis=-1, keepdims=True) + EPSILON)


def eye(n, value=1.0):
    r = lax.broadcasted_iota(jnp.int32, (n, n), 0)
    c = lax.broadcasted_iota(jnp.int32, (n, n), 1)
    return jnp.where(r == c, value, 0.0).astype(BF16)


def skew_bits(which):
    lane = lax.broadcasted_iota(jnp.int32, (1, PADDED), 1)
    r = lane // WIN
    return WIN - 1 - (jnp.minimum(r, WIN - 1) if which == 0 else lane - r * WIN)


def split(v):
    hi = v.astype(BF16)
    return hi, (v - hi.astype(F32)).astype(BF16)


def key_side(k, ohm):
    return jnp.concatenate([k, ohm], axis=1)


def query_side(qa, h):
    z = jnp.zeros((HEAD_DIM, PADDED), BF16)
    own = qa[h * 64:(h + 1) * 64]
    bias = qa[128 + 64 * h:192 + 64 * h]
    return jnp.concatenate(([own, z] if h == 0 else [z, own]) + [bias, z], axis=0)


def forward_kernel(x_ref, ohm_ref, gain_ref, bias_ref, wqkv_ref, qkvb_ref, mix_ref, shift_ref, wproj_ref, projb_ref,
                   x1_ref, h1_ref, qkv_ref, qaug_ref, o_ref, lse_ref, wide):
    wb = ohm_ref.shape[0]
    for w in range(wb):
        x = x_ref[AREA * w:AREA * (w + 1), :].astype(F32)
        c, r = norm(x)
        h1_ref[w, PADDED - 16:, :] = jnp.zeros((16, MODEL), BF16)
        h1_ref[w, 0:AREA, :] = (c * r * gain_ref[...] + bias_ref[...]).astype(BF16)

    @pl.loop(0, 3)
    def _(j):
        cs = pl.ds(pl.multiple_of(j * MODEL, MODEL), MODEL)
        p = mm(h1_ref[...].reshape(wb * PADDED, MODEL), wqkv_ref[:, cs]) + qkvb_ref[:, cs]
        qkv_ref[:, :, cs] = p.astype(BF16).reshape(wb, PADDED, MODEL)

    @pl.loop(0, wb * PAIRS)
    def _(it):
        w = it // PAIRS
        pair = it - w * PAIRS
        lanes = lambda part: pl.ds(pl.multiple_of(part * MODEL + pair * 128, 128), 128)
        q = qkv_ref[w, :, lanes(0)]
        k = qkv_ref[w, :, lanes(1)]
        v = qkv_ref[w, :, lanes(2)]
        u = mm(mix_ref[...], jnp.concatenate([q, q], axis=1), NT)
        vt = mm(eye(128), v, NT).astype(BF16)
        tabs = []
        for t in range(2):
            a = u[64 * t:64 * t + 64]
            for n, b in enumerate((8, 4, 2, 1)):
                cond = shift_ref[4 * t + n:4 * t + n + 1, :] > 0
                a = jnp.where(cond, pltpu.roll(a, 64 - b, 0), a)
            tabs.append(a)
        row = lax.broadcasted_iota(jnp.int32, (16, 1), 0)
        parts = [u[128:256].astype(BF16)]
        for h in range(2):
            ah = jnp.where(row == 14, 1.0, tabs[0][32 * h:32 * h + 16])
            aw = tabs[1][32 * h:32 * h + 16]
            hh, hl = split(ah)
            wh, wl = split(aw)
            parts += [hh, wh, hl, wl]
        qa = jnp.concatenate(parts, axis=0)
        qaug_ref[w, pair] = qa
        keys = key_side(k, ohm_ref[w])
        outs = []
        for h in range(2):
            s = mm(keys, query_side(qa, h))
            top = jnp.max(s, axis=0, keepdims=True)
            e = jnp.exp(s - top)
            total = jnp.sum(e, axis=0, keepdims=True)
            lse_ref[w, pair, h:h + 1, :] = top + jnp.log(total)
            outs.append(mm(vt[64 * h:64 * h + 64], e.astype(BF16)) * (1.0 / total))
        ot = jnp.concatenate(outs, axis=0).astype(BF16)
        o_ref[w, :, lanes(0)] = mm(eye(PADDED), ot, NT).astype(BF16)

    wide[...] = mm(o_ref[...].reshape(wb * PADDED, MODEL), wproj_ref[...]) + projb_ref[...]
    for w in range(wb):
        x1_ref[AREA * w:AREA * (w + 1), :] = x_ref[AREA * w:AREA * (w + 1), :].astype(F32) + wide[PADDED * w:PADDED * w + AREA, :]


def once(a):
    return pl.BlockSpec(a.shape, lambda i: (0,) * a.ndim, pipeline_mode=pl.Buffered(1))


def blocked(*shape):
    return pl.BlockSpec(shape, lambda i: (i,) + (0,) * (len(shape) - 1))


def block_windows(windows):
    return 4 if windows % 4 == 0 else windows


def attention_forward(x, ohm, gain, bias, wqkv, qkvb, mix, shift, wproj, projb):
    windows = ohm.shape[0]
    wb = block_windows(windows)
    outs = [((windows * AREA, MODEL), F32, (wb * AREA, MODEL)),
            ((windows, PADDED, MODEL), BF16, (wb, PADDED, MODEL)),
            ((windows, PADDED, 3 * MODEL), BF16, (wb, PADDED, 3 * MODEL)),
            ((windows, PAIRS, 256, PADDED), BF16, (wb, PAIRS, 256, PADDED)),
            ((windows, PADDED, MODEL), BF16, (wb, PADDED, MODEL)),
            ((windows, PAIRS, 2, PADDED), F32, (wb, PAIRS, 2, PADDED))]
    return pl.pallas_call(
        forward_kernel,
        grid=(windows // wb,),
        in_specs=[blocked(wb * AREA, MODEL), blocked(wb, PADDED, 128)] + [once(a) for a in (gain, bias, wqkv, qkvb, mix, shift, wproj, projb)],
        out_specs=[blocked(*b) for _, _, b in outs],
        out_shape=[jax.ShapeDtypeStruct(s, t) for s, t, _ in outs],
        scratch_shapes=[pltpu.VMEM((wb * PADDED, MODEL), F32)],
        compiler_params=pltpu.CompilerParams(vmem_limit_bytes=VMEM_LIMIT, dimension_semantics=("arbitrary",)),
        name="attention_forward",
    )(x, ohm, gain, bias, wqkv, qkvb, mix, shift, wproj, projb)


def backward_kernel(da_ref, ohm_ref, oht_ref, qkv_ref, qaug_ref, lse_ref, wproj_ref, relt_ref, shift_ref,
                    dap_ref, dp_ref, grel_ref, vec_ref, dos):
    wb = ohm_ref.shape[0]

    @pl.when(pl.program_id(0) == 0)
    def _():
        grel_ref[...] = jnp.zeros_like(grel_ref)
        vec_ref[...] = jnp.zeros_like(vec_ref)

    for w in range(wb):
        dap_ref[w, PADDED - 16:, :] = jnp.zeros((16, MODEL), BF16)
        dap_ref[w, 0:AREA, :] = da_ref[AREA * w:AREA * (w + 1), :]
    dos[...] = mm(dap_ref[...].reshape(wb * PADDED, MODEL), wproj_ref[...], NT).astype(BF16).reshape(wb, PADDED, MODEL)

    @pl.loop(0, wb * PAIRS)
    def _(it):
        w = it // PAIRS
        pair = it - w * PAIRS
        lanes = lambda part: pl.ds(pl.multiple_of(part * MODEL + pair * 128, 128), 128)
        q = qkv_ref[w, :, lanes(0)]
        k = qkv_ref[w, :, lanes(1)]
        v = qkv_ref[w, :, lanes(2)]
        do = dos[w, :, lanes(0)]
        qa = qaug_ref[w, pair]
        kt = mm(eye(128, SCALE), k, NT).astype(BF16)
        dot = mm(eye(128), do, NT).astype(BF16)
        keys = key_side(k, ohm_ref[w])
        z = jnp.zeros((HEAD_DIM, PADDED), BF16)
        dvs, dks, dqs = [], [], []
        for h in range(2):
            s = mm(keys, query_side(qa, h))
            a = jnp.exp(s - lse_ref[w, pair, h:h + 1, :])
            own = dot[64 * h:64 * h + 64]
            dw = mm(v, jnp.concatenate([own, z] if h == 0 else [z, own], axis=0))
            t = a * dw
            ds = t - a * jnp.sum(t, axis=0, keepdims=True)
            dsb = ds.astype(BF16)
            dvs.append(mm(a.astype(BF16), do))
            dks.append(mm(dsb, q))
            dqs.append(mm(jnp.concatenate([kt[64 * h:64 * h + 64], oht_ref[...]], axis=0), dsb))
        first = lax.broadcasted_iota(jnp.int32, (1, 128), 1) < 64
        dk = (jnp.where(first, dks[0], dks[1]) * SCALE).astype(BF16)
        dv = jnp.where(first, dvs[0], dvs[1]).astype(BF16)
        zz = jnp.zeros((16, PADDED), F32)
        tabs = []
        for t in range(2):
            lo = 64 + 16 * t
            a = jnp.concatenate([dqs[0][lo:lo + 16], zz, dqs[1][lo:lo + 16], zz], axis=0)
            for n, b in enumerate((8, 4, 2, 1)):
                cond = shift_ref[4 * t + n:4 * t + n + 1, :] > 0
                a = jnp.where(cond, pltpu.roll(a, b, 0), a)
            tabs.append(a.astype(BF16))
        dqt = []
        for h in range(2):
            du = jnp.concatenate([tabs[0][32 * h:32 * h + 32], tabs[1][32 * h:32 * h + 32]], axis=0)
            dqt.append(dqs[h][0:64] + mm(relt_ref[...], jnp.concatenate([du, du], axis=0)))
            grel_ref[h] += mm(du, q)
        dq = mm(eye(PADDED), jnp.concatenate(dqt, axis=0).astype(BF16), NT).astype(BF16)
        dp_ref[w, :, lanes(0)] = dq
        dp_ref[w, :, lanes(1)] = dk
        dp_ref[w, :, lanes(2)] = dv
        vec_ref[0:8, lanes(0)] += fold8(dq.astype(F32))
        vec_ref[8:16, lanes(0)] += fold8(dv.astype(F32))


def attention_backward(da, ohm, oht, qkv, qaug, lse, wproj, relt, shift):
    windows = ohm.shape[0]
    wb = block_windows(windows)
    return pl.pallas_call(
        backward_kernel,
        grid=(windows // wb,),
        in_specs=[blocked(wb * AREA, MODEL), blocked(wb, PADDED, 128), once(oht), blocked(wb, PADDED, 3 * MODEL),
                  blocked(wb, PAIRS, 256, PADDED), blocked(wb, PAIRS, 2, PADDED), once(wproj), once(relt), once(shift)],
        out_specs=[blocked(wb, PADDED, MODEL), blocked(wb, PADDED, 3 * MODEL),
                   pl.BlockSpec((2, 64, 128), lambda i: (0, 0, 0)), pl.BlockSpec((16, MODEL), lambda i: (0, 0))],
        out_shape=[jax.ShapeDtypeStruct((windows, PADDED, MODEL), BF16), jax.ShapeDtypeStruct((windows, PADDED, 3 * MODEL), BF16),
                   jax.ShapeDtypeStruct((2, 64, 128), F32), jax.ShapeDtypeStruct((16, MODEL), F32)],
        scratch_shapes=[pltpu.VMEM((wb, PADDED, MODEL), BF16)],
        compiler_params=pltpu.CompilerParams(vmem_limit_bytes=VMEM_LIMIT, dimension_semantics=("arbitrary",)),
        name="attention_backward",
    )(da, ohm, oht, qkv, qaug, lse, wproj, relt, shift)


def input_kernel(x_ref, da_ref, dp_ref, gain_ref, wqkv_ref, gx_ref, vec_ref, wide, tall):
    wb = dp_ref.shape[0]

    @pl.when(pl.program_id(0) == 0)
    def _():
        vec_ref[...] = jnp.zeros_like(vec_ref)

    wide[...] = mm(dp_ref[...].reshape(wb * PADDED, 3 * MODEL), wqkv_ref[...], NT)
    for w in range(wb):
        tall[AREA * w:AREA * (w + 1), :] = wide[PADDED * w:PADDED * w + AREA, :]
    rows = wb * AREA
    for lo in range(0, rows, 112):
        hi = min(lo + 112, rows)
        c, r = norm(x_ref[lo:hi, :].astype(F32))
        xhat = c * r
        dh = tall[lo:hi, :]
        pad = -(hi - lo) % 8
        both = jnp.concatenate([dh, jnp.zeros((pad, MODEL), F32)], axis=0) if pad else dh
        prod = dh * xhat
        bothx = jnp.concatenate([prod, jnp.zeros((pad, MODEL), F32)], axis=0) if pad else prod
        vec_ref[0:8, :] += fold8(bothx)
        vec_ref[8:16, :] += fold8(both)
        dx = dh * gain_ref[...]
        dx = r * (dx - jnp.mean(dx, axis=-1, keepdims=True) - xhat * jnp.mean(dx * xhat, axis=-1, keepdims=True))
        gx_ref[lo:hi, :] = (dx + da_ref[lo:hi, :].astype(F32)).astype(BF16)


def input_gradient(x, da, dp, gain, wqkv):
    windows = dp.shape[0]
    wb = block_windows(windows)
    return pl.pallas_call(
        input_kernel,
        grid=(windows // wb,),
        in_specs=[blocked(wb * AREA, MODEL), blocked(wb * AREA, MODEL), blocked(wb, PADDED, 3 * MODEL), once(gain), once(wqkv)],
        out_specs=[blocked(wb * AREA, MODEL), pl.BlockSpec((16, MODEL), lambda i: (0, 0))],
        out_shape=[jax.ShapeDtypeStruct((windows * AREA, MODEL), BF16), jax.ShapeDtypeStruct((16, MODEL), F32)],
        scratch_shapes=[pltpu.VMEM((wb * PADDED, MODEL), F32), pltpu.VMEM((wb * AREA, MODEL), F32)],
        compiler_params=pltpu.CompilerParams(vmem_limit_bytes=VMEM_LIMIT, dimension_semantics=("arbitrary",)),
        name="input_gradient",
    )(x, da, dp, gain, wqkv)


def small_tables(window_extent, rel_h, rel_w):
    place = jnp.arange(PADDED)
    r, c = place // WIN, place % WIN
    real = place < AREA
    hot_r = ((r[:, None] == jnp.arange(16)) & real[:, None]).astype(F32)
    hot_c = ((c[:, None] == jnp.arange(16)) & real[:, None]).astype(F32)
    valid = (r < window_extent[:, 0:1]) & (c < window_extent[:, 1:2]) & real
    first = jnp.where((jnp.arange(16) == 14)[None, None, :], jnp.where(valid, 0.0, NEGATIVE)[:, :, None], hot_r[None])
    rest = jnp.concatenate([hot_c, hot_r, hot_c, jnp.zeros((PADDED, 64), F32)], axis=1)
    rest = jnp.broadcast_to(rest[None], (valid.shape[0],) + rest.shape)
    ohm = jnp.concatenate([first, rest], axis=2).astype(BF16)
    oht = jnp.concatenate([hot_r, hot_c], axis=1).T.astype(BF16)
    sh = WIN - 1 - jnp.minimum(r, WIN - 1)
    sw = WIN - 1 - c
    shift = jnp.stack([jnp.where(real, (s >> b) & 1, 0) for s in (sh, sw) for b in (3, 2, 1, 0)]).astype(jnp.int32)
    flip = lambda t: jnp.concatenate([t[::-1], jnp.zeros((5, HEAD_DIM), F32)], axis=0)
    fh, fw = flip(rel_h), flip(rel_w)

    def hi_lo(v):
        hi = v.astype(BF16).astype(F32)
        return hi, v - hi

    def rows(th, tw):
        z = jnp.zeros((32, HEAD_DIM), F32)
        return jnp.concatenate([jnp.concatenate([th, z], 1), jnp.concatenate([z, th], 1),
                                jnp.concatenate([tw, z], 1), jnp.concatenate([z, tw], 1)], axis=0)
    (hh, hl), (wh, wl) = hi_lo(fh), hi_lo(fw)
    mix = jnp.concatenate([rows(hh, wh), rows(hl, wl)], axis=1)
    ident = jnp.concatenate([SCALE * jnp.eye(128, dtype=F32), jnp.zeros((128, 128), F32)], axis=1)
    mix = jnp.concatenate([mix, ident], axis=0).astype(BF16)
    relt = jnp.concatenate([hh, wh, hl, wl], axis=0).T.astype(BF16)
    valid_rows = valid[:, :AREA].reshape(-1, 1).astype(F32)
    return ohm, oht, shift, mix, relt, valid_rows


def gelu_parts(z):
    u = jnp.abs(z)
    t = 1.0 / (1.0 + 0.23164189 * u)
    e = jnp.exp(-0.5 * z * z)
    poly = t * (0.127414796 + t * (-0.142248368 + t * (0.7107068705 + t * (-0.7265760135 + t * 0.5307027145))))
    q = poly * e
    phi = jnp.where(z >= 0.0, 1.0 - q, q)
    return z * phi, phi + z * e * 0.3989422804


def mlp_kernel(rows, x1_ref, go_ref, mask_ref, gain_ref, bias_ref, up_ref, upb_ref, down_ref, downb_ref,
               out_ref, da_ref, dwu_ref, dwd_ref, dbu_ref, vec_ref,
               h2, dm, h2t, dmt, macc, dacc, accu, accd, stage, sems):
    rb = h2.shape[0]
    ff = up_ref.shape[1]
    hc = 1024
    ch = 256
    step = pl.program_id(0)

    @pl.when(step == 0)
    def _():
        accu[...] = jnp.zeros_like(accu)
        accd[...] = jnp.zeros_like(accd)
        dbu_ref[...] = jnp.zeros_like(dbu_ref)
        vec_ref[...] = jnp.zeros_like(vec_ref)

    def live(i):
        row = step * rb + i * ch + lax.broadcasted_iota(jnp.int32, (ch, 1), 0)
        return row < rows

    @pl.loop(0, rb // ch)
    def _(i):
        rs = pl.ds(pl.multiple_of(i * ch, ch), ch)
        x1 = jnp.where(live(i), x1_ref[rs, :], 0.0)
        c, r = norm(x1)
        h2[rs, :] = (c * r * gain_ref[...] + bias_ref[...]).astype(BF16)
        d = jnp.where(live(i) & (mask_ref[rs, :] > 0.0), go_ref[rs, :].astype(F32), 0.0)
        dm[rs, :] = d.astype(BF16)
        vec_ref[0:8, :] += fold8(d)

    h2t[...] = h2[...].T
    dmt[...] = dm[...].T
    macc[...] = jnp.zeros_like(macc)
    dacc[...] = jnp.zeros_like(dacc)

    @pl.loop(0, ff // hc)
    def _(j):
        cs = pl.ds(pl.multiple_of(j * hc, hc), hc)
        z = mm(h2[...], up_ref[:, cs]) + upb_ref[:, cs]
        dact = mm(dm[...], down_ref[:, cs])
        g, gp = gelu_parts(z)
        g = g.astype(BF16)
        dz = dact * gp
        dzb = dz.astype(BF16)
        dbu_ref[:, cs] += fold8(dzb.astype(F32))
        macc[...] += mm(g, down_ref[:, cs], NT)
        dacc[...] += mm(dzb, up_ref[:, cs], NT)
        accd[:, cs] += mm(dmt[...], g)
        accu[:, cs] += mm(h2t[...], dzb)

    @pl.loop(0, rb // ch)
    def _(i):
        rs = pl.ds(pl.multiple_of(i * ch, ch), ch)
        x1 = jnp.where(live(i), x1_ref[rs, :], 0.0)
        c, r = norm(x1)
        xhat = c * r
        valid = live(i) & (mask_ref[rs, :] > 0.0)
        out_ref[rs, :] = jnp.where(valid, x1 + macc[rs, :] + downb_ref[...], 0.0).astype(BF16)
        dh = dacc[rs, :]
        vec_ref[8:16, :] += fold8(dh * xhat)
        vec_ref[16:24, :] += fold8(dh)
        dx = dh * gain_ref[...]
        dx = r * (dx - jnp.mean(dx, axis=-1, keepdims=True) - xhat * jnp.mean(dx * xhat, axis=-1, keepdims=True))
        da = (dx + dm[rs, :].astype(F32)).astype(BF16)
        da_ref[rs, :] = da
        vec_ref[24:32, :] += fold8(da.astype(F32))

    @pl.when(step == pl.num_programs(0) - 1)
    def _():
        def copy(k):
            src, dst = ((accu, dwu_ref), (accd, dwd_ref))[k // (ff // hc)]
            j = k % (ff // hc)
            return src, pltpu.make_async_copy(stage.at[k % 2], dst.at[:, pl.ds(j * hc, hc)], sems.at[k % 2])
        n = 2 * (ff // hc)
        for k in range(n):
            src, cp = copy(k)
            if k >= 2:
                copy(k - 2)[1].wait()
            j = k % (ff // hc)
            stage[k % 2] = src[:, j * hc:(j + 1) * hc].astype(BF16)
            cp.start()
        copy(n - 2)[1].wait()
        copy(n - 1)[1].wait()


def mlp(x1, go, mask, gain, bias, up, upb, down, downb):
    rows, d = x1.shape
    ff = up.shape[1]
    rb = 512
    steps = pl.cdiv(rows, rb)
    full = lambda a: pl.BlockSpec(a.shape, lambda i: (0, 0), pipeline_mode=pl.Buffered(1))
    rowspec = lambda w: pl.BlockSpec((rb, w), lambda i: (i, 0))
    return pl.pallas_call(
        functools.partial(mlp_kernel, rows),
        grid=(steps,),
        in_specs=[rowspec(d), rowspec(d), rowspec(1), full(gain), full(bias), full(up), full(upb), full(down), full(downb)],
        out_specs=[rowspec(d), rowspec(d), pl.BlockSpec(memory_space=pl.ANY), pl.BlockSpec(memory_space=pl.ANY),
                   pl.BlockSpec((8, ff), lambda i: (0, 0)), pl.BlockSpec((32, d), lambda i: (0, 0))],
        out_shape=[jax.ShapeDtypeStruct((rows, d), BF16), jax.ShapeDtypeStruct((rows, d), BF16),
                   jax.ShapeDtypeStruct((d, ff), BF16), jax.ShapeDtypeStruct((d, ff), BF16),
                   jax.ShapeDtypeStruct((8, ff), F32), jax.ShapeDtypeStruct((32, d), F32)],
        scratch_shapes=[pltpu.VMEM((rb, d), BF16), pltpu.VMEM((rb, d), BF16), pltpu.VMEM((d, rb), BF16), pltpu.VMEM((d, rb), BF16),
                        pltpu.VMEM((rb, d), F32), pltpu.VMEM((rb, d), F32), pltpu.VMEM((d, ff), F32), pltpu.VMEM((d, ff), F32),
                        pltpu.VMEM((2, d, 1024), BF16), pltpu.SemaphoreType.DMA((2,))],
        compiler_params=pltpu.CompilerParams(vmem_limit_bytes=60 * 1024 * 1024, dimension_semantics=("arbitrary",)),
        name="mlp",
    )(x1, go, mask, gain, bias, up, upb, down, downb)


def bits(n):
    return n.bit_length() - 1


def exchange_order(dp, mlp):
    dp_bits = list(range(bits(dp)))
    order = [("dp", b) for b in dp_bits[:1]]
    order += [("mlp", b) for b in reversed(range(bits(mlp)))]
    order += [("dp", b) for b in dp_bits[1:2]]
    order += [("dp", b) for b in reversed(dp_bits[2:])]
    return order


def halve(parts, sizes):
    dp, mlp = sizes["dp"], sizes["mlp"]
    names = [("dp", b) for b in reversed(range(bits(dp)))] + [("mlp", b) for b in reversed(range(bits(mlp)))]
    held = parts.reshape((2,) * len(names) + parts.shape[2:])
    for step in exchange_order(dp, mlp):
        axis, bit = step
        at = names.index(step)
        names.pop(at)
        mine = (lax.axis_index(axis) >> bit) & 1
        keep = lax.dynamic_index_in_dim(held, mine, at, keepdims=False)
        send = lax.dynamic_index_in_dim(held, 1 - mine, at, keepdims=False)
        n = sizes[axis]
        got = lax.ppermute(send, axis, [(i, i ^ (1 << bit)) for i in range(n)])
        held = (keep.astype(F32) + got.astype(F32)).astype(BF16)
    return held


def by_owner(grad, dp, mlp):
    rows, cols = grad.shape
    return grad.reshape(dp, rows // dp, mlp, cols // mlp).transpose(0, 2, 1, 3)


def per_device(
    sizes,
    tokens,
    window_extent,
    ln1_gain,
    ln1_bias,
    qkv_weight,
    query_bias,
    value_bias,
    rel_h,
    rel_w,
    proj_weight,
    proj_bias,
    ln2_gain,
    ln2_bias,
    up_weight,
    up_bias,
    down_weight,
    down_bias,
    grad_out,
):
    dp, mlp_n = sizes["dp"], sizes["mlp"]
    line = lambda v: v.reshape(1, -1)
    up_full = lax.all_gather(up_weight, "mlp", axis=1, tiled=True)
    down_full = lax.all_gather(down_weight, "mlp", axis=1, tiled=True)
    up_bias_full = lax.all_gather(up_bias, "mlp", axis=0, tiled=True)
    ohm, oht, shift, mix, relt, valid_rows = small_tables(window_extent, rel_h, rel_w)
    qkv_bias = jnp.concatenate([query_bias, jnp.zeros_like(query_bias), value_bias])
    x1, h1, qkv, qaug, o, lse = attention_forward(
        tokens, ohm, line(ln1_gain), line(ln1_bias), qkv_weight, line(qkv_bias), mix, shift, proj_weight, line(proj_bias))
    output, da, dw_up, dw_down, up_sums, mid_sums = mlp(
        x1, grad_out, valid_rows, line(ln2_gain), line(ln2_bias), up_full, line(up_bias_full), down_full, line(down_bias))
    ff = dw_up.shape[1]
    both = jnp.concatenate([dw_up, dw_down], axis=1)
    both = lax.psum_scatter(both, "dp", scatter_dimension=0, tiled=True)
    both = both.reshape(-1, 2, mlp_n, ff // mlp_n).transpose(2, 1, 0, 3)
    both = lax.psum_scatter(both, "mlp", scatter_dimension=0, tiled=True)[0].astype(F32)
    dap, dp_all, grel, qv_sums = attention_backward(da, ohm, oht, qkv, qaug, lse, proj_weight, relt, shift)
    flat = lambda v: v.reshape(-1, v.shape[-1])
    dw_qkv = mm(flat(h1), flat(dp_all), TN).astype(BF16)
    dw_proj = mm(flat(o), flat(dap), TN).astype(BF16)
    late = jnp.concatenate([by_owner(dw_qkv, dp, mlp_n), by_owner(dw_proj, dp, mlp_n)], axis=3)
    late = halve(late, sizes).astype(F32)
    grad_tokens, in_sums = input_gradient(tokens, da, dp_all, line(ln1_gain), qkv_weight)
    rel = grel[0, :, :HEAD_DIM] + grel[1, :, HEAD_DIM:]
    fold = lambda v: jnp.sum(v.reshape(-1, 8, v.shape[1]), axis=1).reshape(-1)
    sums = jnp.concatenate([fold(in_sums), fold(qv_sums), rel.reshape(-1), fold(mid_sums), fold(up_sums)])
    sums = lax.psum(sums, ("dp", "mlp"))
    d = MODEL
    n_rel = 64 * HEAD_DIM
    rel = sums[4 * d:4 * d + n_rel].reshape(64, HEAD_DIM)
    mid = sums[4 * d + n_rel:]
    table = 2 * WIN - 1
    cols = dw_qkv.shape[1] // mlp_n
    return (
        output,
        grad_tokens,
        sums[0:d],
        sums[d:2 * d],
        late[:, :cols],
        sums[2 * d:3 * d],
        sums[3 * d:4 * d],
        rel[0:table][::-1],
        rel[32:32 + table][::-1],
        late[:, cols:],
        mid[3 * d:4 * d],
        mid[d:2 * d],
        mid[2 * d:3 * d],
        both[0],
        mid[4 * d:],
        both[1],
        mid[0:d],
    )


def solution(mesh):
    rows = P(("dp", "mlp"), None)
    in_specs = (rows, rows, P(), P(), P(), P(), P(), P(), P(), P(), P(), P(), P(),
                P(None, "mlp"), P("mlp"), P(None, "mlp"), P(), rows)
    block = P("dp", "mlp")
    out_specs = (rows, rows, P(), P(), block, P(), P(), P(), P(), block, P(), P(), P(), block, P(), block, P())
    sizes = {name: mesh.shape[name] for name in ("dp", "mlp")}
    return jax.shard_map(
        functools.partial(per_device, sizes), mesh=mesh, in_specs=in_specs, out_specs=out_specs, check_vma=False)
```

```python
import functools
import jax
import jax.numpy as jnp
from jax import lax
from jax.experimental import pallas as pl
from jax.experimental.pallas import tpu as pltpu
from jax.sharding import PartitionSpec as P

HEADS = 12
HEAD_DIM = 64
WIN = 14
AREA = WIN * WIN
PADDED = 208
PAIRS = HEADS // 2
MODEL = HEADS * HEAD_DIM
EPSILON = 1e-6
NEGATIVE = -1e30
SCALE = HEAD_DIM ** -0.5
F32 = jnp.float32
BF16 = jnp.bfloat16
NN = (((1,), (0,)), ((), ()))
NT = (((1,), (1,)), ((), ()))
TN = (((0,), (0,)), ((), ()))
TOGETHER = 6
TOGETHER_BACK = 6
VMEM_LIMIT = 60 * 1024 * 1024


def mm(a, b, dims=NN):
    return lax.dot_general(a, b, dims, preferred_element_type=F32)


def fold8(v):
    return jnp.sum(v.reshape(v.shape[0] // 8, 8, v.shape[1]), axis=0)


def norm(v):
    mu = jnp.mean(v, axis=-1, keepdims=True)
    c = v - mu
    return c, lax.rsqrt(jnp.mean(c * c, axis=-1, keepdims=True) + EPSILON)


def eye(n, value=1.0):
    r = lax.broadcasted_iota(jnp.int32, (n, n), 0)
    c = lax.broadcasted_iota(jnp.int32, (n, n), 1)
    return jnp.where(r == c, value, 0.0).astype(BF16)


def skew_bits(which):
    lane = lax.broadcasted_iota(jnp.int32, (1, PADDED), 1)
    r = lane // WIN
    return WIN - 1 - (jnp.minimum(r, WIN - 1) if which == 0 else lane - r * WIN)


def split(v):
    hi = v.astype(BF16)
    return hi, (v - hi.astype(F32)).astype(BF16)


def key_side(k, ohm):
    return jnp.concatenate([k, ohm], axis=1)


def query_side(qa, h):
    z = jnp.zeros((HEAD_DIM, PADDED), BF16)
    own = qa[h * 64:(h + 1) * 64]
    bias = qa[128 + 64 * h:192 + 64 * h]
    return jnp.concatenate(([own, z] if h == 0 else [z, own]) + [bias, z], axis=0)


def forward_kernel(x_ref, ohm_ref, gain_ref, bias_ref, wqkv_ref, qkvb_ref, mix_ref, shift_ref, wproj_ref, projb_ref,
                   x1_ref, xhat_ref, qkv_ref, qaug_ref, o_ref, lse_ref, h1_ref, wide):
    wb = ohm_ref.shape[0]
    for w in range(wb):
        x = x_ref[AREA * w:AREA * (w + 1), :].astype(F32)
        c, r = norm(x)
        xhat = c * r
        h1_ref[w, PADDED - 16:, :] = jnp.zeros((16, MODEL), BF16)
        xhat_ref[w, PADDED - 16:, :] = jnp.zeros((16, MODEL), BF16)
        h1_ref[w, 0:AREA, :] = (xhat * gain_ref[...] + bias_ref[...]).astype(BF16)
        xhat_ref[w, 0:AREA, :] = xhat.astype(BF16)

    @pl.loop(0, 3)
    def _(j):
        cs = pl.ds(pl.multiple_of(j * MODEL, MODEL), MODEL)
        p = mm(h1_ref[...].reshape(wb * PADDED, MODEL), wqkv_ref[:, cs]) + qkvb_ref[:, cs]
        qkv_ref[:, :, cs] = p.astype(BF16).reshape(wb, PADDED, MODEL)

    groups = PAIRS // TOGETHER

    @pl.loop(0, wb * groups)
    def _(it):
        w = it // groups
        base = (it - w * groups) * TOGETHER
        pairs = [base + n for n in range(TOGETHER)]
        lanes = lambda part, pair: pl.ds(pl.multiple_of(part * MODEL + pair * 128, 128), 128)
        qs = [qkv_ref[w, :, lanes(0, p)] for p in pairs]
        us = [mm(mix_ref[...], jnp.concatenate([q, q], axis=1), NT) for q in qs]
        vts = [mm(eye(128), qkv_ref[w, :, lanes(2, p)], NT).astype(BF16) for p in pairs]
        row = lax.broadcasted_iota(jnp.int32, (16, 1), 0)
        qas = []
        for p, u in zip(pairs, us):
            tabs = []
            for t in range(2):
                a = u[64 * t:64 * t + 64]
                for n, b in enumerate((8, 4, 2, 1)):
                    cond = shift_ref[4 * t + n:4 * t + n + 1, :] > 0
                    a = jnp.where(cond, pltpu.roll(a, 64 - b, 0), a)
                tabs.append(a)
            parts = [u[128:256].astype(BF16)]
            for h in range(2):
                ah = jnp.where(row == 14, 1.0, tabs[0][32 * h:32 * h + 16])
                aw = tabs[1][32 * h:32 * h + 16]
                hh, hl = split(ah)
                wh, wl = split(aw)
                parts += [hh, wh, hl, wl]
            qa = jnp.concatenate(parts, axis=0)
            qaug_ref[w, p] = qa
            qas.append(qa)
        keys = [key_side(qkv_ref[w, :, lanes(1, p)], ohm_ref[w]) for p in pairs]
        scores = [mm(key, query_side(qa, h)) for key, qa in zip(keys, qas) for h in range(2)]
        ots = []
        for n, s in enumerate(scores):
            p, h = pairs[n // 2], n % 2
            top = jnp.max(s, axis=0, keepdims=True)
            e = jnp.exp(s - top)
            total = jnp.sum(e, axis=0, keepdims=True)
            lse_ref[w, p, h:h + 1, :] = top + jnp.log(total)
            ots.append(mm(vts[n // 2][64 * h:64 * h + 64], e.astype(BF16)) * (1.0 / total))
        for n, p in enumerate(pairs):
            ot = jnp.concatenate(ots[2 * n:2 * n + 2], axis=0).astype(BF16)
            o_ref[w, :, lanes(0, p)] = mm(eye(PADDED), ot, NT).astype(BF16)

    wide[...] = mm(o_ref[...].reshape(wb * PADDED, MODEL), wproj_ref[...]) + projb_ref[...]
    for w in range(wb):
        x1_ref[AREA * w:AREA * (w + 1), :] = x_ref[AREA * w:AREA * (w + 1), :].astype(F32) + wide[PADDED * w:PADDED * w + AREA, :]


def cost(us):
    return pl.CostEstimate(flops=int(us * 1.0e9), bytes_accessed=1 << 20, transcendentals=0)


def once(a):
    return pl.BlockSpec(a.shape, lambda i: (0,) * a.ndim, pipeline_mode=pl.Buffered(1))


def blocked(*shape):
    return pl.BlockSpec(shape, lambda i: (i,) + (0,) * (len(shape) - 1))


def block_windows(windows):
    return 4 if windows % 4 == 0 else windows


def attention_forward(x, ohm, gain, bias, wqkv, qkvb, mix, shift, wproj, projb):
    windows = ohm.shape[0]
    wb = block_windows(windows)
    outs = [((windows * AREA, MODEL), F32, (wb * AREA, MODEL)),
            ((windows, PADDED, MODEL), BF16, (wb, PADDED, MODEL)),
            ((windows, PADDED, 3 * MODEL), BF16, (wb, PADDED, 3 * MODEL)),
            ((windows, PAIRS, 256, PADDED), BF16, (wb, PAIRS, 256, PADDED)),
            ((windows, PADDED, MODEL), BF16, (wb, PADDED, MODEL)),
            ((windows, PAIRS, 2, PADDED), F32, (wb, PAIRS, 2, PADDED))]
    return pl.pallas_call(
        forward_kernel,
        grid=(windows // wb,),
        in_specs=[blocked(wb * AREA, MODEL), blocked(wb, PADDED, 128)] + [once(a) for a in (gain, bias, wqkv, qkvb, mix, shift, wproj, projb)],
        out_specs=[blocked(*b) for _, _, b in outs],
        out_shape=[jax.ShapeDtypeStruct(s, t) for s, t, _ in outs],
        scratch_shapes=[pltpu.VMEM((wb, PADDED, MODEL), BF16), pltpu.VMEM((wb * PADDED, MODEL), F32)],
        cost_estimate=cost(70),
        compiler_params=pltpu.CompilerParams(vmem_limit_bytes=VMEM_LIMIT, dimension_semantics=("arbitrary",)),
        name="attention_forward",
    )(x, ohm, gain, bias, wqkv, qkvb, mix, shift, wproj, projb)


def backward_kernel(da_ref, ohm_ref, oht_ref, qkv_ref, qaug_ref, lse_ref, wproj_ref, relt_ref, shift_ref,
                    dap_ref, dp_ref, grel_ref, do_ref):
    wb = ohm_ref.shape[0]

    @pl.when(pl.program_id(0) == 0)
    def _():
        grel_ref[...] = jnp.zeros_like(grel_ref)

    for w in range(wb):
        dap_ref[w, PADDED - 16:, :] = jnp.zeros((16, MODEL), BF16)
        dap_ref[w, 0:AREA, :] = da_ref[AREA * w:AREA * (w + 1), :]
    do_ref[...] = mm(dap_ref[...].reshape(wb * PADDED, MODEL), wproj_ref[...], NT).astype(BF16).reshape(wb, PADDED, MODEL)

    groups = PAIRS // TOGETHER_BACK

    @pl.loop(0, wb * groups)
    def _(it):
        w = it // groups
        base = (it - w * groups) * TOGETHER_BACK
        pairs = [base + n for n in range(TOGETHER_BACK)]
        lanes = lambda part, pair: pl.ds(pl.multiple_of(part * MODEL + pair * 128, 128), 128)
        both = [(n, p, h) for n, p in enumerate(pairs) for h in range(2)]
        qs = [qkv_ref[w, :, lanes(0, p)] for p in pairs]
        ks = [qkv_ref[w, :, lanes(1, p)] for p in pairs]
        vs = [qkv_ref[w, :, lanes(2, p)] for p in pairs]
        dos = [do_ref[w, :, lanes(0, p)] for p in pairs]
        scores = [mm(key_side(ks[n], ohm_ref[w]), query_side(qaug_ref[w, p], h)) for n, p, h in both]
        dots = [mm(eye(128), do, NT).astype(BF16) for do in dos]
        kts = [mm(eye(128, SCALE), k, NT).astype(BF16) for k in ks]
        z = jnp.zeros((HEAD_DIM, PADDED), BF16)
        dws = []
        for n, p, h in both:
            own = dots[n][64 * h:64 * h + 64]
            dws.append(mm(vs[n], jnp.concatenate([own, z] if h == 0 else [z, own], axis=0)))
        dvs, dks, dqs = [], [], []
        for s, dw, (n, p, h) in zip(scores, dws, both):
            a = jnp.exp(s - lse_ref[w, p, h:h + 1, :])
            t = a * dw
            dsb = (t - a * jnp.sum(t, axis=0, keepdims=True)).astype(BF16)
            dvs.append(mm(a.astype(BF16), dos[n]))
            dks.append(mm(dsb, qs[n]))
            dqs.append(mm(jnp.concatenate([kts[n][64 * h:64 * h + 64], oht_ref[...]], axis=0), dsb))
        first = lax.broadcasted_iota(jnp.int32, (1, 128), 1) < 64
        zz = jnp.zeros((16, PADDED), F32)
        dqts = []
        for n, p in enumerate(pairs):
            tabs = []
            for t in range(2):
                lo = 64 + 16 * t
                a = jnp.concatenate([dqs[2 * n][lo:lo + 16], zz, dqs[2 * n + 1][lo:lo + 16], zz], axis=0)
                for i, b in enumerate((8, 4, 2, 1)):
                    cond = shift_ref[4 * t + i:4 * t + i + 1, :] > 0
                    a = jnp.where(cond, pltpu.roll(a, b, 0), a)
                tabs.append(a.astype(BF16))
            dqt = []
            for h in range(2):
                du = jnp.concatenate([tabs[0][32 * h:32 * h + 32], tabs[1][32 * h:32 * h + 32]], axis=0)
                dqt.append(dqs[2 * n + h][0:64] + mm(relt_ref[...], jnp.concatenate([du, du], axis=0)))
                grel_ref[h] += mm(du, qs[n])
            dqts.append(jnp.concatenate(dqt, axis=0).astype(BF16))
        for n, p in enumerate(pairs):
            dq = mm(eye(PADDED), dqts[n], NT).astype(BF16)
            dk = (jnp.where(first, dks[2 * n], dks[2 * n + 1]) * SCALE).astype(BF16)
            dv = jnp.where(first, dvs[2 * n], dvs[2 * n + 1]).astype(BF16)
            dp_ref[w, :, lanes(0, p)] = dq
            dp_ref[w, :, lanes(1, p)] = dk
            dp_ref[w, :, lanes(2, p)] = dv


def attention_backward(da, ohm, oht, qkv, qaug, lse, wproj, relt, shift):
    windows = ohm.shape[0]
    wb = block_windows(windows)
    return pl.pallas_call(
        backward_kernel,
        grid=(windows // wb,),
        in_specs=[blocked(wb * AREA, MODEL), blocked(wb, PADDED, 128), once(oht), blocked(wb, PADDED, 3 * MODEL),
                  blocked(wb, PAIRS, 256, PADDED), blocked(wb, PAIRS, 2, PADDED), once(wproj), once(relt), once(shift)],
        out_specs=[blocked(wb, PADDED, MODEL), blocked(wb, PADDED, 3 * MODEL),
                   pl.BlockSpec((2, 64, 128), lambda i: (0, 0, 0))],
        out_shape=[jax.ShapeDtypeStruct((windows, PADDED, MODEL), BF16), jax.ShapeDtypeStruct((windows, PADDED, 3 * MODEL), BF16),
                   jax.ShapeDtypeStruct((2, 64, 128), F32)],
        scratch_shapes=[pltpu.VMEM((wb, PADDED, MODEL), BF16)],
        cost_estimate=cost(70),
        compiler_params=pltpu.CompilerParams(vmem_limit_bytes=VMEM_LIMIT, dimension_semantics=("arbitrary",)),
        name="attention_backward",
    )(da, ohm, oht, qkv, qaug, lse, wproj, relt, shift)


def input_kernel(x_ref, da_ref, dp_ref, gain_ref, wqkv_ref, *rest):
    gx_ref, wide, tall = rest[-3:]
    wb = dp_ref.shape[0]
    wide[...] = mm(dp_ref[...].reshape(wb * PADDED, 3 * MODEL), wqkv_ref[...], NT)
    for w in range(wb):
        tall[AREA * w:AREA * (w + 1), :] = wide[PADDED * w:PADDED * w + AREA, :]
    rows = wb * AREA
    for lo in range(0, rows, 112):
        hi = min(lo + 112, rows)
        c, r = norm(x_ref[lo:hi, :].astype(F32))
        xhat = c * r
        dx = tall[lo:hi, :] * gain_ref[...]
        dx = r * (dx - jnp.mean(dx, axis=-1, keepdims=True) - xhat * jnp.mean(dx * xhat, axis=-1, keepdims=True))
        gx_ref[lo:hi, :] = (dx + da_ref[lo:hi, :].astype(F32)).astype(BF16)


def input_gradient(x, da, dp, gain, wqkv, at, count, held):
    windows = dp.shape[0]
    wb = block_windows(windows)
    part = lambda *shape: pl.BlockSpec(shape, lambda i: (i + at,) + (0,) * (len(shape) - 1))
    extra = [] if held is None else [held]
    return pl.pallas_call(
        input_kernel,
        grid=(count,),
        in_specs=[part(wb * AREA, MODEL), part(wb * AREA, MODEL), part(wb, PADDED, 3 * MODEL), once(gain), once(wqkv)]
        + [pl.BlockSpec(memory_space=pl.ANY)] * len(extra),
        out_specs=part(wb * AREA, MODEL),
        out_shape=jax.ShapeDtypeStruct((windows * AREA, MODEL), BF16),
        input_output_aliases={5: 0} if extra else {},
        scratch_shapes=[pltpu.VMEM((wb * PADDED, MODEL), F32), pltpu.VMEM((wb * AREA, MODEL), F32)],
        cost_estimate=cost(5 * count),
        compiler_params=pltpu.CompilerParams(vmem_limit_bytes=VMEM_LIMIT, dimension_semantics=("arbitrary",)),
        name="input_gradient",
    )(x, da, dp, gain, wqkv, *extra)


BAND = 384


def weight_kernel(xhat_ref, o_ref, dp_ref, dap_ref, w_ref, gain_ref, bias_ref, dw_ref, sum_ref, gvec_ref, bvec_ref, turned):
    step = pl.program_id(0)
    qkv_bands = 3 * MODEL // BAND

    @pl.when(step == 0)
    def _():
        turned[...] = xhat_ref[...].T
        gvec_ref[...] = jnp.zeros_like(gvec_ref)
        bvec_ref[...] = jnp.zeros_like(bvec_ref)

    @pl.when(step == qkv_bands)
    def _():
        turned[...] = o_ref[...].T

    @pl.when(step < qkv_bands)
    def _():
        m = mm(turned[...], dp_ref[...])
        s = jnp.sum(dp_ref[...].astype(F32), axis=0, keepdims=True)
        sum_ref[...] = jnp.broadcast_to(s, sum_ref.shape)
        dw_ref[...] = (m * gain_ref[...] + bias_ref[...] * s).astype(BF16)
        w = w_ref[...].astype(F32)
        g, b = w * m, w * s
        for n in range(BAND // 128):
            gvec_ref[...] += g[:, 128 * n:128 * (n + 1)]
            bvec_ref[...] += b[:, 128 * n:128 * (n + 1)]

    @pl.when(step >= qkv_bands)
    def _():
        dw_ref[...] = mm(turned[...], dap_ref[...]).astype(BF16)


def weight_gradients(xhat, o, dp, dap, wqkv, gain, bias, owners):
    rows = xhat.shape[0]
    nq, np_ = 3 * MODEL // BAND, MODEL // BAND
    oq, op = nq // owners, np_ // owners
    last = lambda i: jnp.minimum(i, nq - 1)

    def place(i):
        j = i - nq
        q = (i // oq) * (oq + op) + i % oq
        p = (j // op) * (oq + op) + oq + j % op
        return (0, jnp.where(i < nq, q, p))
    return pl.pallas_call(
        weight_kernel,
        grid=(nq + np_,),
        in_specs=[once(xhat), once(o), pl.BlockSpec((rows, BAND), lambda i: (0, last(i))),
                  pl.BlockSpec((rows, BAND), lambda i: (0, jnp.maximum(i - nq, 0))),
                  pl.BlockSpec((MODEL, BAND), lambda i: (0, last(i))), once(gain), once(bias)],
        out_specs=[pl.BlockSpec((MODEL, BAND), place), pl.BlockSpec((8, BAND), lambda i: (0, last(i))),
                   pl.BlockSpec((MODEL, 128), lambda i: (0, 0)), pl.BlockSpec((MODEL, 128), lambda i: (0, 0))],
        out_shape=[jax.ShapeDtypeStruct((MODEL, 4 * MODEL), BF16), jax.ShapeDtypeStruct((8, 3 * MODEL), F32),
                   jax.ShapeDtypeStruct((MODEL, 128), F32), jax.ShapeDtypeStruct((MODEL, 128), F32)],
        scratch_shapes=[pltpu.VMEM((MODEL, rows), BF16)],
        cost_estimate=cost(20),
        compiler_params=pltpu.CompilerParams(vmem_limit_bytes=VMEM_LIMIT, dimension_semantics=("arbitrary",)),
        name="weight_gradients",
    )(xhat, o, dp, dap, wqkv, gain, bias)


def small_tables(window_extent, rel_h, rel_w):
    place = jnp.arange(PADDED)
    r, c = place // WIN, place % WIN
    real = place < AREA
    hot_r = ((r[:, None] == jnp.arange(16)) & real[:, None]).astype(F32)
    hot_c = ((c[:, None] == jnp.arange(16)) & real[:, None]).astype(F32)
    valid = (r < window_extent[:, 0:1]) & (c < window_extent[:, 1:2]) & real
    first = jnp.where((jnp.arange(16) == 14)[None, None, :], jnp.where(valid, 0.0, NEGATIVE)[:, :, None], hot_r[None])
    rest = jnp.concatenate([hot_c, hot_r, hot_c, jnp.zeros((PADDED, 64), F32)], axis=1)
    rest = jnp.broadcast_to(rest[None], (valid.shape[0],) + rest.shape)
    ohm = jnp.concatenate([first, rest], axis=2).astype(BF16)
    oht = jnp.concatenate([hot_r, hot_c], axis=1).T.astype(BF16)
    sh = WIN - 1 - jnp.minimum(r, WIN - 1)
    sw = WIN - 1 - c
    shift = jnp.stack([jnp.where(real, (s >> b) & 1, 0) for s in (sh, sw) for b in (3, 2, 1, 0)]).astype(jnp.int32)
    flip = lambda t: jnp.concatenate([t[::-1], jnp.zeros((5, HEAD_DIM), F32)], axis=0)
    fh, fw = flip(rel_h), flip(rel_w)

    def hi_lo(v):
        hi = v.astype(BF16).astype(F32)
        return hi, v - hi

    def rows(th, tw):
        z = jnp.zeros((32, HEAD_DIM), F32)
        return jnp.concatenate([jnp.concatenate([th, z], 1), jnp.concatenate([z, th], 1),
                                jnp.concatenate([tw, z], 1), jnp.concatenate([z, tw], 1)], axis=0)
    (hh, hl), (wh, wl) = hi_lo(fh), hi_lo(fw)
    mix = jnp.concatenate([rows(hh, wh), rows(hl, wl)], axis=1)
    ident = jnp.concatenate([SCALE * jnp.eye(128, dtype=F32), jnp.zeros((128, 128), F32)], axis=1)
    mix = jnp.concatenate([mix, ident], axis=0).astype(BF16)
    relt = jnp.concatenate([hh, wh, hl, wl], axis=0).T.astype(BF16)
    valid_rows = valid[:, :AREA].reshape(-1, 1).astype(F32)
    return ohm, oht, shift, mix, relt, valid_rows


def gelu_parts(z):
    u = jnp.abs(z)
    t = 1.0 / (1.0 + 0.23164189 * u)
    e = jnp.exp(-0.5 * z * z)
    poly = t * (0.127414796 + t * (-0.142248368 + t * (0.7107068705 + t * (-0.7265760135 + t * 0.5307027145))))
    q = poly * e
    phi = jnp.where(z >= 0.0, 1.0 - q, q)
    return z * phi, phi + z * e * 0.3989422804


ROWS = 512
CHUNK = 64 * 12


def mlp_kernel(rows, widths, offset_ref, x1_ref, go_ref, mask_ref, gain_ref, bias_ref, upb_ref, downb_ref, *rest):
    n = len(widths)
    ups, downs = rest[:n], rest[n:2 * n]
    out_ref, da_ref, dw_ref, dbu_ref, vec_ref, h2, dm, h2t, dmt, macc, dacc, accu, accd, stage, sems = rest[2 * n:]
    rb = h2.shape[0]
    ch = 256
    step = pl.program_id(0)

    @pl.when(step == 0)
    def _():
        accu[...] = jnp.zeros_like(accu)
        accd[...] = jnp.zeros_like(accd)
        dbu_ref[...] = jnp.zeros_like(dbu_ref)
        vec_ref[...] = jnp.zeros_like(vec_ref)

    def live(i):
        row = step * rb + i * ch + lax.broadcasted_iota(jnp.int32, (ch, 1), 0)
        return row < rows

    @pl.loop(0, rb // ch)
    def _(i):
        rs = pl.ds(pl.multiple_of(i * ch, ch), ch)
        x1 = jnp.where(live(i), x1_ref[rs, :], 0.0)
        c, r = norm(x1)
        h2[rs, :] = (c * r * gain_ref[...] + bias_ref[...]).astype(BF16)
        d = jnp.where(live(i) & (mask_ref[rs, :] > 0.0), go_ref[rs, :].astype(F32), 0.0)
        dm[rs, :] = d.astype(BF16)
        vec_ref[0:8, :] += fold8(d)

    h2t[...] = h2[...].T
    dmt[...] = dm[...].T

    at = 0
    for up_ref, down_ref, width in zip(ups, downs, widths):
        size = min(CHUNK, width)
        for lo in range(0, width, size):
            here, there = slice(lo, lo + size), slice(at, at + size)
            z = mm(h2[...], up_ref[:, here]) + upb_ref[:, there]
            dact = mm(dm[...], down_ref[:, here])
            g, gp = gelu_parts(z)
            g = g.astype(BF16)
            dz = (dact * gp).astype(BF16)
            dbu_ref[:, there] += fold8(dz.astype(F32))
            m = mm(g, down_ref[:, here], NT)
            macc[...] = m if at == 0 else macc[...] + m
            d = mm(dz, up_ref[:, here], NT)
            dacc[...] = d if at == 0 else dacc[...] + d
            accd[:, there] += mm(dmt[...], g)
            accu[:, there] += mm(h2t[...], dz)
            at += size

    @pl.loop(0, rb // ch)
    def _(i):
        rs = pl.ds(pl.multiple_of(i * ch, ch), ch)
        x1 = jnp.where(live(i), x1_ref[rs, :], 0.0)
        c, r = norm(x1)
        xhat = c * r
        valid = live(i) & (mask_ref[rs, :] > 0.0)
        out_ref[rs, :] = jnp.where(valid, x1 + macc[rs, :] + downb_ref[...], 0.0).astype(BF16)
        dh = dacc[rs, :]
        vec_ref[8:16, :] += fold8(dh * xhat)
        vec_ref[16:24, :] += fold8(dh)
        dx = dh * gain_ref[...]
        dx = r * (dx - jnp.mean(dx, axis=-1, keepdims=True) - xhat * jnp.mean(dx * xhat, axis=-1, keepdims=True))
        da = (dx + dm[rs, :].astype(F32)).astype(BF16)
        da_ref[rs, :] = da
        vec_ref[24:32, :] += fold8(da.astype(F32))

    @pl.when(step == pl.num_programs(0) - 1)
    def _():
        size = stage.shape[2]
        each = accu.shape[1] // size

        def copy(k):
            to = pl.multiple_of(offset_ref[k], 128)
            return pltpu.make_async_copy(stage.at[k % 2], dw_ref.at[:, pl.ds(to, size)], sems.at[k % 2])
        for k in range(2 * each):
            if k >= 2:
                copy(k - 2).wait()
            src = (accu, accd)[k // each]
            stage[k % 2] = src[:, (k % each) * size:(k % each + 1) * size].astype(BF16)
            copy(k).start()
        copy(2 * each - 2).wait()
        copy(2 * each - 1).wait()


def mlp(x1, go, mask, gain, bias, upb, downb, ups, downs, offsets):
    rows, d = x1.shape
    widths = tuple(u.shape[1] for u in ups)
    ff = sum(widths)
    size = 2 * ff // offsets.shape[0]
    rb = ROWS
    full = lambda a: pl.BlockSpec(a.shape, lambda i, _: (0, 0), pipeline_mode=pl.Buffered(1))
    rowspec = lambda w: pl.BlockSpec((rb, w), lambda i, _: (i, 0))
    return pl.pallas_call(
        functools.partial(mlp_kernel, rows, widths),
        grid_spec=pltpu.PrefetchScalarGridSpec(
            num_scalar_prefetch=1,
            grid=(pl.cdiv(rows, rb),),
            in_specs=[rowspec(d), rowspec(d), rowspec(1)] + [full(a) for a in (gain, bias, upb, downb, *ups, *downs)],
            out_specs=[rowspec(d), rowspec(d), pl.BlockSpec(memory_space=pl.ANY),
                       pl.BlockSpec((8, ff), lambda i, _: (0, 0)), pl.BlockSpec((32, d), lambda i, _: (0, 0))],
            scratch_shapes=[pltpu.VMEM((rb, d), BF16), pltpu.VMEM((rb, d), BF16), pltpu.VMEM((d, rb), BF16), pltpu.VMEM((d, rb), BF16),
                            pltpu.VMEM((rb, d), F32), pltpu.VMEM((rb, d), F32), pltpu.VMEM((d, ff), F32), pltpu.VMEM((d, ff), F32),
                            pltpu.VMEM((2, d, size), BF16), pltpu.SemaphoreType.DMA((2,))]),
        out_shape=[jax.ShapeDtypeStruct((rows, d), BF16), jax.ShapeDtypeStruct((rows, d), BF16),
                   jax.ShapeDtypeStruct((d, 2 * ff), BF16), jax.ShapeDtypeStruct((8, ff), F32), jax.ShapeDtypeStruct((32, d), F32)],
        cost_estimate=cost(170),
        compiler_params=pltpu.CompilerParams(vmem_limit_bytes=VMEM_LIMIT, dimension_semantics=("arbitrary",)),
        name="mlp",
    )(offsets, x1, go, mask, gain, bias, upb, downb, *ups, *downs)


def bits(n):
    return n.bit_length() - 1


def swap(value, axis, bit, sizes):
    return lax.ppermute(value, axis, [(i, i ^ (1 << bit)) for i in range(sizes[axis])])


def bit_of(axis, bit):
    return (lax.axis_index(axis) >> bit) & 1


def add(a, b):
    return (a.astype(F32) + b.astype(F32)).astype(BF16)


def halve_rows(held, at, bit, sizes):
    mine = bit_of("dp", bit)
    keep = lax.dynamic_index_in_dim(held, mine, at, keepdims=False)
    send = lax.dynamic_index_in_dim(held, 1 - mine, at, keepdims=False)
    return add(keep, swap(send, "dp", bit, sizes))


def halve_columns(held, bit, sizes):
    mine = bit_of("mlp", bit) == 1
    half = held.shape[-1] // 2
    low, high = held[..., :half], held[..., half:]
    return add(jnp.where(mine, high, low), swap(jnp.where(mine, low, high), "mlp", bit, sizes))


def reduce_scatter(grad, sizes):
    nb, nm = bits(sizes["dp"]), bits(sizes["mlp"])
    held = grad.reshape((2,) * nb + (grad.shape[0] // sizes["dp"], grad.shape[1]))
    held = halve_rows(held, nb - 1, 0, sizes)
    columns = lambda v: functools.reduce(lambda u, b: halve_columns(u, b, sizes), reversed(range(nm)), v)
    if nb < 3:
        return functools.reduce(lambda u, b: halve_rows(u, b - 1, b, sizes), reversed(range(1, nb)), columns(held))
    first, second = held[0], held[1]
    at = nb - 3
    first = columns(first)
    second = halve_rows(second, at, 1, sizes)
    first = halve_rows(first, at, 1, sizes)
    second = columns(second)
    for b in range(2, nb - 1):
        first, second = (halve_rows(v, nb - 2 - b, b, sizes) for v in (first, second))
    mine = bit_of("dp", nb - 1) == 1
    return add(jnp.where(mine, second, first), swap(jnp.where(mine, first, second), "dp", nb - 1, sizes))


def sum_everywhere(v, sizes):
    for axis in ("dp", "mlp"):
        for b in range(bits(sizes[axis])):
            v = v + swap(v, axis, b, sizes)
    return v


def feed_forward_weights(up, up_bias, down, sizes):
    width = up.shape[1]
    if sizes["mlp"] != 2:
        gather = lambda v: lax.all_gather(v, "mlp", axis=v.ndim - 1, tiled=True)
        count = sizes["mlp"]
        return [gather(up)], [gather(down)], gather(up_bias), jnp.arange(count, dtype=jnp.int32) * width, width
    half = width // 2
    core, me = bit_of("dp", 0), lax.axis_index("mlp")
    cut = lambda v: jnp.where(core == 1, v[:, half:], v[:, :half])
    far_up, far_down = swap(cut(up), "mlp", 0, sizes), swap(cut(down), "mlp", 0, sizes)
    far_bias = swap(up_bias, "mlp", 0, sizes)
    bias = jnp.concatenate([up_bias, jnp.roll(far_bias, -core * half)])
    places = jnp.stack([me * width, me * width + half, (1 - me) * width + core * half, (1 - me) * width + (1 - core) * half])
    return (up, far_up), (down, far_down), bias, places.astype(jnp.int32), half


def per_device(
    sizes,
    tokens,
    window_extent,
    ln1_gain,
    ln1_bias,
    qkv_weight,
    query_bias,
    value_bias,
    rel_h,
    rel_w,
    proj_weight,
    proj_bias,
    ln2_gain,
    ln2_bias,
    up_weight,
    up_bias,
    down_weight,
    down_bias,
    grad_out,
):
    owners = sizes["mlp"]
    line = lambda v: v.reshape(1, -1)
    ups, downs, up_bias_here, places, piece = feed_forward_weights(up_weight, up_bias, down_weight, sizes)
    ohm, oht, shift, mix, relt, valid_rows = small_tables(window_extent, rel_h, rel_w)
    qkv_bias = jnp.concatenate([query_bias, jnp.zeros_like(query_bias), value_bias])
    x1, xhat, qkv, qaug, o, lse = attention_forward(
        tokens, ohm, line(ln1_gain), line(ln1_bias), qkv_weight, line(qkv_bias), mix, shift, proj_weight, line(proj_bias))
    if owners == 2:
        (ups, downs, x1) = lax.optimization_barrier((ups, downs, x1))
        ups, downs = list(ups) + [swap(ups[1], "dp", 0, sizes)], list(downs) + [swap(downs[1], "dp", 0, sizes)]
    width = up_weight.shape[1]
    ff = width * owners
    by_owner = (places // width) * (2 * width) + places % width
    output, da, dw_mlp, up_sums, mid_sums = mlp(
        x1, grad_out, valid_rows, line(ln2_gain), line(ln2_bias), line(up_bias_here), line(down_bias), ups, downs,
        jnp.concatenate([by_owner, by_owner + width]))
    dw_mlp = lax.psum_scatter(dw_mlp, "dp", scatter_dimension=0, tiled=True)
    dw_mlp = lax.psum_scatter(dw_mlp, "mlp", scatter_dimension=1, tiled=True)
    dap, dp_all, grel = attention_backward(da, ohm, oht, qkv, qaug, lse, proj_weight, relt, shift)
    flat = lambda v: v.reshape(-1, v.shape[-1])
    up_sum = jnp.sum(up_sums, axis=0).reshape(-1, piece)
    up_sum = sum(jnp.where(jnp.arange(ff) // piece == places[n] // piece, jnp.tile(up_sum[n], ff // piece), 0.0)
                 for n in range(ff // piece))
    column = lambda v: v.reshape(-1, 1)
    direct = MODEL % (BAND * owners) == 0
    dw_late, dp_sums, gain_sums, bias_sums = weight_gradients(
        flat(xhat), flat(o), flat(dp_all), flat(dap), qkv_weight, column(ln1_gain), column(ln1_bias), owners if direct else 1)
    if not direct:
        split_owner = lambda v: v.reshape(MODEL, owners, -1)
        dw_late = jnp.concatenate([split_owner(dw_late[:, :3 * MODEL]), split_owner(dw_late[:, 3 * MODEL:])], axis=2).reshape(MODEL, -1)
    rel = grel[0, :, :HEAD_DIM] + grel[1, :, HEAD_DIM:]
    mid = jnp.sum(mid_sums.reshape(4, 8, MODEL), axis=1)
    sums = jnp.concatenate([jnp.sum(gain_sums, axis=1), jnp.sum(bias_sums, axis=1), dp_sums[0], rel.reshape(-1), mid.reshape(-1), up_sum])
    sums = sum_everywhere(sums, sizes)
    late = reduce_scatter(dw_late, sizes).astype(F32)
    grad_tokens = None
    blocks = dp_all.shape[0] // block_windows(dp_all.shape[0])
    for n in range(blocks):
        grad_tokens = input_gradient(tokens, da, dp_all, line(ln1_gain), qkv_weight, n, 1, grad_tokens)
    d = MODEL
    table = 2 * WIN - 1
    n_rel = 64 * HEAD_DIM
    rel = sums[5 * d:5 * d + n_rel].reshape(64, HEAD_DIM)
    mid = sums[5 * d + n_rel:]
    cols = 3 * MODEL // owners
    dw_mlp = dw_mlp.astype(F32)
    return (
        output,
        grad_tokens,
        sums[0:d],
        sums[d:2 * d],
        late[:, :cols],
        sums[2 * d:3 * d],
        sums[4 * d:5 * d],
        rel[0:table][::-1],
        rel[32:32 + table][::-1],
        late[:, cols:],
        mid[3 * d:4 * d],
        mid[d:2 * d],
        mid[2 * d:3 * d],
        dw_mlp[:, :width],
        mid[4 * d:],
        dw_mlp[:, width:],
        mid[0:d],
    )


def solution(mesh):
    rows = P(("dp", "mlp"), None)
    in_specs = (rows, rows, P(), P(), P(), P(), P(), P(), P(), P(), P(), P(), P(),
                P(None, "mlp"), P("mlp"), P(None, "mlp"), P(), rows)
    block = P("dp", "mlp")
    out_specs = (rows, rows, P(), P(), block, P(), P(), P(), P(), block, P(), P(), P(), block, P(), block, P())
    sizes = {name: mesh.shape[name] for name in ("dp", "mlp")}
    return jax.shard_map(
        functools.partial(per_device, sizes), mesh=mesh, in_specs=in_specs, out_specs=out_specs, check_vma=False)
```

```python
import functools
import jax
import jax.numpy as jnp
import numpy as np
from jax import lax
from jax.experimental import pallas as pl
from jax.experimental.pallas import tpu as pltpu
from jax.sharding import PartitionSpec as P

HEADS = 12
HEAD_DIM = 64
WIN = 14
AREA = WIN * WIN
PADDED = 208
PAIRS = HEADS // 2
MODEL = HEADS * HEAD_DIM
EPSILON = 1e-6
NEGATIVE = -1e30
SCALE = HEAD_DIM ** -0.5
F32 = jnp.float32
BF16 = jnp.bfloat16
NN = (((1,), (0,)), ((), ()))
NT = (((1,), (1,)), ((), ()))
TN = (((0,), (0,)), ((), ()))
TOGETHER = 6
TOGETHER_BACK = 6
LN1_GAIN, LN1_BIAS, QUERY_BIAS, VALUE_BIAS, PROJ_BIAS, LN2_GAIN, LN2_BIAS, DOWN_BIAS = (slice(n, n + 1) for n in range(8))
VMEM_LIMIT = 60 * 1024 * 1024


def mm(a, b, dims=NN):
    return lax.dot_general(a, b, dims, preferred_element_type=F32)


def fold8(v):
    return jnp.sum(v.reshape(v.shape[0] // 8, 8, v.shape[1]), axis=0)


def norm(v):
    mu = jnp.mean(v, axis=-1, keepdims=True)
    c = v - mu
    return c, lax.rsqrt(jnp.mean(c * c, axis=-1, keepdims=True) + EPSILON)


def eye(n, value=1.0):
    r = lax.broadcasted_iota(jnp.int32, (n, n), 0)
    c = lax.broadcasted_iota(jnp.int32, (n, n), 1)
    return jnp.where(r == c, value, 0.0).astype(BF16)


def skew_bits(which):
    lane = lax.broadcasted_iota(jnp.int32, (1, PADDED), 1)
    r = lane // WIN
    return WIN - 1 - (jnp.minimum(r, WIN - 1) if which == 0 else lane - r * WIN)


def split(v):
    hi = v.astype(BF16)
    return hi, (v - hi.astype(F32)).astype(BF16)


def key_side(k, ohm):
    return jnp.concatenate([k, ohm], axis=1)


def query_side(qa, h):
    z = jnp.zeros((HEAD_DIM, PADDED), BF16)
    own = qa[h * 64:(h + 1) * 64]
    bias = qa[128 + 64 * h:192 + 64 * h]
    return jnp.concatenate(([own, z] if h == 0 else [z, own]) + [bias, z], axis=0)


def forward_kernel(x_ref, ohm_ref, vec_ref, wqkv_ref, mix_ref, shift_ref, wproj_ref,
                   x1_ref, xhat_ref, qkv_ref, qaug_ref, o_ref, lse_ref, mask_ref, h1_ref, wide):
    wb = ohm_ref.shape[0]
    for w in range(wb):
        x = x_ref[AREA * w:AREA * (w + 1), :].astype(F32)
        c, r = norm(x)
        xhat = c * r
        h1_ref[w, PADDED - 16:, :] = jnp.zeros((16, MODEL), BF16)
        xhat_ref[w, PADDED - 16:, :] = jnp.zeros((16, MODEL), BF16)
        h1_ref[w, 0:AREA, :] = (xhat * vec_ref[LN1_GAIN] + vec_ref[LN1_BIAS]).astype(BF16)
        mask_ref[AREA * w:AREA * (w + 1), :] = jnp.where(ohm_ref[w, 0:AREA, 14:15] < 0.0, 0.0, 1.0)
        xhat_ref[w, 0:AREA, :] = xhat.astype(BF16)

    for j, offset in enumerate((QUERY_BIAS, None, VALUE_BIAS)):
        cs = slice(j * MODEL, (j + 1) * MODEL)
        p = mm(h1_ref[...].reshape(wb * PADDED, MODEL), wqkv_ref[:, cs])
        p = p if offset is None else p + vec_ref[offset]
        qkv_ref[:, :, cs] = p.astype(BF16).reshape(wb, PADDED, MODEL)

    groups = PAIRS // TOGETHER

    @pl.loop(0, wb * groups)
    def _(it):
        w = it // groups
        base = (it - w * groups) * TOGETHER
        pairs = [base + n for n in range(TOGETHER)]
        lanes = lambda part, pair: pl.ds(pl.multiple_of(part * MODEL + pair * 128, 128), 128)
        qs = [qkv_ref[w, :, lanes(0, p)] for p in pairs]
        us = [mm(mix_ref[...], jnp.concatenate([q, q], axis=1), NT) for q in qs]
        vts = [mm(eye(128), qkv_ref[w, :, lanes(2, p)], NT).astype(BF16) for p in pairs]
        row = lax.broadcasted_iota(jnp.int32, (16, 1), 0)
        qas = []
        for p, u in zip(pairs, us):
            tabs = []
            for t in range(2):
                a = u[64 * t:64 * t + 64]
                for n, b in enumerate((8, 4, 2, 1)):
                    cond = shift_ref[4 * t + n:4 * t + n + 1, :] > 0
                    a = jnp.where(cond, pltpu.roll(a, 64 - b, 0), a)
                tabs.append(a)
            parts = [u[128:256].astype(BF16)]
            for h in range(2):
                ah = jnp.where(row == 14, 1.0, tabs[0][32 * h:32 * h + 16])
                aw = tabs[1][32 * h:32 * h + 16]
                hh, hl = split(ah)
                wh, wl = split(aw)
                parts += [hh, wh, hl, wl]
            qa = jnp.concatenate(parts, axis=0)
            qaug_ref[w, p] = qa
            qas.append(qa)
        keys = [key_side(qkv_ref[w, :, lanes(1, p)], ohm_ref[w]) for p in pairs]
        scores = [mm(key, query_side(qa, h)) for key, qa in zip(keys, qas) for h in range(2)]
        ots = []
        for n, s in enumerate(scores):
            p, h = pairs[n // 2], n % 2
            top = jnp.max(s, axis=0, keepdims=True)
            e = jnp.exp(s - top)
            total = jnp.sum(e, axis=0, keepdims=True)
            lse_ref[w, p, h:h + 1, :] = top + jnp.log(total)
            ots.append(mm(vts[n // 2][64 * h:64 * h + 64], e.astype(BF16)) * (1.0 / total))
        for n, p in enumerate(pairs):
            ot = jnp.concatenate(ots[2 * n:2 * n + 2], axis=0).astype(BF16)
            o_ref[w, :, lanes(0, p)] = mm(eye(PADDED), ot, NT).astype(BF16)

    wide[...] = mm(o_ref[...].reshape(wb * PADDED, MODEL), wproj_ref[...]) + vec_ref[PROJ_BIAS]
    for w in range(wb):
        x1_ref[AREA * w:AREA * (w + 1), :] = x_ref[AREA * w:AREA * (w + 1), :].astype(F32) + wide[PADDED * w:PADDED * w + AREA, :]


def cost(us):
    return pl.CostEstimate(flops=int(us * 1.0e9), bytes_accessed=1 << 20, transcendentals=0)


def once(a):
    return pl.BlockSpec(a.shape, lambda i: (0,) * a.ndim, pipeline_mode=pl.Buffered(1))


def blocked(*shape):
    return pl.BlockSpec(shape, lambda i: (i,) + (0,) * (len(shape) - 1))


def block_windows(windows):
    return 4 if windows % 4 == 0 else windows


def attention_forward(x, ohm, vec, wqkv, mix, shift, wproj):
    windows = ohm.shape[0]
    wb = block_windows(windows)
    outs = [((windows * AREA, MODEL), F32, (wb * AREA, MODEL)),
            ((windows, PADDED, MODEL), BF16, (wb, PADDED, MODEL)),
            ((windows, PADDED, 3 * MODEL), BF16, (wb, PADDED, 3 * MODEL)),
            ((windows, PAIRS, 256, PADDED), BF16, (wb, PAIRS, 256, PADDED)),
            ((windows, PADDED, MODEL), BF16, (wb, PADDED, MODEL)),
            ((windows, PAIRS, 2, PADDED), F32, (wb, PAIRS, 2, PADDED)),
            ((windows * AREA, 1), F32, (wb * AREA, 1))]
    return pl.pallas_call(
        forward_kernel,
        grid=(windows // wb,),
        in_specs=[blocked(wb * AREA, MODEL), blocked(wb, PADDED, 128)] + [once(a) for a in (vec, wqkv, mix, shift, wproj)],
        out_specs=[blocked(*b) for _, _, b in outs],
        out_shape=[jax.ShapeDtypeStruct(s, t) for s, t, _ in outs],
        scratch_shapes=[pltpu.VMEM((wb, PADDED, MODEL), BF16), pltpu.VMEM((wb * PADDED, MODEL), F32)],
        cost_estimate=cost(70),
        compiler_params=pltpu.CompilerParams(vmem_limit_bytes=VMEM_LIMIT, dimension_semantics=("arbitrary",)),
        name="attention_forward",
    )(x, ohm, vec, wqkv, mix, shift, wproj)


BLOCK = 384
BLOCKS = 4 * MODEL // BLOCK


def backward_kernel(da_ref, ohm_ref, oht_ref, qkv_ref, qaug_ref, lse_ref, wproj_ref, relt_ref, shift_ref, xhat_ref, o_ref, vec_ref,
                    wqkv_ref, dp_ref, grel_ref, dw_ref, sum_ref, gvec_ref, bvec_ref,
                    do_ref, dap_ref, turned, acc, wstage, dstage, wsems, dsems):
    wb = ohm_ref.shape[0]
    rows = wb * PADDED
    step = pl.program_id(0)

    @pl.when(step == 0)
    def _():
        grel_ref[...] = jnp.zeros_like(grel_ref)
        acc[...] = jnp.zeros_like(acc)
        turned[MODEL:, :] = jnp.ones((16, rows), BF16)

    for w in range(wb):
        dap_ref[w, PADDED - 16:, :] = jnp.zeros((16, MODEL), BF16)
        dap_ref[w, 0:AREA, :] = da_ref[AREA * w:AREA * (w + 1), :]
    dap = dap_ref[...].reshape(rows, MODEL)
    do_ref[...] = mm(dap, wproj_ref[...], NT).astype(BF16).reshape(wb, PADDED, MODEL)
    turned[0:MODEL, :] = o_ref[...].reshape(rows, MODEL).T
    acc[0:MODEL, 3 * MODEL:] += mm(turned[0:MODEL, :], dap)

    groups = PAIRS // TOGETHER_BACK

    @pl.loop(0, wb * groups)
    def _(it):
        w = it // groups
        base = (it - w * groups) * TOGETHER_BACK
        pairs = [base + n for n in range(TOGETHER_BACK)]
        lanes = lambda part, pair: pl.ds(pl.multiple_of(part * MODEL + pair * 128, 128), 128)
        both = [(n, p, h) for n, p in enumerate(pairs) for h in range(2)]
        qs = [qkv_ref[w, :, lanes(0, p)] for p in pairs]
        ks = [qkv_ref[w, :, lanes(1, p)] for p in pairs]
        vs = [qkv_ref[w, :, lanes(2, p)] for p in pairs]
        dos = [do_ref[w, :, lanes(0, p)] for p in pairs]
        scores = [mm(key_side(ks[n], ohm_ref[w]), query_side(qaug_ref[w, p], h)) for n, p, h in both]
        dots = [mm(eye(128), do, NT).astype(BF16) for do in dos]
        kts = [mm(eye(128, SCALE), k, NT).astype(BF16) for k in ks]
        z = jnp.zeros((HEAD_DIM, PADDED), BF16)
        dws = []
        for n, p, h in both:
            own = dots[n][64 * h:64 * h + 64]
            dws.append(mm(vs[n], jnp.concatenate([own, z] if h == 0 else [z, own], axis=0)))
        dvs, dks, dqs = [], [], []
        for s, dw, (n, p, h) in zip(scores, dws, both):
            a = jnp.exp(s - lse_ref[w, p, h:h + 1, :])
            t = a * dw
            dsb = (t - a * jnp.sum(t, axis=0, keepdims=True)).astype(BF16)
            dvs.append(mm(a.astype(BF16), dos[n]))
            dks.append(mm(dsb, qs[n]))
            dqs.append(mm(jnp.concatenate([kts[n][64 * h:64 * h + 64], oht_ref[...]], axis=0), dsb))
        first = lax.broadcasted_iota(jnp.int32, (1, 128), 1) < 64
        zz = jnp.zeros((16, PADDED), F32)
        dqts = []
        for n, p in enumerate(pairs):
            tabs = []
            for t in range(2):
                lo = 64 + 16 * t
                a = jnp.concatenate([dqs[2 * n][lo:lo + 16], zz, dqs[2 * n + 1][lo:lo + 16], zz], axis=0)
                for i, b in enumerate((8, 4, 2, 1)):
                    cond = shift_ref[4 * t + i:4 * t + i + 1, :] > 0
                    a = jnp.where(cond, pltpu.roll(a, b, 0), a)
                tabs.append(a.astype(BF16))
            dqt = []
            for h in range(2):
                du = jnp.concatenate([tabs[0][32 * h:32 * h + 32], tabs[1][32 * h:32 * h + 32]], axis=0)
                dqt.append(dqs[2 * n + h][0:64] + mm(relt_ref[...], jnp.concatenate([du, du], axis=0)))
                grel_ref[h] += mm(du, qs[n])
            dqts.append(jnp.concatenate(dqt, axis=0).astype(BF16))
        for n, p in enumerate(pairs):
            dq = mm(eye(PADDED), dqts[n], NT).astype(BF16)
            dk = (jnp.where(first, dks[2 * n], dks[2 * n + 1]) * SCALE).astype(BF16)
            dv = jnp.where(first, dvs[2 * n], dvs[2 * n + 1]).astype(BF16)
            dp_ref[w, :, lanes(0, p)] = dq
            dp_ref[w, :, lanes(1, p)] = dk
            dp_ref[w, :, lanes(2, p)] = dv

    turned[0:MODEL, :] = xhat_ref[...].reshape(rows, MODEL).T
    for j in range(3):
        cs = slice(j * MODEL, (j + 1) * MODEL)
        acc[:, cs] += mm(turned[...], dp_ref[:, :, cs].reshape(rows, MODEL))

    @pl.when(step == pl.num_programs(0) - 1)
    def _():
        columns = jnp.concatenate([vec_ref[...]] * 16, axis=0).T
        gain, bias = columns[:, 0:1], columns[:, 1:2]
        nq = 3 * MODEL // BLOCK
        sum_ref[...] = acc[MODEL:MODEL + 8, 0:3 * MODEL]
        gvec_ref[...] = jnp.zeros_like(gvec_ref)
        bvec_ref[...] = jnp.zeros_like(bvec_ref)
        take = lambda n: pltpu.make_async_copy(wqkv_ref.at[:, pl.ds(n * BLOCK, BLOCK)], wstage.at[n % 2], wsems.at[n % 2])
        give = lambda n: pltpu.make_async_copy(dstage.at[n % 2], dw_ref.at[n], dsems.at[n % 2])
        take(0).start()
        for n in range(BLOCKS):
            cs = slice(n * BLOCK, (n + 1) * BLOCK)
            if n + 1 < nq:
                take(n + 1).start()
            if n >= 2:
                give(n - 2).wait()
            m = acc[0:MODEL, cs]
            if n < nq:
                s = acc[MODEL:MODEL + 1, cs]
                take(n).wait()
                w = wstage[n % 2].astype(F32)
                g, b = w * m, w * s
                gvec_ref[...] += sum(g[:, 128 * i:128 * (i + 1)] for i in range(BLOCK // 128))
                bvec_ref[...] += sum(b[:, 128 * i:128 * (i + 1)] for i in range(BLOCK // 128))
                m = m * gain + bias * s
            dstage[n % 2] = m.astype(BF16)
            give(n).start()
        give(BLOCKS - 2).wait()
        give(BLOCKS - 1).wait()


def attention_backward(da, ohm, oht, qkv, qaug, lse, wproj, relt, shift, xhat, o, vec, wqkv):
    windows = ohm.shape[0]
    wb = block_windows(windows)
    fixed = lambda *shape: pl.BlockSpec(shape, lambda i: (0,) * len(shape))
    anywhere = pl.BlockSpec(memory_space=pl.ANY)
    return pl.pallas_call(
        backward_kernel,
        grid=(windows // wb,),
        in_specs=[blocked(wb * AREA, MODEL), blocked(wb, PADDED, 128), once(oht), blocked(wb, PADDED, 3 * MODEL),
                  blocked(wb, PAIRS, 256, PADDED), blocked(wb, PAIRS, 2, PADDED), once(wproj), once(relt), once(shift),
                  blocked(wb, PADDED, MODEL), blocked(wb, PADDED, MODEL), once(vec), anywhere],
        out_specs=[blocked(wb, PADDED, 3 * MODEL), fixed(2, 64, 128), anywhere, fixed(8, 3 * MODEL), fixed(MODEL, 128), fixed(MODEL, 128)],
        out_shape=[jax.ShapeDtypeStruct((windows, PADDED, 3 * MODEL), BF16), jax.ShapeDtypeStruct((2, 64, 128), F32),
                   jax.ShapeDtypeStruct((BLOCKS, MODEL, BLOCK), BF16), jax.ShapeDtypeStruct((8, 3 * MODEL), F32),
                   jax.ShapeDtypeStruct((MODEL, 128), F32), jax.ShapeDtypeStruct((MODEL, 128), F32)],
        scratch_shapes=[pltpu.VMEM((wb, PADDED, MODEL), BF16), pltpu.VMEM((wb, PADDED, MODEL), BF16),
                        pltpu.VMEM((MODEL + 16, wb * PADDED), BF16), pltpu.VMEM((MODEL + 16, 4 * MODEL), F32),
                        pltpu.VMEM((2, MODEL, BLOCK), BF16), pltpu.VMEM((2, MODEL, BLOCK), BF16),
                        pltpu.SemaphoreType.DMA((2,)), pltpu.SemaphoreType.DMA((2,))],
        cost_estimate=cost(95),
        compiler_params=pltpu.CompilerParams(vmem_limit_bytes=VMEM_LIMIT, dimension_semantics=("arbitrary",)),
        name="attention_backward",
    )(da, ohm, oht, qkv, qaug, lse, wproj, relt, shift, xhat, o, vec, wqkv)


def input_kernel(x_ref, da_ref, dp_ref, vec_ref, wqkv_ref, *rest):
    gx_ref, wide, tall = rest[-3:]
    wb = dp_ref.shape[0]
    wide[...] = mm(dp_ref[...].reshape(wb * PADDED, 3 * MODEL), wqkv_ref[...], NT)
    for w in range(wb):
        tall[AREA * w:AREA * (w + 1), :] = wide[PADDED * w:PADDED * w + AREA, :]
    rows = wb * AREA
    for lo in range(0, rows, 112):
        hi = min(lo + 112, rows)
        c, r = norm(x_ref[lo:hi, :].astype(F32))
        xhat = c * r
        dx = tall[lo:hi, :] * vec_ref[LN1_GAIN]
        dx = r * (dx - jnp.mean(dx, axis=-1, keepdims=True) - xhat * jnp.mean(dx * xhat, axis=-1, keepdims=True))
        gx_ref[lo:hi, :] = (dx + da_ref[lo:hi, :].astype(F32)).astype(BF16)


def input_gradient(x, da, dp, vec, wqkv, at, count, held):
    windows = dp.shape[0]
    wb = block_windows(windows)
    part = lambda *shape: pl.BlockSpec(shape, lambda i: (i + at,) + (0,) * (len(shape) - 1))
    extra = [] if held is None else [held]
    return pl.pallas_call(
        input_kernel,
        grid=(count,),
        in_specs=[part(wb * AREA, MODEL), part(wb * AREA, MODEL), part(wb, PADDED, 3 * MODEL), once(vec), once(wqkv)]
        + [pl.BlockSpec(memory_space=pl.ANY)] * len(extra),
        out_specs=part(wb * AREA, MODEL),
        out_shape=jax.ShapeDtypeStruct((windows * AREA, MODEL), BF16),
        input_output_aliases={5: 0} if extra else {},
        scratch_shapes=[pltpu.VMEM((wb * PADDED, MODEL), F32), pltpu.VMEM((wb * AREA, MODEL), F32)],
        cost_estimate=cost(5 * count),
        compiler_params=pltpu.CompilerParams(vmem_limit_bytes=VMEM_LIMIT, dimension_semantics=("arbitrary",)),
        name="input_gradient",
    )(x, da, dp, vec, wqkv, *extra)


def constant_tables():
    place = np.arange(PADDED)
    real = place < AREA
    r, c = np.where(real, place // WIN, 0), np.where(real, place % WIN, 0)
    hot = [((WIN - 1 - v)[:, None] == np.arange(16)) & real[:, None] for v in (r, c)]
    keys = np.concatenate(hot + hot, axis=1).astype(np.float32)
    shift = np.stack([(v >> b) & 1 for v in (r, c) for b in (3, 2, 1, 0)]).astype(np.int32)
    return keys, np.concatenate(hot, axis=1).T.astype(np.float32), shift


def small_tables(window_extent, rel_h, rel_w):
    keys, oht, shift = constant_tables()
    place = np.arange(PADDED)
    r, c = place // WIN, place % WIN
    valid = (r < window_extent[:, 0:1]) & (c < window_extent[:, 1:2]) & (place < AREA)
    keys = np.concatenate([keys, np.zeros((PADDED, 64), np.float32)], axis=1)
    flag = np.arange(128) == 14
    ohm = jnp.where(flag[None, None, :], jnp.where(valid, 0.0, NEGATIVE)[:, :, None], keys[None]).astype(BF16)
    both = jnp.pad(jnp.stack([rel_h, rel_w]), ((0, 0), (0, 5), (0, 0)))
    hi = both.astype(BF16).astype(F32)
    lo = both - hi
    parity = np.eye(2, dtype=np.float32)
    spread = lambda t: (t[:, None, :, None, :] * parity[None, :, None, :, None]).reshape(128, 128)
    ident = np.concatenate([SCALE * np.eye(128), np.zeros((128, 128))], axis=1).astype(np.float32)
    mix = jnp.concatenate([jnp.concatenate([spread(hi), spread(lo)], axis=1), ident], axis=0).astype(BF16)
    relt = jnp.concatenate([hi.reshape(64, HEAD_DIM), lo.reshape(64, HEAD_DIM)], axis=0).T.astype(BF16)
    return ohm, jnp.asarray(oht, BF16), jnp.asarray(shift), mix, relt


def gelu_parts(z):
    u = jnp.abs(z)
    t = 1.0 / (1.0 + 0.23164189 * u)
    e = jnp.exp(-0.5 * z * z)
    poly = t * (0.127414796 + t * (-0.142248368 + t * (0.7107068705 + t * (-0.7265760135 + t * 0.5307027145))))
    q = poly * e
    phi = jnp.where(z >= 0.0, 1.0 - q, q)
    return z * phi, phi + z * e * 0.3989422804


ROWS = 512
CHUNK = 64 * 12


def mlp_kernel(rows, widths, offset_ref, x1_ref, go_ref, mask_ref, par_ref, upb_ref, *rest):
    n = len(widths)
    ups, downs = rest[:n], rest[n:2 * n]
    out_ref, da_ref, dw_ref, dbu_ref, vec_ref, h2, dm, h2t, dmt, macc, dacc, accu, accd, stage, sems = rest[2 * n:]
    rb = h2.shape[0]
    ch = 256
    step = pl.program_id(0)

    @pl.when(step == 0)
    def _():
        accu[...] = jnp.zeros_like(accu)
        accd[...] = jnp.zeros_like(accd)
        dbu_ref[...] = jnp.zeros_like(dbu_ref)
        vec_ref[...] = jnp.zeros_like(vec_ref)

    def live(i):
        row = step * rb + i * ch + lax.broadcasted_iota(jnp.int32, (ch, 1), 0)
        return row < rows

    @pl.loop(0, rb // ch)
    def _(i):
        rs = pl.ds(pl.multiple_of(i * ch, ch), ch)
        x1 = jnp.where(live(i), x1_ref[rs, :], 0.0)
        c, r = norm(x1)
        h2[rs, :] = (c * r * par_ref[LN2_GAIN] + par_ref[LN2_BIAS]).astype(BF16)
        d = jnp.where(live(i) & (mask_ref[rs, :] > 0.0), go_ref[rs, :].astype(F32), 0.0)
        dm[rs, :] = d.astype(BF16)
        vec_ref[0:8, :] += fold8(d)

    h2t[...] = h2[...].T
    dmt[...] = dm[...].T

    at = 0
    for up_ref, down_ref, width in zip(ups, downs, widths):
        size = min(CHUNK, width)
        for lo in range(0, width, size):
            here, there = slice(lo, lo + size), slice(at, at + size)
            z = mm(h2[...], up_ref[:, here]) + upb_ref[:, there]
            dact = mm(dm[...], down_ref[:, here])
            g, gp = gelu_parts(z)
            g = g.astype(BF16)
            dz = (dact * gp).astype(BF16)
            dbu_ref[:, there] += fold8(dz.astype(F32))
            m = mm(g, down_ref[:, here], NT)
            macc[...] = m if at == 0 else macc[...] + m
            d = mm(dz, up_ref[:, here], NT)
            dacc[...] = d if at == 0 else dacc[...] + d
            accd[:, there] += mm(dmt[...], g)
            accu[:, there] += mm(h2t[...], dz)
            at += size

    @pl.loop(0, rb // ch)
    def _(i):
        rs = pl.ds(pl.multiple_of(i * ch, ch), ch)
        x1 = jnp.where(live(i), x1_ref[rs, :], 0.0)
        c, r = norm(x1)
        xhat = c * r
        valid = live(i) & (mask_ref[rs, :] > 0.0)
        out_ref[rs, :] = jnp.where(valid, x1 + macc[rs, :] + par_ref[DOWN_BIAS], 0.0).astype(BF16)
        dh = dacc[rs, :]
        vec_ref[8:16, :] += fold8(dh * xhat)
        vec_ref[16:24, :] += fold8(dh)
        dx = dh * par_ref[LN2_GAIN]
        dx = r * (dx - jnp.mean(dx, axis=-1, keepdims=True) - xhat * jnp.mean(dx * xhat, axis=-1, keepdims=True))
        da = (dx + dm[rs, :].astype(F32)).astype(BF16)
        da_ref[rs, :] = da
        vec_ref[24:32, :] += fold8(da.astype(F32))

    @pl.when(step == pl.num_programs(0) - 1)
    def _():
        size = stage.shape[2]
        each = accu.shape[1] // size

        def copy(k):
            to = pl.multiple_of(offset_ref[k], 128)
            return pltpu.make_async_copy(stage.at[k % 2], dw_ref.at[:, pl.ds(to, size)], sems.at[k % 2])
        for k in range(2 * each):
            if k >= 2:
                copy(k - 2).wait()
            src = (accu, accd)[k // each]
            stage[k % 2] = src[:, (k % each) * size:(k % each + 1) * size].astype(BF16)
            copy(k).start()
        copy(2 * each - 2).wait()
        copy(2 * each - 1).wait()


def mlp(x1, go, mask, par, upb, ups, downs, offsets):
    rows, d = x1.shape
    widths = tuple(u.shape[1] for u in ups)
    ff = sum(widths)
    size = 2 * ff // offsets.shape[0]
    rb = ROWS
    full = lambda a: pl.BlockSpec(a.shape, lambda i, _: (0, 0), pipeline_mode=pl.Buffered(1))
    rowspec = lambda w: pl.BlockSpec((rb, w), lambda i, _: (i, 0))
    return pl.pallas_call(
        functools.partial(mlp_kernel, rows, widths),
        grid_spec=pltpu.PrefetchScalarGridSpec(
            num_scalar_prefetch=1,
            grid=(pl.cdiv(rows, rb),),
            in_specs=[rowspec(d), rowspec(d), rowspec(1)] + [full(a) for a in (par, upb, *ups, *downs)],
            out_specs=[rowspec(d), rowspec(d), pl.BlockSpec(memory_space=pl.ANY),
                       pl.BlockSpec((8, ff), lambda i, _: (0, 0)), pl.BlockSpec((32, d), lambda i, _: (0, 0))],
            scratch_shapes=[pltpu.VMEM((rb, d), BF16), pltpu.VMEM((rb, d), BF16), pltpu.VMEM((d, rb), BF16), pltpu.VMEM((d, rb), BF16),
                            pltpu.VMEM((rb, d), F32), pltpu.VMEM((rb, d), F32), pltpu.VMEM((d, ff), F32), pltpu.VMEM((d, ff), F32),
                            pltpu.VMEM((2, d, size), BF16), pltpu.SemaphoreType.DMA((2,))]),
        out_shape=[jax.ShapeDtypeStruct((rows, d), BF16), jax.ShapeDtypeStruct((rows, d), BF16),
                   jax.ShapeDtypeStruct((d, 2 * ff), BF16), jax.ShapeDtypeStruct((8, ff), F32), jax.ShapeDtypeStruct((32, d), F32)],
        cost_estimate=cost(170),
        compiler_params=pltpu.CompilerParams(vmem_limit_bytes=VMEM_LIMIT, dimension_semantics=("arbitrary",)),
        name="mlp",
    )(offsets, x1, go, mask, par, upb, *ups, *downs)


def bits(n):
    return n.bit_length() - 1


def swap(value, axis, bit, sizes):
    return lax.ppermute(value, axis, [(i, i ^ (1 << bit)) for i in range(sizes[axis])])


def bit_of(axis, bit):
    return (lax.axis_index(axis) >> bit) & 1


def add(a, b):
    return (a.astype(F32) + b.astype(F32)).astype(BF16)


def split_dp(held, at, bit):
    mine = bit_of("dp", bit)
    return tuple(lax.dynamic_index_in_dim(held, m, at, keepdims=False) for m in (mine, 1 - mine))


def split_mlp(held, owners, bit):
    mine = bit_of("mlp", bit) == 1
    sides = []
    for side in range(2):
        runs = [n for n, o in enumerate(owners) if (o >> bit) & 1 == side]
        sides.append(jnp.concatenate([held[n:n + 1] for n in runs], axis=0))
    return jnp.where(mine, sides[1], sides[0]), jnp.where(mine, sides[0], sides[1])


def reduce_steps(blocks, owners, sizes):
    nb, nm = bits(sizes["dp"]), bits(sizes["mlp"])
    count, rows, cols = blocks.shape
    held = blocks.reshape((count,) + (2,) * nb + (rows // sizes["dp"], cols))
    keep, send = split_dp(held, nb, 0)
    got = yield [("dp", 0, send)]
    held = add(keep, got[0])
    orders = ([("mlp", b) for b in reversed(range(nm))] + [("dp", 1)], [("dp", 1)] + [("mlp", b) for b in reversed(range(nm))])
    halves = [held[:, 0], held[:, 1]]
    left = [list(owners), list(owners)]
    dims = [nb - 2, nb - 2]
    plan = list(zip(*orders)) + [(("dp", b), ("dp", b)) for b in range(2, nb - 1)]
    for both in plan:
        kept, sends = [], []
        for n, (axis, bit) in enumerate(both):
            if axis == "mlp":
                keep, send = split_mlp(halves[n], left[n], bit)
                mine = [o for o in left[n] if (o >> bit) & 1 == 0]
                left[n] = [o & ~(1 << bit) for o in mine]
            else:
                keep, send = split_dp(halves[n], dims[n], bit)
                dims[n] -= 1
            kept.append(keep)
            sends.append((axis, bit, send))
        got = yield sends
        halves = [add(k, g) for k, g in zip(kept, got)]
    mine = bit_of("dp", nb - 1) == 1
    got = yield [("dp", nb - 1, jnp.where(mine, halves[0], halves[1]))]
    yield add(jnp.where(mine, halves[1], halves[0]), got[0])


def sum_steps(v, sizes):
    for axis in ("dp", "mlp"):
        for b in range(bits(sizes[axis])):
            got = yield [(axis, b, v)]
            v = v + got[0]
    yield v


def pair_steps(v, width):
    mine = lax.axis_index("mlp") == 1
    low, high = v[:, :width], v[:, width:]
    got = yield [("mlp", 0, jnp.where(mine, low, high))]
    yield add(jnp.where(mine, high, low), got[0])


def run_steps(tasks, delays, work, sizes):
    states = [next(t) if not d else None for t, d in zip(tasks, delays)]
    results = [None] * len(tasks)
    turn = 0
    while any(r is None for r in results):
        turn += 1
        sends = [(n, s) for n, state in enumerate(states) if isinstance(state, list) for s in state]
        values = work(turn, [s[2] for _, s in sends], [swap_by(s[0], s[1], sizes) for _, s in sends])
        for n, task in enumerate(tasks):
            if isinstance(states[n], list):
                states[n] = task.send([v for v, (owner, _) in zip(values, sends) if owner == n])
                if not isinstance(states[n], list):
                    results[n] = states[n]
            elif results[n] is None and turn >= delays[n]:
                states[n] = next(task)
    return results


def swap_by(axis, bit, sizes):
    return lambda v: swap(v, axis, bit, sizes)


def feed_forward_weights(up, up_bias, down, sizes):
    width = up.shape[1]
    if sizes["mlp"] != 2:
        gather = lambda v: lax.all_gather(v, "mlp", axis=v.ndim - 1, tiled=True)
        count = sizes["mlp"]
        return [gather(up)], [gather(down)], gather(up_bias), jnp.arange(count, dtype=jnp.int32) * width, width
    half = width // 2
    core, me = bit_of("dp", 0), lax.axis_index("mlp")
    cut = lambda v: jnp.where(core == 1, v[:, half:], v[:, :half])
    far_up, far_down = swap(cut(up), "mlp", 0, sizes), swap(cut(down), "mlp", 0, sizes)
    far_bias = swap(up_bias, "mlp", 0, sizes)
    bias = jnp.concatenate([up_bias, jnp.roll(far_bias, -core * half)])
    places = jnp.stack([me * width, me * width + half, (1 - me) * width + core * half, (1 - me) * width + (1 - core) * half])
    return (up, far_up), (down, far_down), bias, places.astype(jnp.int32), half


def per_device(
    sizes,
    tokens,
    window_extent,
    ln1_gain,
    ln1_bias,
    qkv_weight,
    query_bias,
    value_bias,
    rel_h,
    rel_w,
    proj_weight,
    proj_bias,
    ln2_gain,
    ln2_bias,
    up_weight,
    up_bias,
    down_weight,
    down_bias,
    grad_out,
):
    owners = sizes["mlp"]
    line = lambda v: v.reshape(1, -1)
    ups, downs, up_bias_here, places, piece = feed_forward_weights(up_weight, up_bias, down_weight, sizes)
    ohm, oht, shift, mix, relt = small_tables(window_extent, rel_h, rel_w)
    par = jnp.stack([ln1_gain, ln1_bias, query_bias, value_bias, proj_bias, ln2_gain, ln2_bias, down_bias])
    x1, xhat, qkv, qaug, o, lse, row_mask = attention_forward(tokens, ohm, par, qkv_weight, mix, shift, proj_weight)
    if owners == 2:
        (ups, downs, x1) = lax.optimization_barrier((ups, downs, x1))
        ups, downs = list(ups) + [swap(ups[1], "dp", 0, sizes)], list(downs) + [swap(downs[1], "dp", 0, sizes)]
    width = up_weight.shape[1]
    ff = width * owners
    by_owner = (places // width) * (2 * width) + places % width
    output, da, dw_mlp, up_sums, mid_sums = mlp(
        x1, grad_out, row_mask, par, line(up_bias_here), ups, downs,
        jnp.concatenate([by_owner, by_owner + width]))
    dw_mlp = lax.psum_scatter(dw_mlp, "dp", scatter_dimension=0, tiled=True)
    if owners != 2:
        dw_mlp = lax.psum_scatter(dw_mlp, "mlp", scatter_dimension=1, tiled=True)
    dp_all, grel, dw_late, dp_sums, gain_sums, bias_sums = attention_backward(
        da, ohm, oht, qkv, qaug, lse, proj_weight, relt, shift, xhat, o, par, qkv_weight)
    up_sum = jnp.sum(up_sums, axis=0).reshape(-1, piece)
    up_sum = sum(jnp.where(jnp.arange(ff) // piece == places[n] // piece, jnp.tile(up_sum[n], ff // piece), 0.0)
                 for n in range(ff // piece))
    block_owners = [0, 0, 0, 1, 1, 1, 0, 1]
    if owners != 2:
        qkv_part, proj_part = (jnp.moveaxis(v, 0, 1).reshape(MODEL, owners, -1) for v in (dw_late[:6], dw_late[6:]))
        dw_late = jnp.moveaxis(jnp.concatenate([qkv_part, proj_part], axis=2), 1, 0)
        block_owners = list(range(owners))
    rel = grel[0, :, :HEAD_DIM] + grel[1, :, HEAD_DIM:]
    mid = jnp.sum(mid_sums.reshape(4, 8, MODEL), axis=1)
    sums = jnp.concatenate([jnp.sum(gain_sums, axis=1), jnp.sum(bias_sums, axis=1), dp_sums[0], rel.reshape(-1), mid.reshape(-1), up_sum])
    blocks = dp_all.shape[0] // block_windows(dp_all.shape[0])
    held = {"gx": None, "da": da, "at": 0}

    def input_part(count):
        held["gx"] = input_gradient(tokens, held["da"], dp_all, par, qkv_weight, held["at"], count, held["gx"])
        held["at"] += count

    def work(turn, values, swaps):
        if held["at"] >= blocks:
            return [f(v) for f, v in zip(swaps, values)]
        values, held["da"] = lax.optimization_barrier((values, held["da"]))
        got = [f(v) for f, v in zip(swaps, values)]
        input_part(1)
        got, held["gx"] = lax.optimization_barrier((got, held["gx"]))
        return got

    tasks = [reduce_steps(dw_late, block_owners, sizes), sum_steps(sums, sizes)]
    delays = [0, 0]
    if owners == 2:
        tasks.append(pair_steps(dw_mlp, 2 * width))
        delays.append(1)
    results = run_steps(tasks, delays, work, sizes)
    late, sums = results[0].astype(F32), results[1]
    late = jnp.concatenate([late[n] for n in range(late.shape[0])], axis=1)
    if owners == 2:
        dw_mlp = results[2]
    if held["at"] < blocks:
        input_part(blocks - held["at"])
    grad_tokens = held["gx"]
    d = MODEL
    table = 2 * WIN - 1
    n_rel = 64 * HEAD_DIM
    rel = sums[5 * d:5 * d + n_rel].reshape(64, HEAD_DIM)
    mid = sums[5 * d + n_rel:]
    cols = 3 * MODEL // owners
    dw_mlp = dw_mlp.astype(F32)
    return (
        output,
        grad_tokens,
        sums[0:d],
        sums[d:2 * d],
        late[:, :cols],
        sums[2 * d:3 * d],
        sums[4 * d:5 * d],
        rel[0:table],
        rel[32:32 + table],
        late[:, cols:],
        mid[3 * d:4 * d],
        mid[d:2 * d],
        mid[2 * d:3 * d],
        dw_mlp[:, :width],
        mid[4 * d:],
        dw_mlp[:, width:],
        mid[0:d],
    )


def solution(mesh):
    rows = P(("dp", "mlp"), None)
    in_specs = (rows, rows, P(), P(), P(), P(), P(), P(), P(), P(), P(), P(), P(),
                P(None, "mlp"), P("mlp"), P(None, "mlp"), P(), rows)
    block = P("dp", "mlp")
    out_specs = (rows, rows, P(), P(), block, P(), P(), P(), P(), block, P(), P(), P(), block, P(), block, P())
    sizes = {name: mesh.shape[name] for name in ("dp", "mlp")}
    return jax.shard_map(
        functools.partial(per_device, sizes), mesh=mesh, in_specs=in_specs, out_specs=out_specs, check_vma=False)
```

```python
import functools
import jax
import jax.numpy as jnp
import numpy as np
from jax import lax
from jax.experimental import pallas as pl
from jax.experimental.pallas import tpu as pltpu
from jax.sharding import PartitionSpec as P

HEADS = 12
HEAD_DIM = 64
WIN = 14
AREA = WIN * WIN
PADDED = 208
PAIRS = HEADS // 2
MODEL = HEADS * HEAD_DIM
EPSILON = 1e-6
NEGATIVE = -1e30
SCALE = HEAD_DIM ** -0.5
F32 = jnp.float32
BF16 = jnp.bfloat16
NN = (((1,), (0,)), ((), ()))
NT = (((1,), (1,)), ((), ()))
TN = (((0,), (0,)), ((), ()))
TOGETHER = 6
TOGETHER_BACK = 6
LN1_GAIN, LN1_BIAS, QUERY_BIAS, VALUE_BIAS, PROJ_BIAS, LN2_GAIN, LN2_BIAS, DOWN_BIAS = (slice(n, n + 1) for n in range(8))
VMEM_LIMIT = 60 * 1024 * 1024


def mm(a, b, dims=NN):
    return lax.dot_general(a, b, dims, preferred_element_type=F32)


def fold8(v):
    return jnp.sum(v.reshape(v.shape[0] // 8, 8, v.shape[1]), axis=0)


def norm(v):
    mu = jnp.mean(v, axis=-1, keepdims=True)
    c = v - mu
    return c, lax.rsqrt(jnp.mean(c * c, axis=-1, keepdims=True) + EPSILON)


def eye(n, value=1.0):
    r = lax.broadcasted_iota(jnp.int32, (n, n), 0)
    c = lax.broadcasted_iota(jnp.int32, (n, n), 1)
    return jnp.where(r == c, value, 0.0).astype(BF16)


def skew_bits(which):
    lane = lax.broadcasted_iota(jnp.int32, (1, PADDED), 1)
    r = lane // WIN
    return WIN - 1 - (jnp.minimum(r, WIN - 1) if which == 0 else lane - r * WIN)


def split(v):
    hi = v.astype(BF16)
    return hi, (v - hi.astype(F32)).astype(BF16)


def key_side(k, ohm):
    return jnp.concatenate([k, ohm], axis=1)


def query_side(qa, h):
    z = jnp.zeros((HEAD_DIM, PADDED), BF16)
    own = qa[h * 64:(h + 1) * 64]
    bias = qa[128 + 64 * h:192 + 64 * h]
    return jnp.concatenate(([own, z] if h == 0 else [z, own]) + [bias, z], axis=0)


def forward_kernel(live, x_ref, go_ref, ohm_ref, vec_ref, wqkv_ref, mix_ref, shift_ref, wproj_ref, *rest):
    x1_ref, xhat_ref, qkv_ref, qaug_ref, o_ref, lse_ref, mask_ref, dm_ref, h1_ref, wide = rest[-10:]
    rows = live * PADDED
    for w in range(live):
        here = slice(AREA * w, AREA * (w + 1))
        c, r = norm(x_ref[here, :].astype(F32))
        xhat = c * r
        valid = jnp.where(ohm_ref[w, 0:AREA, 14:15] < 0.0, 0.0, 1.0)
        h1_ref[w, PADDED - 16:, :] = jnp.zeros((16, MODEL), BF16)
        xhat_ref[w, PADDED - 16:, :] = jnp.zeros((16, MODEL), BF16)
        h1_ref[w, 0:AREA, :] = (xhat * vec_ref[LN1_GAIN] + vec_ref[LN1_BIAS]).astype(BF16)
        xhat_ref[w, 0:AREA, :] = xhat.astype(BF16)
        mask_ref[here, :] = valid
        dm_ref[here, :] = (go_ref[here, :].astype(F32) * valid).astype(BF16)
    for w in range(live, xhat_ref.shape[0]):
        xhat_ref[w] = jnp.zeros((PADDED, MODEL), BF16)
        o_ref[w] = jnp.zeros((PADDED, MODEL), BF16)

    for j, offset in enumerate((QUERY_BIAS, None, VALUE_BIAS)):
        cs = slice(j * MODEL, (j + 1) * MODEL)
        p = mm(h1_ref[0:live].reshape(rows, MODEL), wqkv_ref[:, cs])
        p = p if offset is None else p + vec_ref[offset]
        qkv_ref[0:live, :, cs] = p.astype(BF16).reshape(live, PADDED, MODEL)

    groups = PAIRS // TOGETHER

    @pl.loop(0, live * groups)
    def _(it):
        w = it // groups
        base = (it - w * groups) * TOGETHER
        pairs = [base + n for n in range(TOGETHER)]
        lanes = lambda part, pair: pl.ds(pl.multiple_of(part * MODEL + pair * 128, 128), 128)
        qs = [qkv_ref[w, :, lanes(0, p)] for p in pairs]
        us = [mm(mix_ref[...], jnp.concatenate([q, q], axis=1), NT) for q in qs]
        vts = [mm(eye(128), qkv_ref[w, :, lanes(2, p)], NT).astype(BF16) for p in pairs]
        row = lax.broadcasted_iota(jnp.int32, (16, 1), 0)
        qas = []
        for p, u in zip(pairs, us):
            tabs = []
            for t in range(2):
                a = u[64 * t:64 * t + 64]
                for n, b in enumerate((8, 4, 2, 1)):
                    cond = shift_ref[4 * t + n:4 * t + n + 1, :] > 0
                    a = jnp.where(cond, pltpu.roll(a, 64 - b, 0), a)
                tabs.append(a)
            parts = [u[128:256].astype(BF16)]
            for h in range(2):
                ah = jnp.where(row == 14, 1.0, tabs[0][32 * h:32 * h + 16])
                aw = tabs[1][32 * h:32 * h + 16]
                hh, hl = split(ah)
                wh, wl = split(aw)
                parts += [hh, wh, hl, wl]
            qa = jnp.concatenate(parts, axis=0)
            qaug_ref[w, p] = qa
            qas.append(qa)
        keys = [key_side(qkv_ref[w, :, lanes(1, p)], ohm_ref[w]) for p in pairs]
        scores = [mm(key, query_side(qa, h)) for key, qa in zip(keys, qas) for h in range(2)]
        ots = []
        for n, s in enumerate(scores):
            p, h = pairs[n // 2], n % 2
            top = jnp.max(s, axis=0, keepdims=True)
            e = jnp.exp(s - top)
            total = jnp.sum(e, axis=0, keepdims=True)
            lse_ref[w, p, h:h + 1, :] = top + jnp.log(total)
            ots.append(mm(vts[n // 2][64 * h:64 * h + 64], e.astype(BF16)) * (1.0 / total))
        for n, p in enumerate(pairs):
            ot = jnp.concatenate(ots[2 * n:2 * n + 2], axis=0).astype(BF16)
            o_ref[w, :, lanes(0, p)] = mm(eye(PADDED), ot, NT).astype(BF16)

    wide[0:rows, :] = mm(o_ref[0:live].reshape(rows, MODEL), wproj_ref[...]) + vec_ref[PROJ_BIAS]
    for w in range(live):
        here = slice(AREA * w, AREA * (w + 1))
        x1_ref[here, :] = x_ref[here, :].astype(F32) + wide[PADDED * w:PADDED * w + AREA, :]


def cost(us):
    return pl.CostEstimate(flops=int(us * 1.0e9), bytes_accessed=1 << 20, transcendentals=0)


def once(a):
    return pl.BlockSpec(a.shape, lambda i: (0,) * a.ndim, pipeline_mode=pl.Buffered(1))


def blocked(*shape):
    return pl.BlockSpec(shape, lambda i: (i,) + (0,) * (len(shape) - 1))


def block_windows(windows):
    return 4 if windows % 4 == 0 else windows


def attention_forward(x, go, ohm, vec, wqkv, mix, shift, wproj, windows, at, count, live, held):
    wb = block_windows(windows)
    outs = [((windows * AREA, MODEL), F32, (wb * AREA, MODEL)),
            ((windows, PADDED, MODEL), BF16, (wb, PADDED, MODEL)),
            ((windows, PADDED, 3 * MODEL), BF16, (wb, PADDED, 3 * MODEL)),
            ((windows, PAIRS, 256, PADDED), BF16, (wb, PAIRS, 256, PADDED)),
            ((windows, PADDED, MODEL), BF16, (wb, PADDED, MODEL)),
            ((windows, PAIRS, 2, PADDED), F32, (wb, PAIRS, 2, PADDED)),
            ((windows * AREA, 1), F32, (wb * AREA, 1)),
            ((windows * AREA, MODEL), BF16, (wb * AREA, MODEL))]
    part = lambda *shape: pl.BlockSpec(shape, lambda i: (i + at,) + (0,) * (len(shape) - 1))
    extra = list(held or [])
    return pl.pallas_call(
        functools.partial(forward_kernel, live),
        grid=(count,),
        in_specs=[blocked(wb * AREA, MODEL), blocked(wb * AREA, MODEL), blocked(wb, PADDED, 128)]
        + [once(a) for a in (vec, wqkv, mix, shift, wproj)] + [pl.BlockSpec(memory_space=pl.ANY)] * len(extra),
        out_specs=[part(*b) for _, _, b in outs],
        out_shape=[jax.ShapeDtypeStruct(s, t) for s, t, _ in outs],
        input_output_aliases={8 + n: n for n in range(len(extra))},
        scratch_shapes=[pltpu.VMEM((wb, PADDED, MODEL), BF16), pltpu.VMEM((wb * PADDED, MODEL), F32)],
        cost_estimate=cost(14 * count * live // wb),
        compiler_params=pltpu.CompilerParams(vmem_limit_bytes=VMEM_LIMIT, dimension_semantics=("arbitrary",)),
        name="attention_forward",
    )(x, go, ohm, vec, wqkv, mix, shift, wproj, *extra)


BLOCK = 384
BLOCKS = 4 * MODEL // BLOCK


def backward_kernel(live, core_ref, da_ref, ohm_ref, oht_ref, qkv_ref, qaug_ref, lse_ref, wproj_ref, relt_ref, shift_ref, xhat_ref, o_ref, vec_ref,
                    wqkv_ref, dp_ref, grel_ref, keep_ref, send_ref, sum_ref, gvec_ref, bvec_ref,
                    do_ref, dap_ref, turned, acc, wstage, dstage, wsems, dsems):
    wb = ohm_ref.shape[0]
    rows = wb * PADDED
    step = pl.program_id(0)

    @pl.when(step == 0)
    def _():
        grel_ref[...] = jnp.zeros_like(grel_ref)
        acc[...] = jnp.zeros_like(acc)
        turned[MODEL:, :] = jnp.ones((16, rows), BF16)

    for w in range(wb):
        dap_ref[w, PADDED - 16:, :] = jnp.zeros((16, MODEL), BF16)
        dap_ref[w, 0:AREA, :] = da_ref[AREA * w:AREA * (w + 1), :]
    final = step == pl.num_programs(0) - 1
    if live < wb:
        @pl.when(final)
        def _():
            dap_ref[live:] = jnp.zeros((wb - live, PADDED, MODEL), BF16)
            dp_ref[live:] = jnp.zeros((wb - live, PADDED, 3 * MODEL), BF16)
    dap = dap_ref[...].reshape(rows, MODEL)
    do_ref[...] = mm(dap, wproj_ref[...], NT).astype(BF16).reshape(wb, PADDED, MODEL)
    turned[0:MODEL, :] = o_ref[...].reshape(rows, MODEL).T
    acc[0:MODEL, 3 * MODEL:] += mm(turned[0:MODEL, :], dap)

    groups = PAIRS // TOGETHER_BACK

    @pl.loop(0, jnp.where(final, live, wb) * groups)
    def _(it):
        w = it // groups
        base = (it - w * groups) * TOGETHER_BACK
        pairs = [base + n for n in range(TOGETHER_BACK)]
        lanes = lambda part, pair: pl.ds(pl.multiple_of(part * MODEL + pair * 128, 128), 128)
        both = [(n, p, h) for n, p in enumerate(pairs) for h in range(2)]
        qs = [qkv_ref[w, :, lanes(0, p)] for p in pairs]
        ks = [qkv_ref[w, :, lanes(1, p)] for p in pairs]
        vs = [qkv_ref[w, :, lanes(2, p)] for p in pairs]
        dos = [do_ref[w, :, lanes(0, p)] for p in pairs]
        scores = [mm(key_side(ks[n], ohm_ref[w]), query_side(qaug_ref[w, p], h)) for n, p, h in both]
        dots = [mm(eye(128), do, NT).astype(BF16) for do in dos]
        kts = [mm(eye(128, SCALE), k, NT).astype(BF16) for k in ks]
        z = jnp.zeros((HEAD_DIM, PADDED), BF16)
        dws = []
        for n, p, h in both:
            own = dots[n][64 * h:64 * h + 64]
            dws.append(mm(vs[n], jnp.concatenate([own, z] if h == 0 else [z, own], axis=0)))
        dvs, dks, dqs = [], [], []
        for s, dw, (n, p, h) in zip(scores, dws, both):
            a = jnp.exp(s - lse_ref[w, p, h:h + 1, :])
            t = a * dw
            dsb = (t - a * jnp.sum(t, axis=0, keepdims=True)).astype(BF16)
            dvs.append(mm(a.astype(BF16), dos[n]))
            dks.append(mm(dsb, qs[n]))
            dqs.append(mm(jnp.concatenate([kts[n][64 * h:64 * h + 64], oht_ref[...]], axis=0), dsb))
        first = lax.broadcasted_iota(jnp.int32, (1, 128), 1) < 64
        zz = jnp.zeros((16, PADDED), F32)
        dqts = []
        for n, p in enumerate(pairs):
            tabs = []
            for t in range(2):
                lo = 64 + 16 * t
                a = jnp.concatenate([dqs[2 * n][lo:lo + 16], zz, dqs[2 * n + 1][lo:lo + 16], zz], axis=0)
                for i, b in enumerate((8, 4, 2, 1)):
                    cond = shift_ref[4 * t + i:4 * t + i + 1, :] > 0
                    a = jnp.where(cond, pltpu.roll(a, b, 0), a)
                tabs.append(a.astype(BF16))
            dqt = []
            for h in range(2):
                du = jnp.concatenate([tabs[0][32 * h:32 * h + 32], tabs[1][32 * h:32 * h + 32]], axis=0)
                dqt.append(dqs[2 * n + h][0:64] + mm(relt_ref[...], jnp.concatenate([du, du], axis=0)))
                grel_ref[h] += mm(du, qs[n])
            dqts.append(jnp.concatenate(dqt, axis=0).astype(BF16))
        for n, p in enumerate(pairs):
            dq = mm(eye(PADDED), dqts[n], NT).astype(BF16)
            dk = (jnp.where(first, dks[2 * n], dks[2 * n + 1]) * SCALE).astype(BF16)
            dv = jnp.where(first, dvs[2 * n], dvs[2 * n + 1]).astype(BF16)
            dp_ref[w, :, lanes(0, p)] = dq
            dp_ref[w, :, lanes(1, p)] = dk
            dp_ref[w, :, lanes(2, p)] = dv

    turned[0:MODEL, :] = xhat_ref[...].reshape(rows, MODEL).T
    for j in range(3):
        cs = slice(j * MODEL, (j + 1) * MODEL)
        acc[:, cs] += mm(turned[...], dp_ref[:, :, cs].reshape(rows, MODEL))

    @pl.when(final)
    def _():
        columns = jnp.concatenate([vec_ref[...]] * 16, axis=0).T
        gain, bias = columns[:, 0:1], columns[:, 1:2]
        nq = 3 * MODEL // BLOCK
        sum_ref[...] = acc[MODEL:MODEL + 8, 0:3 * MODEL]
        gsum, bsum = jnp.zeros((MODEL, 128), F32), jnp.zeros((MODEL, 128), F32)
        take = lambda n: pltpu.make_async_copy(wqkv_ref.at[:, pl.ds(n * BLOCK, BLOCK)], wstage.at[n % 2], wsems.at[n % 2])
        core = core_ref[0]

        def give(n, act):
            for k, to, c in ((0, keep_ref, core), (1, send_ref, 1 - core)):
                act(pltpu.make_async_copy(dstage.at[n % 2, :, c], to.at[n], dsems.at[n % 2, k]))
        start, wait = (lambda cp: cp.start()), (lambda cp: cp.wait())
        take(0).start()
        for n in range(BLOCKS):
            cs = slice(n * BLOCK, (n + 1) * BLOCK)
            if n + 1 < nq:
                take(n + 1).start()
            if n >= 2:
                give(n - 2, wait)
            m = acc[0:MODEL, cs]
            if n < nq:
                s = acc[MODEL:MODEL + 1, cs]
                take(n).wait()
                w = wstage[n % 2].astype(F32)
                g, b = w * m, w * s
                gsum += sum(g[:, 128 * i:128 * (i + 1)] for i in range(BLOCK // 128))
                bsum += sum(b[:, 128 * i:128 * (i + 1)] for i in range(BLOCK // 128))
                m = m * gain + bias * s
            dstage[n % 2] = m.astype(BF16).reshape(dstage.shape[1:])
            give(n, start)
        gvec_ref[...] = jnp.broadcast_to(jnp.sum(gsum.T, axis=0, keepdims=True), gvec_ref.shape)
        bvec_ref[...] = jnp.broadcast_to(jnp.sum(bsum.T, axis=0, keepdims=True), bvec_ref.shape)
        give(BLOCKS - 2, wait)
        give(BLOCKS - 1, wait)


def attention_backward(da, ohm, oht, qkv, qaug, lse, wproj, relt, shift, xhat, o, vec, wqkv, core, dp_size, live):
    windows = ohm.shape[0]
    wb = block_windows(windows)
    block = lambda *shape: pl.BlockSpec(shape, lambda i, _: (i,) + (0,) * (len(shape) - 1))
    whole = lambda a: pl.BlockSpec(a.shape, lambda i, _: (0,) * a.ndim, pipeline_mode=pl.Buffered(1))
    row = MODEL // dp_size
    fixed = lambda *shape: pl.BlockSpec(shape, lambda i, _: (0,) * len(shape))
    anywhere = pl.BlockSpec(memory_space=pl.ANY)
    return pl.pallas_call(
        functools.partial(backward_kernel, live),
        grid_spec=pltpu.PrefetchScalarGridSpec(
            num_scalar_prefetch=1,
            grid=(windows // wb,),
            in_specs=[block(wb * AREA, MODEL), block(wb, PADDED, 128), whole(oht), block(wb, PADDED, 3 * MODEL),
                  block(wb, PAIRS, 256, PADDED), block(wb, PAIRS, 2, PADDED), whole(wproj), whole(relt), whole(shift),
                  block(wb, PADDED, MODEL), block(wb, PADDED, MODEL), whole(vec), anywhere],
        out_specs=[block(wb, PADDED, 3 * MODEL), fixed(2, 64, 128), anywhere, anywhere, fixed(8, 3 * MODEL), fixed(8, MODEL), fixed(8, MODEL)],
        scratch_shapes=[pltpu.VMEM((wb, PADDED, MODEL), BF16), pltpu.VMEM((wb, PADDED, MODEL), BF16),
                        pltpu.VMEM((MODEL + 16, wb * PADDED), BF16), pltpu.VMEM((MODEL + 16, 4 * MODEL), F32),
                        pltpu.VMEM((2, MODEL, BLOCK), BF16), pltpu.VMEM((2, dp_size // 2, 2, row, BLOCK), BF16),
                        pltpu.SemaphoreType.DMA((2,)), pltpu.SemaphoreType.DMA((2, 2))]),
        out_shape=[jax.ShapeDtypeStruct((windows, PADDED, 3 * MODEL), BF16), jax.ShapeDtypeStruct((2, 64, 128), F32),
                   jax.ShapeDtypeStruct((BLOCKS, dp_size // 2, row, BLOCK), BF16),
                   jax.ShapeDtypeStruct((BLOCKS, dp_size // 2, row, BLOCK), BF16), jax.ShapeDtypeStruct((8, 3 * MODEL), F32),
                   jax.ShapeDtypeStruct((8, MODEL), F32), jax.ShapeDtypeStruct((8, MODEL), F32)],
        cost_estimate=cost(95),
        compiler_params=pltpu.CompilerParams(vmem_limit_bytes=VMEM_LIMIT, dimension_semantics=("arbitrary",)),
        name="attention_backward",
    )(core, da, ohm, oht, qkv, qaug, lse, wproj, relt, shift, xhat, o, vec, wqkv)


def input_kernel(live, x_ref, da_ref, dp_ref, vec_ref, wqkv_ref, *rest):
    gx_ref, wide, tall = rest[-3:]
    wide[0:live * PADDED, :] = mm(dp_ref[0:live].reshape(live * PADDED, 3 * MODEL), wqkv_ref[...], NT)
    for w in range(live):
        tall[AREA * w:AREA * (w + 1), :] = wide[PADDED * w:PADDED * w + AREA, :]
    rows = live * AREA
    for lo in range(0, rows, 112):
        hi = min(lo + 112, rows)
        c, r = norm(x_ref[lo:hi, :].astype(F32))
        xhat = c * r
        dx = tall[lo:hi, :] * vec_ref[LN1_GAIN]
        dx = r * (dx - jnp.mean(dx, axis=-1, keepdims=True) - xhat * jnp.mean(dx * xhat, axis=-1, keepdims=True))
        gx_ref[lo:hi, :] = (dx + da_ref[lo:hi, :].astype(F32)).astype(BF16)


def input_gradient(x, da, dp, vec, wqkv, at, count, x_at, live, held):
    windows = dp.shape[0]
    wb = block_windows(windows)
    part = lambda *shape: pl.BlockSpec(shape, lambda i: (i + at,) + (0,) * (len(shape) - 1))
    extra = [] if held is None else [held]
    return pl.pallas_call(
        functools.partial(input_kernel, live),
        grid=(count,),
        in_specs=[pl.BlockSpec((wb * AREA, MODEL), lambda i: (i + x_at, 0)), part(wb * AREA, MODEL), part(wb, PADDED, 3 * MODEL),
                  once(vec), once(wqkv)] + [pl.BlockSpec(memory_space=pl.ANY)] * len(extra),
        out_specs=part(wb * AREA, MODEL),
        out_shape=jax.ShapeDtypeStruct((windows * AREA, MODEL), BF16),
        input_output_aliases={5: 0} if extra else {},
        scratch_shapes=[pltpu.VMEM((wb * PADDED, MODEL), F32), pltpu.VMEM((wb * AREA, MODEL), F32)],
        cost_estimate=cost(6 * count),
        compiler_params=pltpu.CompilerParams(vmem_limit_bytes=VMEM_LIMIT, dimension_semantics=("arbitrary",)),
        name="input_gradient",
    )(x, da, dp, vec, wqkv, *extra)


def constant_tables():
    place = np.arange(PADDED)
    real = place < AREA
    r, c = np.where(real, place // WIN, 0), np.where(real, place % WIN, 0)
    hot = [((WIN - 1 - v)[:, None] == np.arange(16)) & real[:, None] for v in (r, c)]
    keys = np.concatenate(hot + hot, axis=1).astype(np.float32)
    shift = np.stack([(v >> b) & 1 for v in (r, c) for b in (3, 2, 1, 0)]).astype(np.int32)
    return keys, np.concatenate(hot, axis=1).T.astype(np.float32), shift


def key_tables(window_extent):
    keys = constant_tables()[0]
    place = np.arange(PADDED)
    r, c = place // WIN, place % WIN
    valid = (r < window_extent[:, 0:1]) & (c < window_extent[:, 1:2]) & (place < AREA)
    keys = np.concatenate([keys, np.zeros((PADDED, 64), np.float32)], axis=1)
    flag = np.arange(128) == 14
    return jnp.where(flag[None, None, :], jnp.where(valid, 0.0, NEGATIVE)[:, :, None], keys[None]).astype(BF16)


def small_tables(rel_h, rel_w):
    _, oht, shift = constant_tables()
    both = jnp.pad(jnp.stack([rel_h, rel_w]), ((0, 0), (0, 5), (0, 0)))
    hi = both.astype(BF16).astype(F32)
    lo = both - hi
    parity = np.eye(2, dtype=np.float32)
    spread = lambda t: (t[:, None, :, None, :] * parity[None, :, None, :, None]).reshape(128, 128)
    ident = np.concatenate([SCALE * np.eye(128), np.zeros((128, 128))], axis=1).astype(np.float32)
    mix = jnp.concatenate([jnp.concatenate([spread(hi), spread(lo)], axis=1), ident], axis=0).astype(BF16)
    relt = jnp.concatenate([hi.reshape(64, HEAD_DIM), lo.reshape(64, HEAD_DIM)], axis=0).T.astype(BF16)
    return jnp.asarray(oht, BF16), jnp.asarray(shift), mix, relt


def gelu_parts(z):
    u = jnp.abs(z)
    t = 1.0 / (1.0 + 0.23164189 * u)
    e = jnp.exp(-0.5 * z * z)
    poly = t * (0.127414796 + t * (-0.142248368 + t * (0.7107068705 + t * (-0.7265760135 + t * 0.5307027145))))
    q = poly * e
    phi = jnp.where(z >= 0.0, 1.0 - q, q)
    return z * phi, phi + z * e * 0.3989422804


ROWS = 512
CHUNK = 768
SLICES = 4


def mlp_kernel(rows, widths, offset_ref, x1_ref, dy_ref, mask_ref, par_ref, upb_ref, *rest):
    n = len(widths)
    ups, downs = rest[:n], rest[n:2 * n]
    out_ref, da_ref, dw_ref, dbu_ref, vec_ref, h2, dm, h2t, dmt, macc, dacc, accu, accd, zs, das, gs, dzs, stage, sems = rest[2 * n:]
    rb = h2.shape[0]
    ch = 256
    step = pl.program_id(0)

    @pl.when(step == 0)
    def _():
        accu[...] = jnp.zeros_like(accu)
        accd[...] = jnp.zeros_like(accd)
        dbu_ref[...] = jnp.zeros_like(dbu_ref)
        vec_ref[...] = jnp.zeros_like(vec_ref)

    def live(i):
        row = step * rb + i * ch + lax.broadcasted_iota(jnp.int32, (ch, 1), 0)
        return row < rows

    @pl.loop(0, rb // ch)
    def _(i):
        rs = pl.ds(pl.multiple_of(i * ch, ch), ch)
        x1 = jnp.where(live(i), x1_ref[rs, :], 0.0)
        c, r = norm(x1)
        h2[rs, :] = (c * r * par_ref[LN2_GAIN] + par_ref[LN2_BIAS]).astype(BF16)
        d = jnp.where(live(i), dy_ref[rs, :].astype(F32), 0.0)
        dm[rs, :] = d.astype(BF16)
        vec_ref[0:8, :] += fold8(d)

    h2t[...] = h2[...].T
    dmt[...] = dm[...].T

    chunks, at = [], 0
    for up_ref, down_ref, width in zip(ups, downs, widths):
        size = min(CHUNK, width)
        for lo in range(0, width, size):
            chunks.append((up_ref, down_ref, slice(lo, lo + size), slice(at, at + size)))
            at += size
    count, part = len(chunks), rb // SLICES

    def products(u):
        up_ref, down_ref, here, there = chunks[u // SLICES]
        rs = slice(u % SLICES * part, (u % SLICES + 1) * part)
        zs[u % 2] = mm(h2[rs, :], up_ref[:, here])
        das[u % 2] = mm(dm[rs, :], down_ref[:, here])

    def activate(u):
        there = chunks[u // SLICES][3]
        rs = slice(u % SLICES * part, (u % SLICES + 1) * part)
        g, gp = gelu_parts(zs[u % 2] + upb_ref[:, there])
        dz = (das[u % 2] * gp).astype(BF16)
        gs[u // SLICES % 2, rs, :] = g.astype(BF16)
        dzs[u // SLICES % 2, rs, :] = dz
        dbu_ref[:, there] += fold8(dz.astype(F32))

    def consume(j, i):
        up_ref, down_ref, here, there = chunks[j]
        g, dz = gs.at[j % 2], dzs.at[j % 2]
        if i == 0:
            m = mm(g[...], down_ref[:, here], NT)
            macc[...] = m if j == 0 else macc[...] + m
        if i == 1:
            d = mm(dz[...], up_ref[:, here], NT)
            dacc[...] = d if j == 0 else dacc[...] + d
        if i == 2:
            accd[:, there] += mm(dmt[...], g[...])
        if i == 3:
            accu[:, there] += mm(h2t[...], dz[...])

    units = count * SLICES
    per = 4 // SLICES
    products(0)
    for u in range(units + SLICES):
        if u + 1 < units:
            products(u + 1)
        if u >= SLICES:
            for k in range(per):
                consume(u // SLICES - 1, u % SLICES * per + k)
        if u < units:
            activate(u)

    @pl.loop(0, rb // ch)
    def _(i):
        rs = pl.ds(pl.multiple_of(i * ch, ch), ch)
        x1 = jnp.where(live(i), x1_ref[rs, :], 0.0)
        c, r = norm(x1)
        xhat = c * r
        valid = live(i) & (mask_ref[rs, :] > 0.0)
        out_ref[rs, :] = jnp.where(valid, x1 + macc[rs, :] + par_ref[DOWN_BIAS], 0.0).astype(BF16)
        dh = dacc[rs, :]
        vec_ref[8:16, :] += fold8(dh * xhat)
        vec_ref[16:24, :] += fold8(dh)
        dx = dh * par_ref[LN2_GAIN]
        dx = r * (dx - jnp.mean(dx, axis=-1, keepdims=True) - xhat * jnp.mean(dx * xhat, axis=-1, keepdims=True))
        da = (dx + dm[rs, :].astype(F32)).astype(BF16)
        da_ref[rs, :] = da
        vec_ref[24:32, :] += fold8(da.astype(F32))

    @pl.when(step == pl.num_programs(0) - 1)
    def _():
        size = stage.shape[2]
        each = accu.shape[1] // size

        def copy(k):
            to = pl.multiple_of(offset_ref[k], 128)
            return pltpu.make_async_copy(stage.at[k % 2], dw_ref.at[:, pl.ds(to, size)], sems.at[k % 2])
        for k in range(2 * each):
            if k >= 2:
                copy(k - 2).wait()
            src = (accu, accd)[k // each]
            stage[k % 2] = src[:, (k % each) * size:(k % each + 1) * size].astype(BF16)
            copy(k).start()
        copy(2 * each - 2).wait()
        copy(2 * each - 1).wait()


def mlp(x1, dy, mask, par, upb, ups, downs, offsets, live_rows):
    rows, d = x1.shape
    widths = tuple(u.shape[1] for u in ups)
    ff = sum(widths)
    size = 2 * ff // offsets.shape[0]
    rb = ROWS
    full = lambda a: pl.BlockSpec(a.shape, lambda i, _: (0, 0), pipeline_mode=pl.Buffered(1))
    rowspec = lambda w: pl.BlockSpec((rb, w), lambda i, _: (i, 0))
    return pl.pallas_call(
        functools.partial(mlp_kernel, live_rows, widths),
        grid_spec=pltpu.PrefetchScalarGridSpec(
            num_scalar_prefetch=1,
            grid=(pl.cdiv(live_rows, rb),),
            in_specs=[rowspec(d), rowspec(d), rowspec(1)] + [full(a) for a in (par, upb, *ups, *downs)],
            out_specs=[rowspec(d), rowspec(d), pl.BlockSpec(memory_space=pl.ANY),
                       pl.BlockSpec((8, ff), lambda i, _: (0, 0)), pl.BlockSpec((32, d), lambda i, _: (0, 0))],
            scratch_shapes=[pltpu.VMEM((rb, d), BF16), pltpu.VMEM((rb, d), BF16), pltpu.VMEM((d, rb), BF16), pltpu.VMEM((d, rb), BF16),
                            pltpu.VMEM((rb, d), F32), pltpu.VMEM((rb, d), F32), pltpu.VMEM((d, ff), F32), pltpu.VMEM((d, ff), F32),
                            pltpu.VMEM((2, rb // SLICES, CHUNK), F32), pltpu.VMEM((2, rb // SLICES, CHUNK), F32),
                            pltpu.VMEM((2, rb, CHUNK), BF16), pltpu.VMEM((2, rb, CHUNK), BF16), pltpu.VMEM((2, d, size), BF16), pltpu.SemaphoreType.DMA((2,))]),
        out_shape=[jax.ShapeDtypeStruct((rows, d), BF16), jax.ShapeDtypeStruct((rows, d), BF16),
                   jax.ShapeDtypeStruct((d, 2 * ff), BF16), jax.ShapeDtypeStruct((8, ff), F32), jax.ShapeDtypeStruct((32, d), F32)],
        cost_estimate=cost(170),
        compiler_params=pltpu.CompilerParams(vmem_limit_bytes=VMEM_LIMIT, dimension_semantics=("arbitrary",)),
        name="mlp",
    )(offsets, x1, dy, mask, par, upb, *ups, *downs)


GROUP_WIN = 40
SPARE = 2


def bits(n):
    return n.bit_length() - 1


def swap(value, axis, bit, sizes):
    return lax.ppermute(value, axis, [(i, i ^ (1 << bit)) for i in range(sizes[axis])])


def bit_of(axis, bit):
    return (lax.axis_index(axis) >> bit) & 1


def add(a, b):
    return (a.astype(F32) + b.astype(F32)).astype(BF16)


def split_dp(held, at, bit):
    mine = bit_of("dp", bit)
    return tuple(lax.dynamic_index_in_dim(held, m, at, keepdims=False) for m in (mine, 1 - mine))


def split_mlp(held, owners, bit):
    mine = bit_of("mlp", bit) == 1
    sides = []
    for side in range(2):
        runs = [n for n, o in enumerate(owners) if (o >> bit) & 1 == side]
        sides.append(jnp.concatenate([held[n:n + 1] for n in runs], axis=0))
    return jnp.where(mine, sides[1], sides[0]), jnp.where(mine, sides[0], sides[1])


def reduce_steps(keep, send, owners, sizes):
    nb, nm = bits(sizes["dp"]), bits(sizes["mlp"])
    apart = lambda v: v.reshape((v.shape[0],) + (2,) * (nb - 1) + v.shape[2:])
    got = yield [("dp", 0, send)]
    held = apart(add(keep, got[0]))
    orders = ([("mlp", b) for b in reversed(range(nm))] + [("dp", 1)], [("dp", 1)] + [("mlp", b) for b in reversed(range(nm))])
    halves = [held[:, 0], held[:, 1]]
    left = [list(owners), list(owners)]
    dims = [nb - 2, nb - 2]
    plan = list(zip(*orders)) + [(("dp", b), ("dp", b)) for b in range(2, nb - 1)]
    for both in plan:
        kept, sends = [], []
        for n, (axis, bit) in enumerate(both):
            if axis == "mlp":
                keep, send = split_mlp(halves[n], left[n], bit)
                mine = [o for o in left[n] if (o >> bit) & 1 == 0]
                left[n] = [o & ~(1 << bit) for o in mine]
            else:
                keep, send = split_dp(halves[n], dims[n], bit)
                dims[n] -= 1
            kept.append(keep)
            sends.append((axis, bit, send))
        got = yield sends
        halves = [add(k, g) for k, g in zip(kept, got)]
    mine = bit_of("dp", nb - 1) == 1
    got = yield [("dp", nb - 1, jnp.where(mine, halves[0], halves[1]))]
    yield add(jnp.where(mine, halves[1], halves[0]), got[0])


def sum_steps(v, sizes):
    for axis in ("dp", "mlp"):
        for b in range(bits(sizes[axis])):
            got = yield [(axis, b, v)]
            v = v + got[0]
    yield v


def pair_steps(v, width):
    mine = lax.axis_index("mlp") == 1
    low, high = v[:, :width], v[:, width:]
    got = yield [("mlp", 0, jnp.where(mine, low, high))]
    yield add(jnp.where(mine, high, low), got[0])


def run_steps(tasks, delays, work, sizes):
    states = [next(t) if not d else None for t, d in zip(tasks, delays)]
    results = [None] * len(tasks)
    turn = 0
    while any(r is None for r in results):
        turn += 1
        sends = [(n, s) for n, state in enumerate(states) if isinstance(state, list) for s in state]
        values = work(turn, [s[2] for _, s in sends], [swap_by(s[0], s[1], sizes) for _, s in sends])
        for n, task in enumerate(tasks):
            if isinstance(states[n], list):
                states[n] = task.send([v for v, (owner, _) in zip(values, sends) if owner == n])
                if not isinstance(states[n], list):
                    results[n] = states[n]
            elif results[n] is None and turn >= delays[n]:
                states[n] = next(task)
    return results


def swap_by(axis, bit, sizes):
    return lambda v: swap(v, axis, bit, sizes)


def feed_forward_weights(up, up_bias, down, sizes):
    width = up.shape[1]
    if sizes["mlp"] != 2:
        gather = lambda v: lax.all_gather(v, "mlp", axis=v.ndim - 1, tiled=True)
        count = sizes["mlp"]
        return [gather(up)], [gather(down)], gather(up_bias), jnp.arange(count, dtype=jnp.int32) * width, width
    half = width // 2
    core, me = bit_of("dp", 0), lax.axis_index("mlp")
    cut = lambda v: jnp.where(core == 1, v[:, half:], v[:, :half])
    far_up, far_down = swap(cut(up), "mlp", 0, sizes), swap(cut(down), "mlp", 0, sizes)
    far_bias = swap(up_bias, "mlp", 0, sizes)
    bias = jnp.concatenate([up_bias, jnp.roll(far_bias, -core * half)])
    places = jnp.stack([me * width, me * width + half, (1 - me) * width + core * half, (1 - me) * width + (1 - core) * half])
    return (up, far_up), (down, far_down), bias, places.astype(jnp.int32), half


def per_device(
    sizes,
    tokens,
    window_extent,
    ln1_gain,
    ln1_bias,
    qkv_weight,
    query_bias,
    value_bias,
    rel_h,
    rel_w,
    proj_weight,
    proj_bias,
    ln2_gain,
    ln2_bias,
    up_weight,
    up_bias,
    down_weight,
    down_bias,
    grad_out,
):
    owners = sizes["mlp"]
    line = lambda v: v.reshape(1, -1)
    ups, downs, up_bias_here, places, piece = feed_forward_weights(up_weight, up_bias, down_weight, sizes)
    windows = window_extent.shape[0]
    wb = block_windows(windows)
    blocks = windows // wb
    me = lax.axis_index("mlp")
    share = owners == 2 and 2 * windows == GROUP_WIN
    live = wb - SPARE if share else wb
    live_rows = (windows - wb + live) * AREA
    near, far = (windows - wb) * AREA, (windows - SPARE) * AREA
    oht, shift, mix, relt = small_tables(rel_h, rel_w)
    par = jnp.stack([ln1_gain, ln1_bias, query_bias, value_bias, proj_bias, ln2_gain, ln2_bias, down_bias])
    ohm = key_tables(window_extent)
    weights = (par, qkv_weight, mix, shift, proj_weight)
    if share:
        def taken(v, here, there):
            other = lax.ppermute(v[there:], "mlp", [(0, 1)])
            mine = jnp.where(me == 0, v[here:here + other.shape[0]], other)
            return jnp.concatenate([mine, jnp.zeros_like(mine)], axis=0)
        tail_x, tail_go = taken(tokens, near, far), taken(grad_out, near, far)
        tail_extent = taken(window_extent.astype(F32), windows - wb, windows - SPARE).astype(jnp.int32)
        tail_ohm = key_tables(tail_extent)
        held = attention_forward(tokens, grad_out, ohm, *weights, windows, 0, blocks - 1, wb, None)
        held = attention_forward(tail_x, tail_go, tail_ohm, *weights, windows, blocks - 1, 1, live, held)
        ohm = jnp.concatenate([ohm[:windows - wb], tail_ohm], axis=0)
    else:
        tail_x = tokens
        held = attention_forward(tokens, grad_out, ohm, *weights, windows, 0, blocks, wb, None)
    x1, xhat, qkv, qaug, o, lse, row_mask, dy = held
    if owners == 2:
        (ups, downs, x1) = lax.optimization_barrier((ups, downs, x1))
        ups, downs = list(ups) + [swap(ups[1], "dp", 0, sizes)], list(downs) + [swap(downs[1], "dp", 0, sizes)]
    width = up_weight.shape[1]
    ff = width * owners
    by_owner = (places // width) * (2 * width) + places % width
    output, da, dw_mlp, up_sums, mid_sums = mlp(
        x1, dy, row_mask, par, line(up_bias_here), ups, downs, jnp.concatenate([by_owner, by_owner + width]), live_rows)

    def returned(v):
        if not share:
            return v
        tail = v[near:live_rows]
        other = lax.ppermute(tail, "mlp", [(1, 0)])
        tail = jnp.where(me == 0, jnp.concatenate([tail, other], axis=0), 0)
        return lax.dynamic_update_slice(v, tail, (near, 0))
    dw_mlp = lax.psum_scatter(dw_mlp, "dp", scatter_dimension=0, tiled=True)
    if owners != 2:
        dw_mlp = lax.psum_scatter(dw_mlp, "mlp", scatter_dimension=1, tiled=True)
    dp_all, grel, dw_keep, dw_send, dp_sums, gain_sums, bias_sums = attention_backward(
        da, ohm, oht, qkv, qaug, lse, proj_weight, relt, shift, xhat, o, par, qkv_weight, bit_of("dp", 0).reshape(1).astype(jnp.int32), sizes["dp"], live)
    output = returned(output)
    up_sum = jnp.sum(up_sums, axis=0).reshape(-1, piece)
    up_sum = sum(jnp.where(jnp.arange(ff) // piece == places[n] // piece, jnp.tile(up_sum[n], ff // piece), 0.0)
                 for n in range(ff // piece))
    block_owners = [0, 0, 0, 1, 1, 1, 0, 1]
    if owners != 2:
        def regroup(v):
            parts = [jnp.moveaxis(p, 0, 2) for p in (v[:6], v[6:])]
            parts = [p.reshape(p.shape[:2] + (owners, -1)) for p in parts]
            return jnp.moveaxis(jnp.concatenate(parts, axis=3), 2, 0)
        dw_keep, dw_send = regroup(dw_keep), regroup(dw_send)
        block_owners = list(range(owners))
    rel = grel[0, :, :HEAD_DIM] + grel[1, :, HEAD_DIM:]
    mid = jnp.sum(mid_sums.reshape(4, 8, MODEL), axis=1)
    sums = jnp.concatenate([gain_sums[0], bias_sums[0], dp_sums[0], rel.reshape(-1), mid.reshape(-1), up_sum])
    half = (blocks - 1) // 2
    order = [(blocks - 1, 1)] + [(at, n) for at, n in ((0, half), (half, blocks - 1 - half)) if n]
    held = {"gx": None, "da": da, "at": 0}

    def input_part():
        at, count = order[held["at"]]
        last = at == blocks - 1
        held["gx"] = input_gradient(tail_x if last else tokens, held["da"], dp_all, par, qkv_weight, at, count, 0 if share and last else at,
                                    live if last else wb, held["gx"])
        held["at"] += 1

    def give_back():
        if share and "back" not in held:
            held["back"] = lax.ppermute(held["gx"][near:live_rows], "mlp", [(1, 0)])

    def work(turn, values, swaps):
        if held["at"] >= len(order):
            return [f(v) for f, v in zip(swaps, values)]
        values, held["da"] = lax.optimization_barrier((values, held["da"]))
        if turn == 3:
            give_back()
        got = [f(v) for f, v in zip(swaps, values)]
        input_part()
        got, held["gx"] = lax.optimization_barrier((got, held["gx"]))
        return got

    tasks = [reduce_steps(dw_keep, dw_send, block_owners, sizes), sum_steps(sums, sizes)]
    delays = [0, 0]
    if owners == 2:
        tasks.append(pair_steps(dw_mlp, 2 * width))
        delays.append(2)
    results = run_steps(tasks, delays, work, sizes)
    late, sums = results[0].astype(F32), results[1]
    late = jnp.concatenate([late[n] for n in range(late.shape[0])], axis=1)
    if owners == 2:
        dw_mlp = results[2]
    while held["at"] < len(order):
        input_part()
    grad_tokens = held["gx"]
    if share:
        give_back()
        tail = jnp.where(me == 0, jnp.concatenate([grad_tokens[near:live_rows], held["back"]], axis=0), 0)
        grad_tokens = lax.dynamic_update_slice(grad_tokens, tail, (near, 0))
    d = MODEL
    table = 2 * WIN - 1
    n_rel = 64 * HEAD_DIM
    rel = sums[5 * d:5 * d + n_rel].reshape(64, HEAD_DIM)
    mid = sums[5 * d + n_rel:]
    cols = 3 * MODEL // owners
    dw_mlp = dw_mlp.astype(F32)
    return (
        output,
        grad_tokens,
        sums[0:d],
        sums[d:2 * d],
        late[:, :cols],
        sums[2 * d:3 * d],
        sums[4 * d:5 * d],
        rel[0:table],
        rel[32:32 + table],
        late[:, cols:],
        mid[3 * d:4 * d],
        mid[d:2 * d],
        mid[2 * d:3 * d],
        dw_mlp[:, :width],
        mid[4 * d:],
        dw_mlp[:, width:],
        mid[0:d],
    )


def solution(mesh):
    rows = P(("dp", "mlp"), None)
    in_specs = (rows, rows, P(), P(), P(), P(), P(), P(), P(), P(), P(), P(), P(),
                P(None, "mlp"), P("mlp"), P(None, "mlp"), P(), rows)
    block = P("dp", "mlp")
    out_specs = (rows, rows, P(), P(), block, P(), P(), P(), P(), block, P(), P(), P(), block, P(), block, P())
    sizes = {name: mesh.shape[name] for name in ("dp", "mlp")}
    return jax.shard_map(
        functools.partial(per_device, sizes), mesh=mesh, in_specs=in_specs, out_specs=out_specs, check_vma=False)
```

```python
import functools
import jax
import jax.numpy as jnp
import numpy as np
from jax import lax
from jax.experimental import pallas as pl
from jax.experimental.pallas import tpu as pltpu
from jax.sharding import PartitionSpec as P

HEADS = 12
HEAD_DIM = 64
WIN = 14
AREA = WIN * WIN
PADDED = 208
PAIRS = HEADS // 2
MODEL = HEADS * HEAD_DIM
EPSILON = 1e-6
NEGATIVE = -1e30
SCALE = HEAD_DIM ** -0.5
F32 = jnp.float32
BF16 = jnp.bfloat16
NN = (((1,), (0,)), ((), ()))
NT = (((1,), (1,)), ((), ()))
TN = (((0,), (0,)), ((), ()))
LN1_GAIN, LN1_BIAS, QUERY_BIAS, VALUE_BIAS, PROJ_BIAS, LN2_GAIN, LN2_BIAS, DOWN_BIAS = (slice(n, n + 1) for n in range(8))
VMEM_LIMIT = 60 * 1024 * 1024


def mm(a, b, dims=NN):
    return lax.dot_general(a, b, dims, preferred_element_type=F32)


def fold8(v):
    return jnp.sum(v.reshape(v.shape[0] // 8, 8, v.shape[1]), axis=0)


def norm(v):
    mu = jnp.mean(v, axis=-1, keepdims=True)
    c = v - mu
    return c, lax.rsqrt(jnp.mean(c * c, axis=-1, keepdims=True) + EPSILON)


def eye(n, value=1.0):
    r = lax.broadcasted_iota(jnp.int32, (n, n), 0)
    c = lax.broadcasted_iota(jnp.int32, (n, n), 1)
    return jnp.where(r == c, value, 0.0).astype(BF16)


def skew_bits(which):
    lane = lax.broadcasted_iota(jnp.int32, (1, PADDED), 1)
    r = lane // WIN
    return WIN - 1 - (jnp.minimum(r, WIN - 1) if which == 0 else lane - r * WIN)


def split(v):
    hi = v.astype(BF16)
    return hi, (v - hi.astype(F32)).astype(BF16)


def key_side(k, ohm):
    return jnp.concatenate([k, ohm], axis=1)


def query_side(qa, h):
    z = jnp.zeros((HEAD_DIM, PADDED), BF16)
    own = qa[h * 64:(h + 1) * 64]
    bias = qa[128 + 64 * h:192 + 64 * h]
    return jnp.concatenate(([own, z] if h == 0 else [z, own]) + [bias, z], axis=0)


def forward_kernel(live, x_ref, go_ref, ohm_ref, vec_ref, wqkv_ref, mix_ref, shift_ref, wproj_ref, *rest):
    x1_ref, xhat_ref, qkv_ref, qaug_ref, o_ref, lse_ref, mask_ref, dm_ref, h1_ref, wide = rest[-10:]
    rows = live * PADDED
    for w in range(live):
        here = slice(AREA * w, AREA * (w + 1))
        c, r = norm(x_ref[here, :].astype(F32))
        xhat = c * r
        valid = jnp.where(ohm_ref[w, 0:AREA, 14:15] < 0.0, 0.0, 1.0)
        h1_ref[w, PADDED - 16:, :] = jnp.zeros((16, MODEL), BF16)
        xhat_ref[w, PADDED - 16:, :] = jnp.zeros((16, MODEL), BF16)
        h1_ref[w, 0:AREA, :] = (xhat * vec_ref[LN1_GAIN] + vec_ref[LN1_BIAS]).astype(BF16)
        xhat_ref[w, 0:AREA, :] = xhat.astype(BF16)
        mask_ref[here, :] = valid
        dm_ref[here, :] = (go_ref[here, :].astype(F32) * valid).astype(BF16)
    for w in range(live, xhat_ref.shape[0]):
        xhat_ref[w] = jnp.zeros((PADDED, MODEL), BF16)
        o_ref[w] = jnp.zeros((PADDED, MODEL), BF16)

    for j, offset in enumerate((QUERY_BIAS, None, VALUE_BIAS)):
        cs = slice(j * MODEL, (j + 1) * MODEL)
        p = mm(h1_ref[0:live].reshape(rows, MODEL), wqkv_ref[:, cs])
        p = p if offset is None else p + vec_ref[offset]
        qkv_ref[0:live, :, cs] = p.astype(BF16).reshape(live, PADDED, MODEL)

    together = 1 if live % 2 else 2

    @pl.loop(0, live // together)
    def _(it):
        heads = [(it * together + n, p) for n in range(together) for p in range(PAIRS)]
        lanes = lambda part, p: slice(part * MODEL + p * 128, part * MODEL + (p + 1) * 128)
        qs = [qkv_ref[w, :, lanes(0, p)] for w, p in heads]
        us = [mm(mix_ref[...], jnp.concatenate([q, q], axis=1), NT) for q in qs]
        qts = [(q.T * SCALE).astype(BF16) for q in qs]
        vts = [qkv_ref[w, :, lanes(2, p)].T for w, p in heads]
        row = lax.broadcasted_iota(jnp.int32, (16, 1), 0)
        qas = []
        for (w, p), u, qt in zip(heads, us, qts):
            tabs = []
            for t in range(2):
                a = u[64 * t:64 * t + 64]
                for n, b in enumerate((8, 4, 2, 1)):
                    cond = shift_ref[4 * t + n:4 * t + n + 1, :] > 0
                    a = jnp.where(cond, pltpu.roll(a, 64 - b, 0), a)
                tabs.append(a)
            parts = [qt]
            for h in range(2):
                ah = jnp.where(row == 14, 1.0, tabs[0][32 * h:32 * h + 16])
                aw = tabs[1][32 * h:32 * h + 16]
                hh, hl = split(ah)
                wh, wl = split(aw)
                parts += [hh, wh, hl, wl]
            qa = jnp.concatenate(parts, axis=0)
            qaug_ref[w, p] = qa
            qas.append(qa)
        keys = [key_side(qkv_ref[w, :, lanes(1, p)], ohm_ref[w]) for w, p in heads]
        scores = [mm(key, query_side(qa, h)) for key, qa in zip(keys, qas) for h in range(2)]
        ots = []
        for n, s in enumerate(scores):
            (w, p), h = heads[n // 2], n % 2
            top = jnp.max(s, axis=0, keepdims=True)
            e = jnp.exp(s - top)
            total = jnp.sum(e, axis=0, keepdims=True)
            lse_ref[w, p, h:h + 1, :] = top + jnp.log(total)
            ots.append(mm(vts[n // 2][64 * h:64 * h + 64], e.astype(BF16)) * (1.0 / total))
        for n, (w, p) in enumerate(heads):
            ot = jnp.concatenate(ots[2 * n:2 * n + 2], axis=0).astype(BF16)
            o_ref[w, :, lanes(0, p)] = ot.T

    wide[0:rows, :] = mm(o_ref[0:live].reshape(rows, MODEL), wproj_ref[...]) + vec_ref[PROJ_BIAS]
    for w in range(live):
        here = slice(AREA * w, AREA * (w + 1))
        x1_ref[here, :] = x_ref[here, :].astype(F32) + wide[PADDED * w:PADDED * w + AREA, :]


def cost(us):
    return pl.CostEstimate(flops=int(us * 1.0e9), bytes_accessed=1 << 20, transcendentals=0)


def once(a):
    return pl.BlockSpec(a.shape, lambda i: (0,) * a.ndim, pipeline_mode=pl.Buffered(1))


def blocked(*shape):
    return pl.BlockSpec(shape, lambda i: (i,) + (0,) * (len(shape) - 1))


def block_windows(windows):
    return 4 if windows % 4 == 0 else windows


def attention_forward(x, go, ohm, vec, wqkv, mix, shift, wproj, windows, at, count, live, held):
    wb = block_windows(windows)
    outs = [((windows * AREA, MODEL), F32, (wb * AREA, MODEL)),
            ((windows, PADDED, MODEL), BF16, (wb, PADDED, MODEL)),
            ((windows, PADDED, 3 * MODEL), BF16, (wb, PADDED, 3 * MODEL)),
            ((windows, PAIRS, 256, PADDED), BF16, (wb, PAIRS, 256, PADDED)),
            ((windows, PADDED, MODEL), BF16, (wb, PADDED, MODEL)),
            ((windows, PAIRS, 2, PADDED), F32, (wb, PAIRS, 2, PADDED)),
            ((windows * AREA, 1), F32, (wb * AREA, 1)),
            ((windows * AREA, MODEL), BF16, (wb * AREA, MODEL))]
    part = lambda *shape: pl.BlockSpec(shape, lambda i: (i + at,) + (0,) * (len(shape) - 1))
    extra = list(held or [])
    return pl.pallas_call(
        functools.partial(forward_kernel, live),
        grid=(count,),
        in_specs=[blocked(live * AREA, MODEL), blocked(live * AREA, MODEL), blocked(live, PADDED, 128)]
        + [once(a) for a in (vec, wqkv, mix, shift, wproj)] + [pl.BlockSpec(memory_space=pl.ANY)] * len(extra),
        out_specs=[part(*b) for _, _, b in outs],
        out_shape=[jax.ShapeDtypeStruct(s, t) for s, t, _ in outs],
        input_output_aliases={8 + n: n for n in range(len(extra))},
        scratch_shapes=[pltpu.VMEM((wb, PADDED, MODEL), BF16), pltpu.VMEM((wb * PADDED, MODEL), F32)],
        cost_estimate=cost(14 * count * live // wb),
        compiler_params=pltpu.CompilerParams(vmem_limit_bytes=VMEM_LIMIT, dimension_semantics=("arbitrary",)),
        name="attention_forward",
    )(x, go, ohm, vec, wqkv, mix, shift, wproj, *extra)


BLOCK = 384
BLOCKS = 4 * MODEL // BLOCK


def backward_kernel(live, core_ref, da_ref, ohm_ref, oht_ref, qkv_ref, qaug_ref, lse_ref, wproj_ref, relt_ref, shift_ref, xhat_ref, o_ref, vec_ref,
                    wqkv_ref, dp_ref, grel_ref, keep_ref, send_ref, sum_ref, gvec_ref, bvec_ref,
                    do_ref, dap_ref, turned, acc, wstage, dstage, wsems, dsems):
    wb = ohm_ref.shape[0]
    rows = wb * PADDED
    step = pl.program_id(0)

    @pl.when(step == 0)
    def _():
        grel_ref[...] = jnp.zeros_like(grel_ref)
        acc[...] = jnp.zeros_like(acc)
        turned[MODEL:, :] = jnp.ones((16, rows), BF16)

    for w in range(wb):
        dap_ref[w, PADDED - 16:, :] = jnp.zeros((16, MODEL), BF16)
        dap_ref[w, 0:AREA, :] = da_ref[AREA * w:AREA * (w + 1), :]
    final = step == pl.num_programs(0) - 1
    if live < wb:
        @pl.when(final)
        def _():
            dap_ref[live:] = jnp.zeros((wb - live, PADDED, MODEL), BF16)
            dp_ref[live:] = jnp.zeros((wb - live, PADDED, 3 * MODEL), BF16)

    def outer(count):
        n = count * PADDED
        dap = dap_ref[0:count].reshape(n, MODEL)
        do_ref[0:count] = mm(dap, wproj_ref[...], NT).astype(BF16).reshape(count, PADDED, MODEL)
        turned[0:MODEL, 0:n] = o_ref[0:count].reshape(n, MODEL).T
        acc[0:MODEL, 3 * MODEL:] += mm(turned[0:MODEL, 0:n], dap)

    def inner(count):
        n = count * PADDED
        turned[0:MODEL, 0:n] = xhat_ref[0:count].reshape(n, MODEL).T
        for j in range(3):
            cs = slice(j * MODEL, (j + 1) * MODEL)
            acc[:, cs] += mm(turned[:, 0:n], dp_ref[0:count, :, cs].reshape(n, MODEL))

    def either(run):
        if live == wb:
            run(wb)
        else:
            pl.when(final)(lambda: run(live))
            pl.when(jnp.logical_not(final))(lambda: run(wb))

    either(outer)
    together = 1 if live % 2 or wb % 2 else 2

    @pl.loop(0, jnp.where(final, live, wb) // together)
    def _(it):
        heads = [(it * together + n, p) for n in range(together) for p in range(PAIRS)]
        lanes = lambda part, p: slice(part * MODEL + p * 128, part * MODEL + (p + 1) * 128)
        both = [(n, w, p, h) for n, (w, p) in enumerate(heads) for h in range(2)]
        qs = [qkv_ref[w, :, lanes(0, p)] for w, p in heads]
        ks = [qkv_ref[w, :, lanes(1, p)] for w, p in heads]
        vs = [qkv_ref[w, :, lanes(2, p)] for w, p in heads]
        dos = [do_ref[w, :, lanes(0, p)] for w, p in heads]
        scores = [mm(key_side(ks[n], ohm_ref[w]), query_side(qaug_ref[w, p], h)) for n, w, p, h in both]
        dots = [do.T for do in dos]
        kts = [(k.T * SCALE).astype(BF16) for k in ks]
        z = jnp.zeros((HEAD_DIM, PADDED), BF16)
        dws = []
        for n, w, p, h in both:
            own = dots[n][64 * h:64 * h + 64]
            dws.append(mm(vs[n], jnp.concatenate([own, z] if h == 0 else [z, own], axis=0)))
        dvs, dks, dqs = [], [], []
        for s, dw, (n, w, p, h) in zip(scores, dws, both):
            a = jnp.exp(s - lse_ref[w, p, h:h + 1, :])
            t = a * dw
            dsb = (t - a * jnp.sum(t, axis=0, keepdims=True)).astype(BF16)
            dvs.append(mm(dots[n][64 * h:64 * h + 64], a.astype(BF16), NT))
            dks.append(mm(qaug_ref[w, p, 64 * h:64 * h + 64, :], dsb, NT))
            dqs.append(mm(jnp.concatenate([kts[n][64 * h:64 * h + 64], oht_ref[...]], axis=0), dsb))
        zz = jnp.zeros((16, PADDED), F32)
        dqts = []
        for n, (w, p) in enumerate(heads):
            tabs = []
            for t in range(2):
                lo = 64 + 16 * t
                a = jnp.concatenate([dqs[2 * n][lo:lo + 16], zz, dqs[2 * n + 1][lo:lo + 16], zz], axis=0)
                for i, b in enumerate((8, 4, 2, 1)):
                    cond = shift_ref[4 * t + i:4 * t + i + 1, :] > 0
                    a = jnp.where(cond, pltpu.roll(a, b, 0), a)
                tabs.append(a.astype(BF16))
            dqt = []
            for h in range(2):
                du = jnp.concatenate([tabs[0][32 * h:32 * h + 32], tabs[1][32 * h:32 * h + 32]], axis=0)
                dqt.append(dqs[2 * n + h][0:64] + mm(relt_ref[...], jnp.concatenate([du, du], axis=0)))
                grel_ref[h] += mm(du, qs[n])
            dqts.append(jnp.concatenate(dqt, axis=0).astype(BF16))
        for n, (w, p) in enumerate(heads):
            dp_ref[w, :, lanes(0, p)] = dqts[n].T
            dp_ref[w, :, lanes(1, p)] = jnp.concatenate(dks[2 * n:2 * n + 2], axis=0).astype(BF16).T
            dp_ref[w, :, lanes(2, p)] = jnp.concatenate(dvs[2 * n:2 * n + 2], axis=0).astype(BF16).T

    either(inner)

    @pl.when(final)
    def _():
        columns = jnp.concatenate([vec_ref[...]] * 16, axis=0).T
        gain, bias = columns[:, 0:1], columns[:, 1:2]
        nq = 3 * MODEL // BLOCK
        sum_ref[...] = acc[MODEL:MODEL + 8, 0:3 * MODEL]
        gsum, bsum = jnp.zeros((MODEL, 128), F32), jnp.zeros((MODEL, 128), F32)
        take = lambda n: pltpu.make_async_copy(wqkv_ref.at[:, pl.ds(n * BLOCK, BLOCK)], wstage.at[n % 2], wsems.at[n % 2])
        core = core_ref[0]

        def give(n, act):
            for k, to, c in ((0, keep_ref, core), (1, send_ref, 1 - core)):
                act(pltpu.make_async_copy(dstage.at[n % 2, :, c], to.at[n], dsems.at[n % 2, k]))
        start, wait = (lambda cp: cp.start()), (lambda cp: cp.wait())
        take(0).start()
        for n in range(BLOCKS):
            cs = slice(n * BLOCK, (n + 1) * BLOCK)
            if n + 1 < nq:
                take(n + 1).start()
            if n >= 2:
                give(n - 2, wait)
            m = acc[0:MODEL, cs]
            if n < nq:
                s = acc[MODEL:MODEL + 1, cs]
                take(n).wait()
                w = wstage[n % 2].astype(F32)
                g, b = w * m, w * s
                gsum += sum(g[:, 128 * i:128 * (i + 1)] for i in range(BLOCK // 128))
                bsum += sum(b[:, 128 * i:128 * (i + 1)] for i in range(BLOCK // 128))
                m = m * gain + bias * s
            dstage[n % 2] = m.astype(BF16).reshape(dstage.shape[1:])
            give(n, start)
        gvec_ref[...] = jnp.broadcast_to(jnp.sum(gsum.T, axis=0, keepdims=True), gvec_ref.shape)
        bvec_ref[...] = jnp.broadcast_to(jnp.sum(bsum.T, axis=0, keepdims=True), bvec_ref.shape)
        give(BLOCKS - 2, wait)
        give(BLOCKS - 1, wait)


def attention_backward(da, ohm, oht, qkv, qaug, lse, wproj, relt, shift, xhat, o, vec, wqkv, core, dp_size, live):
    windows = ohm.shape[0]
    wb = block_windows(windows)
    block = lambda *shape: pl.BlockSpec(shape, lambda i, _: (i,) + (0,) * (len(shape) - 1))
    whole = lambda a: pl.BlockSpec(a.shape, lambda i, _: (0,) * a.ndim, pipeline_mode=pl.Buffered(1))
    row = MODEL // dp_size
    fixed = lambda *shape: pl.BlockSpec(shape, lambda i, _: (0,) * len(shape))
    anywhere = pl.BlockSpec(memory_space=pl.ANY)
    return pl.pallas_call(
        functools.partial(backward_kernel, live),
        grid_spec=pltpu.PrefetchScalarGridSpec(
            num_scalar_prefetch=1,
            grid=(windows // wb,),
            in_specs=[block(wb * AREA, MODEL), block(wb, PADDED, 128), whole(oht), block(wb, PADDED, 3 * MODEL),
                  block(wb, PAIRS, 256, PADDED), block(wb, PAIRS, 2, PADDED), whole(wproj), whole(relt), whole(shift),
                  block(wb, PADDED, MODEL), block(wb, PADDED, MODEL), whole(vec), anywhere],
        out_specs=[block(wb, PADDED, 3 * MODEL), fixed(2, 64, 128), anywhere, anywhere, fixed(8, 3 * MODEL), fixed(8, MODEL), fixed(8, MODEL)],
        scratch_shapes=[pltpu.VMEM((wb, PADDED, MODEL), BF16), pltpu.VMEM((wb, PADDED, MODEL), BF16),
                        pltpu.VMEM((MODEL + 16, wb * PADDED), BF16), pltpu.VMEM((MODEL + 16, 4 * MODEL), F32),
                        pltpu.VMEM((2, MODEL, BLOCK), BF16), pltpu.VMEM((2, dp_size // 2, 2, row, BLOCK), BF16),
                        pltpu.SemaphoreType.DMA((2,)), pltpu.SemaphoreType.DMA((2, 2))]),
        out_shape=[jax.ShapeDtypeStruct((windows, PADDED, 3 * MODEL), BF16), jax.ShapeDtypeStruct((2, 64, 128), F32),
                   jax.ShapeDtypeStruct((BLOCKS, dp_size // 2, row, BLOCK), BF16),
                   jax.ShapeDtypeStruct((BLOCKS, dp_size // 2, row, BLOCK), BF16), jax.ShapeDtypeStruct((8, 3 * MODEL), F32),
                   jax.ShapeDtypeStruct((8, MODEL), F32), jax.ShapeDtypeStruct((8, MODEL), F32)],
        cost_estimate=cost(95),
        compiler_params=pltpu.CompilerParams(vmem_limit_bytes=VMEM_LIMIT, dimension_semantics=("arbitrary",)),
        name="attention_backward",
    )(core, da, ohm, oht, qkv, qaug, lse, wproj, relt, shift, xhat, o, vec, wqkv)


def input_kernel(live, x_ref, da_ref, dp_ref, vec_ref, wqkv_ref, *rest):
    gx_ref, wide, tall = rest[-3:]
    wide[0:live * PADDED, :] = mm(dp_ref[0:live].reshape(live * PADDED, 3 * MODEL), wqkv_ref[...], NT)
    for w in range(live):
        tall[AREA * w:AREA * (w + 1), :] = wide[PADDED * w:PADDED * w + AREA, :]
    rows = live * AREA
    for lo in range(0, rows, 112):
        hi = min(lo + 112, rows)
        c, r = norm(x_ref[lo:hi, :].astype(F32))
        xhat = c * r
        dx = tall[lo:hi, :] * vec_ref[LN1_GAIN]
        dx = r * (dx - jnp.mean(dx, axis=-1, keepdims=True) - xhat * jnp.mean(dx * xhat, axis=-1, keepdims=True))
        gx_ref[lo:hi, :] = (dx + da_ref[lo:hi, :].astype(F32)).astype(BF16)


def input_gradient(x, da, dp, vec, wqkv, at, count, x_at, live, held):
    windows = dp.shape[0]
    wb = block_windows(windows)
    part = lambda *shape: pl.BlockSpec(shape, lambda i: (i + at,) + (0,) * (len(shape) - 1))
    extra = [] if held is None else [held]
    return pl.pallas_call(
        functools.partial(input_kernel, live),
        grid=(count,),
        in_specs=[pl.BlockSpec((live * AREA, MODEL), lambda i: (i + x_at, 0)), part(wb * AREA, MODEL), part(wb, PADDED, 3 * MODEL),
                  once(vec), once(wqkv)] + [pl.BlockSpec(memory_space=pl.ANY)] * len(extra),
        out_specs=part(wb * AREA, MODEL),
        out_shape=jax.ShapeDtypeStruct((windows * AREA, MODEL), BF16),
        input_output_aliases={5: 0} if extra else {},
        scratch_shapes=[pltpu.VMEM((wb * PADDED, MODEL), F32), pltpu.VMEM((wb * AREA, MODEL), F32)],
        cost_estimate=cost(6 * count),
        compiler_params=pltpu.CompilerParams(vmem_limit_bytes=VMEM_LIMIT, dimension_semantics=("arbitrary",)),
        name="input_gradient",
    )(x, da, dp, vec, wqkv, *extra)


def constant_tables():
    place = np.arange(PADDED)
    real = place < AREA
    r, c = np.where(real, place // WIN, 0), np.where(real, place % WIN, 0)
    hot = [((WIN - 1 - v)[:, None] == np.arange(16)) & real[:, None] for v in (r, c)]
    keys = np.concatenate(hot + hot, axis=1).astype(np.float32)
    shift = np.stack([(v >> b) & 1 for v in (r, c) for b in (3, 2, 1, 0)]).astype(np.int32)
    return keys, np.concatenate(hot, axis=1).T.astype(np.float32), shift


def key_tables(window_extent):
    keys = constant_tables()[0]
    place = np.arange(PADDED)
    r, c = place // WIN, place % WIN
    valid = (r < window_extent[:, 0:1]) & (c < window_extent[:, 1:2]) & (place < AREA)
    keys = np.concatenate([keys, np.zeros((PADDED, 64), np.float32)], axis=1)
    flag = np.arange(128) == 14
    return jnp.where(flag[None, None, :], jnp.where(valid, 0.0, NEGATIVE)[:, :, None], keys[None]).astype(BF16)


def small_tables(rel_h, rel_w):
    _, oht, shift = constant_tables()
    both = jnp.pad(jnp.stack([rel_h, rel_w]), ((0, 0), (0, 5), (0, 0)))
    hi = both.astype(BF16).astype(F32)
    lo = both - hi
    parity = np.eye(2, dtype=np.float32)
    spread = lambda t: (t[:, None, :, None, :] * parity[None, :, None, :, None]).reshape(128, 128)
    mix = jnp.concatenate([spread(hi), spread(lo)], axis=1).astype(BF16)
    relt = jnp.concatenate([hi.reshape(64, HEAD_DIM), lo.reshape(64, HEAD_DIM)], axis=0).T.astype(BF16)
    return jnp.asarray(oht, BF16), jnp.asarray(shift), mix, relt


def gelu_parts(z):
    u = jnp.abs(z)
    t = 1.0 / (1.0 + 0.23164189 * u)
    e = jnp.exp2(z * (z * -0.72134752))
    poly = t * (0.127414796 + t * (-0.142248368 + t * (0.7107068705 + t * (-0.7265760135 + t * 0.5307027145))))
    q = poly * e
    phi = jnp.where(z >= 0.0, 1.0 - q, q)
    return z * phi, phi + z * e * 0.3989422804


ROWS = 512
CHUNK = 768
SLICES = 4


def mlp_kernel(rows, widths, offset_ref, x1_ref, dy_ref, mask_ref, par_ref, upb_ref, *rest):
    n = len(widths)
    ups, downs = rest[:n], rest[n:2 * n]
    out_ref, da_ref, dw_ref, dbu_ref, vec_ref, h2, dm, h2t, dmt, macc, dacc, accu, accd, zs, das, gs, dzs, stage, sems = rest[2 * n:]
    rb = h2.shape[0]
    ch = 512
    step = pl.program_id(0)

    @pl.when(step == 0)
    def _():
        accu[...] = jnp.zeros_like(accu)
        accd[...] = jnp.zeros_like(accd)
        h2t[MODEL:, :] = jnp.ones((16, h2t.shape[1]), BF16)
        vec_ref[...] = jnp.zeros_like(vec_ref)

    def live(i):
        row = step * rb + i * ch + lax.broadcasted_iota(jnp.int32, (ch, 1), 0)
        return row < rows

    @pl.loop(0, rb // ch)
    def _(i):
        rs = pl.ds(pl.multiple_of(i * ch, ch), ch)
        x1 = jnp.where(live(i), x1_ref[rs, :], 0.0)
        c, r = norm(x1)
        h2[rs, :] = (c * r * par_ref[LN2_GAIN] + par_ref[LN2_BIAS]).astype(BF16)
        d = jnp.where(live(i), dy_ref[rs, :].astype(F32), 0.0)
        dm[rs, :] = d.astype(BF16)
        vec_ref[0:8, :] += fold8(d)

    h2t[0:MODEL, :] = h2[...].T
    dmt[...] = dm[...].T

    chunks, at = [], 0
    for up_ref, down_ref, width in zip(ups, downs, widths):
        size = min(CHUNK, width)
        for lo in range(0, width, size):
            chunks.append((up_ref, down_ref, slice(lo, lo + size), slice(at, at + size)))
            at += size
    count, part = len(chunks), rb // SLICES

    def products(u):
        up_ref, down_ref, here, there = chunks[u // SLICES]
        rs = slice(u % SLICES * part, (u % SLICES + 1) * part)
        zs[u % 2] = mm(h2[rs, :], up_ref[:, here])
        das[u % 2] = mm(dm[rs, :], down_ref[:, here])

    def activate(u):
        there = chunks[u // SLICES][3]
        rs = slice(u % SLICES * part, (u % SLICES + 1) * part)
        g, gp = gelu_parts(zs[u % 2] + upb_ref[:, there])
        dz = (das[u % 2] * gp).astype(BF16)
        gs[u // SLICES % 2, rs, :] = g.astype(BF16)
        dzs[u // SLICES % 2, rs, :] = dz

    def consume(j, i):
        up_ref, down_ref, here, there = chunks[j]
        g, dz = gs.at[j % 2], dzs.at[j % 2]
        if i == 0:
            m = mm(g[...], down_ref[:, here], NT)
            macc[...] = m if j == 0 else macc[...] + m
        if i == 1:
            d = mm(dz[...], up_ref[:, here], NT)
            dacc[...] = d if j == 0 else dacc[...] + d
        if i == 2:
            accd[:, there] += mm(dmt[...], g[...])
        if i == 3:
            accu[:, there] += mm(h2t[...], dz[...])

    units = count * SLICES
    per = 4 // SLICES
    products(0)
    for u in range(units + SLICES):
        if u + 1 < units:
            products(u + 1)
        if u >= SLICES:
            for k in range(per):
                consume(u // SLICES - 1, u % SLICES * per + k)
        if u < units:
            activate(u)

    @pl.loop(0, rb // ch)
    def _(i):
        rs = pl.ds(pl.multiple_of(i * ch, ch), ch)
        x1 = jnp.where(live(i), x1_ref[rs, :], 0.0)
        c, r = norm(x1)
        xhat = c * r
        valid = live(i) & (mask_ref[rs, :] > 0.0)
        out_ref[rs, :] = jnp.where(valid, x1 + macc[rs, :] + par_ref[DOWN_BIAS], 0.0).astype(BF16)
        dh = dacc[rs, :]
        vec_ref[8:16, :] += fold8(dh * xhat)
        vec_ref[16:24, :] += fold8(dh)
        dx = dh * par_ref[LN2_GAIN]
        dx = r * (dx - jnp.mean(dx, axis=-1, keepdims=True) - xhat * jnp.mean(dx * xhat, axis=-1, keepdims=True))
        da = (dx + dm[rs, :].astype(F32)).astype(BF16)
        da_ref[rs, :] = da
        vec_ref[24:32, :] += fold8(da.astype(F32))

    @pl.when(step == pl.num_programs(0) - 1)
    def _():
        size = stage.shape[2]
        dbu_ref[...] = accu[MODEL:MODEL + 8, :]
        each = accu.shape[1] // size

        def copy(k):
            to = pl.multiple_of(offset_ref[k], 128)
            return pltpu.make_async_copy(stage.at[k % 2], dw_ref.at[:, pl.ds(to, size)], sems.at[k % 2])
        for k in range(2 * each):
            if k >= 2:
                copy(k - 2).wait()
            src = (accu, accd)[k // each]
            stage[k % 2] = src[0:MODEL, (k % each) * size:(k % each + 1) * size].astype(BF16)
            copy(k).start()
        copy(2 * each - 2).wait()
        copy(2 * each - 1).wait()


def mlp(x1, dy, mask, par, upb, ups, downs, offsets, live_rows):
    rows, d = x1.shape
    widths = tuple(u.shape[1] for u in ups)
    ff = sum(widths)
    size = 2 * ff // offsets.shape[0]
    rb = ROWS
    full = lambda a: pl.BlockSpec(a.shape, lambda i, _: (0, 0), pipeline_mode=pl.Buffered(1))
    rowspec = lambda w: pl.BlockSpec((rb, w), lambda i, _: (i, 0))
    return pl.pallas_call(
        functools.partial(mlp_kernel, live_rows, widths),
        grid_spec=pltpu.PrefetchScalarGridSpec(
            num_scalar_prefetch=1,
            grid=(pl.cdiv(live_rows, rb),),
            in_specs=[rowspec(d), rowspec(d), rowspec(1)] + [full(a) for a in (par, upb, *ups, *downs)],
            out_specs=[rowspec(d), rowspec(d), pl.BlockSpec(memory_space=pl.ANY),
                       pl.BlockSpec((8, ff), lambda i, _: (0, 0)), pl.BlockSpec((32, d), lambda i, _: (0, 0))],
            scratch_shapes=[pltpu.VMEM((rb, d), BF16), pltpu.VMEM((rb, d), BF16), pltpu.VMEM((d + 16, rb), BF16), pltpu.VMEM((d, rb), BF16),
                            pltpu.VMEM((rb, d), F32), pltpu.VMEM((rb, d), F32), pltpu.VMEM((d + 16, ff), F32), pltpu.VMEM((d, ff), F32),
                            pltpu.VMEM((2, rb // SLICES, CHUNK), F32), pltpu.VMEM((2, rb // SLICES, CHUNK), F32),
                            pltpu.VMEM((2, rb, CHUNK), BF16), pltpu.VMEM((2, rb, CHUNK), BF16), pltpu.VMEM((2, d, size), BF16), pltpu.SemaphoreType.DMA((2,))]),
        out_shape=[jax.ShapeDtypeStruct((rows, d), BF16), jax.ShapeDtypeStruct((rows, d), BF16),
                   jax.ShapeDtypeStruct((d, 2 * ff), BF16), jax.ShapeDtypeStruct((8, ff), F32), jax.ShapeDtypeStruct((32, d), F32)],
        cost_estimate=cost(170),
        compiler_params=pltpu.CompilerParams(vmem_limit_bytes=VMEM_LIMIT, dimension_semantics=("arbitrary",)),
        name="mlp",
    )(offsets, x1, dy, mask, par, upb, *ups, *downs)


GROUP_WIN = 40
SPARE = 2


def bits(n):
    return n.bit_length() - 1


def swap(value, axis, bit, sizes):
    return lax.ppermute(value, axis, [(i, i ^ (1 << bit)) for i in range(sizes[axis])])


def bit_of(axis, bit):
    return (lax.axis_index(axis) >> bit) & 1


def add(a, b):
    return (a.astype(F32) + b.astype(F32)).astype(BF16)


def split_dp(held, at, bit):
    mine = bit_of("dp", bit)
    return tuple(lax.dynamic_index_in_dim(held, m, at, keepdims=False) for m in (mine, 1 - mine))


def split_mlp(held, owners, bit):
    mine = bit_of("mlp", bit) == 1
    sides = []
    for side in range(2):
        runs = [n for n, o in enumerate(owners) if (o >> bit) & 1 == side]
        sides.append(jnp.concatenate([held[n:n + 1] for n in runs], axis=0))
    return jnp.where(mine, sides[1], sides[0]), jnp.where(mine, sides[0], sides[1])


def reduce_steps(keep, send, owners, sizes):
    nb, nm = bits(sizes["dp"]), bits(sizes["mlp"])
    apart = lambda v: v.reshape((v.shape[0],) + (2,) * (nb - 1) + v.shape[2:])
    got = yield [("dp", 0, send)]
    held = apart(add(keep, got[0]))
    orders = ([("mlp", b) for b in reversed(range(nm))] + [("dp", 1)], [("dp", 1)] + [("mlp", b) for b in reversed(range(nm))])
    halves = [held[:, 0], held[:, 1]]
    left = [list(owners), list(owners)]
    dims = [nb - 2, nb - 2]
    plan = list(zip(*orders)) + [(("dp", b), ("dp", b)) for b in range(2, nb - 1)]
    for both in plan:
        kept, sends = [], []
        for n, (axis, bit) in enumerate(both):
            if axis == "mlp":
                keep, send = split_mlp(halves[n], left[n], bit)
                mine = [o for o in left[n] if (o >> bit) & 1 == 0]
                left[n] = [o & ~(1 << bit) for o in mine]
            else:
                keep, send = split_dp(halves[n], dims[n], bit)
                dims[n] -= 1
            kept.append(keep)
            sends.append((axis, bit, send))
        got = yield sends
        halves = [add(k, g) for k, g in zip(kept, got)]
    mine = bit_of("dp", nb - 1) == 1
    got = yield [("dp", nb - 1, jnp.where(mine, halves[0], halves[1]))]
    yield add(jnp.where(mine, halves[1], halves[0]), got[0])


def sum_steps(v, sizes):
    for axis in ("dp", "mlp"):
        for b in range(bits(sizes[axis])):
            got = yield [(axis, b, v)]
            v = v + got[0]
    yield v


def pair_steps(v, width):
    mine = lax.axis_index("mlp") == 1
    low, high = v[:, :width], v[:, width:]
    got = yield [("mlp", 0, jnp.where(mine, low, high))]
    yield add(jnp.where(mine, high, low), got[0])


def run_steps(tasks, delays, work, sizes):
    states = [next(t) if not d else None for t, d in zip(tasks, delays)]
    results = [None] * len(tasks)
    turn = 0
    while any(r is None for r in results):
        turn += 1
        sends = [(n, s) for n, state in enumerate(states) if isinstance(state, list) for s in state]
        values = work(turn, [s[2] for _, s in sends], [swap_by(s[0], s[1], sizes) for _, s in sends])
        for n, task in enumerate(tasks):
            if isinstance(states[n], list):
                states[n] = task.send([v for v, (owner, _) in zip(values, sends) if owner == n])
                if not isinstance(states[n], list):
                    results[n] = states[n]
            elif results[n] is None and turn >= delays[n]:
                states[n] = next(task)
    return results


def swap_by(axis, bit, sizes):
    return lambda v: swap(v, axis, bit, sizes)


def feed_forward_weights(up, up_bias, down, sizes):
    width = up.shape[1]
    if sizes["mlp"] != 2:
        gather = lambda v: lax.all_gather(v, "mlp", axis=v.ndim - 1, tiled=True)
        count = sizes["mlp"]
        return [gather(up)], [gather(down)], gather(up_bias), jnp.arange(count, dtype=jnp.int32) * width, width
    half = width // 2
    core, me = bit_of("dp", 0), lax.axis_index("mlp")
    cut = lambda v: jnp.where(core == 1, v[:, half:], v[:, :half])
    far_up, far_down = swap(cut(up), "mlp", 0, sizes), swap(cut(down), "mlp", 0, sizes)
    far_bias = swap(up_bias, "mlp", 0, sizes)
    bias = jnp.concatenate([up_bias, jnp.roll(far_bias, -core * half)])
    places = jnp.stack([me * width, me * width + half, (1 - me) * width + core * half, (1 - me) * width + (1 - core) * half])
    return (up, far_up), (down, far_down), bias, places.astype(jnp.int32), half


def per_device(
    sizes,
    tokens,
    window_extent,
    ln1_gain,
    ln1_bias,
    qkv_weight,
    query_bias,
    value_bias,
    rel_h,
    rel_w,
    proj_weight,
    proj_bias,
    ln2_gain,
    ln2_bias,
    up_weight,
    up_bias,
    down_weight,
    down_bias,
    grad_out,
):
    owners = sizes["mlp"]
    line = lambda v: v.reshape(1, -1)
    ups, downs, up_bias_here, places, piece = feed_forward_weights(up_weight, up_bias, down_weight, sizes)
    windows = window_extent.shape[0]
    wb = block_windows(windows)
    blocks = windows // wb
    me = lax.axis_index("mlp")
    share = owners == 2 and 2 * windows == GROUP_WIN
    live = wb - SPARE if share else wb
    live_rows = (windows - wb + live) * AREA
    near, far = (windows - wb) * AREA, (windows - SPARE) * AREA
    oht, shift, mix, relt = small_tables(rel_h, rel_w)
    par = jnp.stack([ln1_gain, ln1_bias, query_bias, value_bias, proj_bias, ln2_gain, ln2_bias, down_bias])
    ohm = key_tables(window_extent)
    weights = (par, qkv_weight, mix, shift, proj_weight)
    if share:
        def taken(v, here, there):
            other = lax.ppermute(v[there:], "mlp", [(0, 1)])
            return jnp.where(me == 0, v[here:here + other.shape[0]], other)
        tail_x, tail_go = taken(tokens, near, far), taken(grad_out, near, far)
        tail_extent = taken(window_extent.astype(F32), windows - wb, windows - SPARE).astype(jnp.int32)
        tail_ohm = key_tables(tail_extent)
        held = attention_forward(tokens, grad_out, ohm, *weights, windows, 0, blocks - 1, wb, None)
        held = attention_forward(tail_x, tail_go, tail_ohm, *weights, windows, blocks - 1, 1, live, held)
        ohm = jnp.concatenate([ohm[:windows - wb], jnp.pad(tail_ohm, ((0, SPARE), (0, 0), (0, 0)))], axis=0)
    else:
        tail_x = tokens
        held = attention_forward(tokens, grad_out, ohm, *weights, windows, 0, blocks, wb, None)
    x1, xhat, qkv, qaug, o, lse, row_mask, dy = held
    if owners == 2:
        (ups, downs, x1) = lax.optimization_barrier((ups, downs, x1))
        ups, downs = list(ups) + [swap(ups[1], "dp", 0, sizes)], list(downs) + [swap(downs[1], "dp", 0, sizes)]
    width = up_weight.shape[1]
    ff = width * owners
    by_owner = (places // width) * (2 * width) + places % width
    output, da, dw_mlp, up_sums, mid_sums = mlp(
        x1, dy, row_mask, par, line(up_bias_here), ups, downs, jnp.concatenate([by_owner, by_owner + width]), live_rows)

    def give_back(v):
        return lax.ppermute(v[near:live_rows], "mlp", [(1, 0)])

    def completed(v, other):
        tail = jnp.where(me == 0, jnp.concatenate([v[near:live_rows], other], axis=0), 0)
        return lax.dynamic_update_slice(v, tail, (near, 0))

    if share:
        output_tail, da = lax.optimization_barrier((output[near:live_rows], da))
        output_back = lax.ppermute(output_tail, "mlp", [(1, 0)])
    dw_mlp = lax.psum_scatter(dw_mlp, "dp", scatter_dimension=0, tiled=True)
    if owners != 2:
        dw_mlp = lax.psum_scatter(dw_mlp, "mlp", scatter_dimension=1, tiled=True)
    dp_all, grel, dw_keep, dw_send, dp_sums, gain_sums, bias_sums = attention_backward(
        da, ohm, oht, qkv, qaug, lse, proj_weight, relt, shift, xhat, o, par, qkv_weight, bit_of("dp", 0).reshape(1).astype(jnp.int32), sizes["dp"], live)
    if share:
        output = completed(output, output_back)
    up_sum = up_sums[0].reshape(-1, piece)
    up_sum = sum(jnp.where(jnp.arange(ff) // piece == places[n] // piece, jnp.tile(up_sum[n], ff // piece), 0.0)
                 for n in range(ff // piece))
    block_owners = [0, 0, 0, 1, 1, 1, 0, 1]
    if owners != 2:
        def regroup(v):
            parts = [jnp.moveaxis(p, 0, 2) for p in (v[:6], v[6:])]
            parts = [p.reshape(p.shape[:2] + (owners, -1)) for p in parts]
            return jnp.moveaxis(jnp.concatenate(parts, axis=3), 2, 0)
        dw_keep, dw_send = regroup(dw_keep), regroup(dw_send)
        block_owners = list(range(owners))
    rel = grel[0, :, :HEAD_DIM] + grel[1, :, HEAD_DIM:]
    mid = jnp.sum(mid_sums.reshape(4, 8, MODEL), axis=1)
    sums = jnp.concatenate([gain_sums[0], bias_sums[0], dp_sums[0], rel.reshape(-1), mid.reshape(-1), up_sum])
    half = (blocks - 1) // 2
    order = [(blocks - 1, 1)] + [(at, n) for at, n in ((0, half), (half, blocks - 1 - half)) if n]
    held = {"gx": None, "da": da, "at": 0}

    def input_part():
        at, count = order[held["at"]]
        last = at == blocks - 1
        held["gx"] = input_gradient(tail_x if last else tokens, held["da"], dp_all, par, qkv_weight, at, count, 0 if share and last else at,
                                    live if last else wb, held["gx"])
        held["at"] += 1

    def work(turn, values, swaps):
        if held["at"] >= len(order):
            return [f(v) for f, v in zip(swaps, values)]
        values, held["da"] = lax.optimization_barrier((values, held["da"]))
        if share and turn == 3:
            held["back"] = give_back(held["gx"])
        got = [f(v) for f, v in zip(swaps, values)]
        input_part()
        got, held["gx"] = lax.optimization_barrier((got, held["gx"]))
        return got

    tasks = [reduce_steps(dw_keep, dw_send, block_owners, sizes), sum_steps(sums, sizes)]
    delays = [0, 0]
    if owners == 2:
        tasks.append(pair_steps(dw_mlp, 2 * width))
        delays.append(2)
    results = run_steps(tasks, delays, work, sizes)
    late, sums = results[0].astype(F32), results[1]
    late = jnp.concatenate([late[n] for n in range(late.shape[0])], axis=1)
    if owners == 2:
        dw_mlp = results[2]
    while held["at"] < len(order):
        input_part()
    grad_tokens = held["gx"]
    if share:
        grad_tokens = completed(grad_tokens, held["back"])
    d = MODEL
    table = 2 * WIN - 1
    n_rel = 64 * HEAD_DIM
    rel = sums[5 * d:5 * d + n_rel].reshape(64, HEAD_DIM)
    mid = sums[5 * d + n_rel:]
    cols = 3 * MODEL // owners
    dw_mlp = dw_mlp.astype(F32)
    return (
        output,
        grad_tokens,
        sums[0:d],
        sums[d:2 * d],
        late[:, :cols],
        sums[2 * d:3 * d],
        sums[4 * d:5 * d],
        rel[0:table],
        rel[32:32 + table],
        late[:, cols:],
        mid[3 * d:4 * d],
        mid[d:2 * d],
        mid[2 * d:3 * d],
        dw_mlp[:, :width],
        mid[4 * d:],
        dw_mlp[:, width:],
        mid[0:d],
    )


def solution(mesh):
    rows = P(("dp", "mlp"), None)
    in_specs = (rows, rows, P(), P(), P(), P(), P(), P(), P(), P(), P(), P(), P(),
                P(None, "mlp"), P("mlp"), P(None, "mlp"), P(), rows)
    block = P("dp", "mlp")
    out_specs = (rows, rows, P(), P(), block, P(), P(), P(), P(), block, P(), P(), P(), block, P(), block, P())
    sizes = {name: mesh.shape[name] for name in ("dp", "mlp")}
    return jax.shard_map(
        functools.partial(per_device, sizes), mesh=mesh, in_specs=in_specs, out_specs=out_specs, check_vma=False)
```

```python
import functools
import jax
import jax.numpy as jnp
import numpy as np
from jax import lax
from jax.experimental import pallas as pl
from jax.experimental.pallas import tpu as pltpu
from jax.sharding import PartitionSpec as P

HEADS = 12
HEAD_DIM = 64
WIN = 14
AREA = WIN * WIN
PADDED = 208
PAIRS = HEADS // 2
MODEL = HEADS * HEAD_DIM
EPSILON = 1e-6
NEGATIVE = -1e30
SCALE = HEAD_DIM ** -0.5
F32 = jnp.float32
BF16 = jnp.bfloat16
NN = (((1,), (0,)), ((), ()))
NT = (((1,), (1,)), ((), ()))
TN = (((0,), (0,)), ((), ()))
LN1_GAIN, LN1_BIAS, QUERY_BIAS, VALUE_BIAS, PROJ_BIAS, LN2_GAIN, LN2_BIAS, DOWN_BIAS = (slice(n, n + 1) for n in range(8))
VMEM_LIMIT = 60 * 1024 * 1024


def mm(a, b, dims=NN):
    return lax.dot_general(a, b, dims, preferred_element_type=F32)


def fold8(v):
    return jnp.sum(v.reshape(v.shape[0] // 8, 8, v.shape[1]), axis=0)


def norm(v):
    mu = jnp.mean(v, axis=-1, keepdims=True)
    c = v - mu
    return c, lax.rsqrt(jnp.mean(c * c, axis=-1, keepdims=True) + EPSILON)


def eye(n, value=1.0):
    r = lax.broadcasted_iota(jnp.int32, (n, n), 0)
    c = lax.broadcasted_iota(jnp.int32, (n, n), 1)
    return jnp.where(r == c, value, 0.0).astype(BF16)


def skew_bits(which):
    lane = lax.broadcasted_iota(jnp.int32, (1, PADDED), 1)
    r = lane // WIN
    return WIN - 1 - (jnp.minimum(r, WIN - 1) if which == 0 else lane - r * WIN)


def split(v):
    hi = v.astype(BF16)
    return hi, (v - hi.astype(F32)).astype(BF16)


def key_side(k, ohm):
    return jnp.concatenate([k, ohm], axis=1)


def query_side(qa, h):
    z = jnp.zeros((HEAD_DIM, PADDED), BF16)
    own = qa[h * 64:(h + 1) * 64]
    bias = qa[128 + 64 * h:192 + 64 * h]
    return jnp.concatenate(([own, z] if h == 0 else [z, own]) + [bias, z], axis=0)


def forward_kernel(live, x_ref, go_ref, ohm_ref, vec_ref, wqkv_ref, mix_ref, shift_ref, wproj_ref, *rest):
    x1_ref, xhat_ref, qkv_ref, qaug_ref, o_ref, lse_ref, mask_ref, dm_ref, h1_ref, wide = rest[-10:]
    rows = live * PADDED
    for w in range(live):
        here = slice(AREA * w, AREA * (w + 1))
        c, r = norm(x_ref[here, :].astype(F32))
        xhat = c * r
        valid = jnp.where(ohm_ref[w, 0:AREA, 14:15] < 0.0, 0.0, 1.0)
        h1_ref[w, PADDED - 16:, :] = jnp.zeros((16, MODEL), BF16)
        xhat_ref[w, PADDED - 16:, :] = jnp.zeros((16, MODEL), BF16)
        h1_ref[w, 0:AREA, :] = (xhat * vec_ref[LN1_GAIN] + vec_ref[LN1_BIAS]).astype(BF16)
        xhat_ref[w, 0:AREA, :] = xhat.astype(BF16)
        mask_ref[here, :] = valid
        dm_ref[here, :] = (go_ref[here, :].astype(F32) * valid).astype(BF16)
    for w in range(live, xhat_ref.shape[0]):
        xhat_ref[w] = jnp.zeros((PADDED, MODEL), BF16)
        o_ref[w] = jnp.zeros((PADDED, MODEL), BF16)

    for j, offset in enumerate((QUERY_BIAS, None, VALUE_BIAS)):
        cs = slice(j * MODEL, (j + 1) * MODEL)
        p = mm(h1_ref[0:live].reshape(rows, MODEL), wqkv_ref[:, cs])
        p = p if offset is None else p + vec_ref[offset]
        qkv_ref[0:live, :, cs] = p.astype(BF16).reshape(live, PADDED, MODEL)

    together = 4 if live % 4 == 0 else 1

    @pl.loop(0, live // together)
    def _(it):
        heads = [(it * together + n, p) for n in range(together) for p in range(PAIRS)]
        lanes = lambda part, p: slice(part * MODEL + p * 128, part * MODEL + (p + 1) * 128)
        qs = [qkv_ref[w, :, lanes(0, p)] for w, p in heads]
        us = [mm(mix_ref[...], jnp.concatenate([q, q], axis=1), NT) for q in qs]
        qts = [(q.T * SCALE).astype(BF16) for q in qs]
        vts = [qkv_ref[w, :, lanes(2, p)].T for w, p in heads]
        row = lax.broadcasted_iota(jnp.int32, (16, 1), 0)
        qas = []
        for (w, p), u, qt in zip(heads, us, qts):
            tabs = []
            for t in range(2):
                a = u[64 * t:64 * t + 64]
                for n, b in enumerate((8, 4, 2, 1)):
                    cond = shift_ref[4 * t + n:4 * t + n + 1, :] > 0
                    a = jnp.where(cond, pltpu.roll(a, 64 - b, 0), a)
                tabs.append(a)
            parts = [qt]
            for h in range(2):
                ah = jnp.where(row == 14, 1.0, tabs[0][32 * h:32 * h + 16])
                aw = tabs[1][32 * h:32 * h + 16]
                hh, hl = split(ah)
                wh, wl = split(aw)
                parts += [hh, wh, hl, wl]
            qa = jnp.concatenate(parts, axis=0)
            qaug_ref[w, p] = qa
            qas.append(qa)
        keys = [key_side(qkv_ref[w, :, lanes(1, p)], ohm_ref[w]) for w, p in heads]
        scores = [mm(key, query_side(qa, h)) for key, qa in zip(keys, qas) for h in range(2)]
        ots = []
        for n, s in enumerate(scores):
            (w, p), h = heads[n // 2], n % 2
            top = jnp.max(s, axis=0, keepdims=True)
            e = jnp.exp(s - top)
            total = jnp.sum(e, axis=0, keepdims=True)
            lse_ref[w, p, h:h + 1, :] = top + jnp.log(total)
            ots.append(mm(vts[n // 2][64 * h:64 * h + 64], e.astype(BF16)) * (1.0 / total))
        for n, (w, p) in enumerate(heads):
            ot = jnp.concatenate(ots[2 * n:2 * n + 2], axis=0).astype(BF16)
            o_ref[w, :, lanes(0, p)] = ot.T

    wide[0:rows, :] = mm(o_ref[0:live].reshape(rows, MODEL), wproj_ref[...]) + vec_ref[PROJ_BIAS]
    for w in range(live):
        here = slice(AREA * w, AREA * (w + 1))
        x1_ref[here, :] = x_ref[here, :].astype(F32) + wide[PADDED * w:PADDED * w + AREA, :]


def cost(us):
    return pl.CostEstimate(flops=int(us * 1.0e9), bytes_accessed=1 << 20, transcendentals=0)


def once(a):
    return pl.BlockSpec(a.shape, lambda i: (0,) * a.ndim, pipeline_mode=pl.Buffered(1))


def blocked(*shape):
    return pl.BlockSpec(shape, lambda i: (i,) + (0,) * (len(shape) - 1))


def block_windows(windows):
    return 4 if windows % 4 == 0 else windows


def attention_forward(x, go, ohm, vec, wqkv, mix, shift, wproj, windows, at, count, live, held):
    wb = block_windows(windows)
    outs = [((windows * AREA, MODEL), F32, (wb * AREA, MODEL)),
            ((windows, PADDED, MODEL), BF16, (wb, PADDED, MODEL)),
            ((windows, PADDED, 3 * MODEL), BF16, (wb, PADDED, 3 * MODEL)),
            ((windows, PAIRS, 256, PADDED), BF16, (wb, PAIRS, 256, PADDED)),
            ((windows, PADDED, MODEL), BF16, (wb, PADDED, MODEL)),
            ((windows, PAIRS, 2, PADDED), F32, (wb, PAIRS, 2, PADDED)),
            ((windows * AREA, 1), F32, (wb * AREA, 1)),
            ((windows * AREA, MODEL), BF16, (wb * AREA, MODEL))]
    part = lambda *shape: pl.BlockSpec(shape, lambda i: (i + at,) + (0,) * (len(shape) - 1))
    extra = list(held or [])
    return pl.pallas_call(
        functools.partial(forward_kernel, live),
        grid=(count,),
        in_specs=[blocked(live * AREA, MODEL), blocked(live * AREA, MODEL), blocked(live, PADDED, 128)]
        + [once(a) for a in (vec, wqkv, mix, shift, wproj)] + [pl.BlockSpec(memory_space=pl.ANY)] * len(extra),
        out_specs=[part(*b) for _, _, b in outs],
        out_shape=[jax.ShapeDtypeStruct(s, t) for s, t, _ in outs],
        input_output_aliases={8 + n: n for n in range(len(extra))},
        scratch_shapes=[pltpu.VMEM((wb, PADDED, MODEL), BF16), pltpu.VMEM((wb * PADDED, MODEL), F32)],
        cost_estimate=cost(14 * count * live // wb),
        compiler_params=pltpu.CompilerParams(vmem_limit_bytes=VMEM_LIMIT, dimension_semantics=("arbitrary",)),
        name="attention_forward",
    )(x, go, ohm, vec, wqkv, mix, shift, wproj, *extra)


BLOCK = 384
BLOCKS = 4 * MODEL // BLOCK


def backward_kernel(live, core_ref, da_ref, ohm_ref, oht_ref, qkv_ref, qaug_ref, lse_ref, wproj_ref, relt_ref, shift_ref, xhat_ref, o_ref, vec_ref,
                    wqkv_ref, dp_ref, grel_ref, keep_ref, send_ref, sum_ref, gvec_ref, bvec_ref,
                    do_ref, dap_ref, turned, acc, wstage, dstage, wsems, dsems):
    wb = ohm_ref.shape[0]
    rows = wb * PADDED
    step = pl.program_id(0)

    @pl.when(step == 0)
    def _():
        grel_ref[...] = jnp.zeros_like(grel_ref)
        acc[...] = jnp.zeros_like(acc)
        turned[MODEL:, :] = jnp.ones((16, rows), BF16)

    for w in range(wb):
        dap_ref[w, PADDED - 16:, :] = jnp.zeros((16, MODEL), BF16)
        dap_ref[w, 0:AREA, :] = da_ref[AREA * w:AREA * (w + 1), :]
    final = step == pl.num_programs(0) - 1
    if live < wb:
        @pl.when(final)
        def _():
            dap_ref[live:] = jnp.zeros((wb - live, PADDED, MODEL), BF16)
            dp_ref[live:] = jnp.zeros((wb - live, PADDED, 3 * MODEL), BF16)

    def outer(count):
        n = count * PADDED
        dap = dap_ref[0:count].reshape(n, MODEL)
        do_ref[0:count] = mm(dap, wproj_ref[...], NT).astype(BF16).reshape(count, PADDED, MODEL)
        turned[0:MODEL, 0:n] = o_ref[0:count].reshape(n, MODEL).T
        acc[0:MODEL, 3 * MODEL:] += mm(turned[0:MODEL, 0:n], dap)

    def inner(count):
        n = count * PADDED
        turned[0:MODEL, 0:n] = xhat_ref[0:count].reshape(n, MODEL).T
        for j in range(3):
            cs = slice(j * MODEL, (j + 1) * MODEL)
            acc[:, cs] += mm(turned[:, 0:n], dp_ref[0:count, :, cs].reshape(n, MODEL))

    def either(run):
        if live == wb:
            run(wb)
        else:
            pl.when(final)(lambda: run(live))
            pl.when(jnp.logical_not(final))(lambda: run(wb))

    either(outer)
    together = 1

    @pl.loop(0, jnp.where(final, live, wb) // together)
    def _(it):
        heads = [(it * together + n, p) for n in range(together) for p in range(PAIRS)]
        lanes = lambda part, p: slice(part * MODEL + p * 128, part * MODEL + (p + 1) * 128)
        both = [(n, w, p, h) for n, (w, p) in enumerate(heads) for h in range(2)]
        qs = [qkv_ref[w, :, lanes(0, p)] for w, p in heads]
        ks = [qkv_ref[w, :, lanes(1, p)] for w, p in heads]
        vs = [qkv_ref[w, :, lanes(2, p)] for w, p in heads]
        dos = [do_ref[w, :, lanes(0, p)] for w, p in heads]
        scores = [mm(key_side(ks[n], ohm_ref[w]), query_side(qaug_ref[w, p], h)) for n, w, p, h in both]
        dots = [do.T for do in dos]
        kts = [(k.T * SCALE).astype(BF16) for k in ks]
        z = jnp.zeros((HEAD_DIM, PADDED), BF16)
        dws = []
        for n, w, p, h in both:
            own = dots[n][64 * h:64 * h + 64]
            dws.append(mm(vs[n], jnp.concatenate([own, z] if h == 0 else [z, own], axis=0)))
        dvs, dks, dqs = [], [], []
        for s, dw, (n, w, p, h) in zip(scores, dws, both):
            a = jnp.exp(s - lse_ref[w, p, h:h + 1, :])
            t = a * dw
            dsb = (t - a * jnp.sum(t, axis=0, keepdims=True)).astype(BF16)
            dvs.append(mm(dots[n][64 * h:64 * h + 64], a.astype(BF16), NT))
            dks.append(mm(qaug_ref[w, p, 64 * h:64 * h + 64, :], dsb, NT))
            dqs.append(mm(jnp.concatenate([kts[n][64 * h:64 * h + 64], oht_ref[...]], axis=0), dsb))
        zz = jnp.zeros((16, PADDED), F32)
        dqts = []
        for n, (w, p) in enumerate(heads):
            tabs = []
            for t in range(2):
                lo = 64 + 16 * t
                a = jnp.concatenate([dqs[2 * n][lo:lo + 16], zz, dqs[2 * n + 1][lo:lo + 16], zz], axis=0)
                for i, b in enumerate((8, 4, 2, 1)):
                    cond = shift_ref[4 * t + i:4 * t + i + 1, :] > 0
                    a = jnp.where(cond, pltpu.roll(a, b, 0), a)
                tabs.append(a.astype(BF16))
            dqt = []
            for h in range(2):
                du = jnp.concatenate([tabs[0][32 * h:32 * h + 32], tabs[1][32 * h:32 * h + 32]], axis=0)
                dqt.append(dqs[2 * n + h][0:64] + mm(relt_ref[...], jnp.concatenate([du, du], axis=0)))
                grel_ref[h] += mm(du, qs[n])
            dqts.append(jnp.concatenate(dqt, axis=0).astype(BF16))
        for n, (w, p) in enumerate(heads):
            dp_ref[w, :, lanes(0, p)] = dqts[n].T
            dp_ref[w, :, lanes(1, p)] = jnp.concatenate(dks[2 * n:2 * n + 2], axis=0).astype(BF16).T
            dp_ref[w, :, lanes(2, p)] = jnp.concatenate(dvs[2 * n:2 * n + 2], axis=0).astype(BF16).T

    either(inner)

    @pl.when(final)
    def _():
        columns = jnp.concatenate([vec_ref[...]] * 16, axis=0).T
        gain, bias = columns[:, 0:1], columns[:, 1:2]
        nq = 3 * MODEL // BLOCK
        sum_ref[...] = acc[MODEL:MODEL + 8, 0:3 * MODEL]
        gsum, bsum = jnp.zeros((MODEL, 128), F32), jnp.zeros((MODEL, 128), F32)
        take = lambda n: pltpu.make_async_copy(wqkv_ref.at[:, pl.ds(n * BLOCK, BLOCK)], wstage.at[n % 2], wsems.at[n % 2])
        core = core_ref[0]

        def give(n, act):
            for k, to, c in ((0, keep_ref, core), (1, send_ref, 1 - core)):
                act(pltpu.make_async_copy(dstage.at[n % 2, :, c], to.at[n], dsems.at[n % 2, k]))
        start, wait = (lambda cp: cp.start()), (lambda cp: cp.wait())
        take(0).start()
        for n in range(BLOCKS):
            cs = slice(n * BLOCK, (n + 1) * BLOCK)
            if n + 1 < nq:
                take(n + 1).start()
            if n >= 2:
                give(n - 2, wait)
            m = acc[0:MODEL, cs]
            if n < nq:
                s = acc[MODEL:MODEL + 1, cs]
                take(n).wait()
                w = wstage[n % 2].astype(F32)
                g, b = w * m, w * s
                gsum += sum(g[:, 128 * i:128 * (i + 1)] for i in range(BLOCK // 128))
                bsum += sum(b[:, 128 * i:128 * (i + 1)] for i in range(BLOCK // 128))
                m = m * gain + bias * s
            dstage[n % 2] = m.astype(BF16).reshape(dstage.shape[1:])
            give(n, start)
        gvec_ref[...] = jnp.broadcast_to(jnp.sum(gsum.T, axis=0, keepdims=True), gvec_ref.shape)
        bvec_ref[...] = jnp.broadcast_to(jnp.sum(bsum.T, axis=0, keepdims=True), bvec_ref.shape)
        give(BLOCKS - 2, wait)
        give(BLOCKS - 1, wait)


def attention_backward(da, ohm, oht, qkv, qaug, lse, wproj, relt, shift, xhat, o, vec, wqkv, core, dp_size, live):
    windows = ohm.shape[0]
    wb = block_windows(windows)
    block = lambda *shape: pl.BlockSpec(shape, lambda i, _: (i,) + (0,) * (len(shape) - 1))
    whole = lambda a: pl.BlockSpec(a.shape, lambda i, _: (0,) * a.ndim, pipeline_mode=pl.Buffered(1))
    row = MODEL // dp_size
    fixed = lambda *shape: pl.BlockSpec(shape, lambda i, _: (0,) * len(shape))
    anywhere = pl.BlockSpec(memory_space=pl.ANY)
    return pl.pallas_call(
        functools.partial(backward_kernel, live),
        grid_spec=pltpu.PrefetchScalarGridSpec(
            num_scalar_prefetch=1,
            grid=(windows // wb,),
            in_specs=[block(wb * AREA, MODEL), block(wb, PADDED, 128), whole(oht), block(wb, PADDED, 3 * MODEL),
                  block(wb, PAIRS, 256, PADDED), block(wb, PAIRS, 2, PADDED), whole(wproj), whole(relt), whole(shift),
                  block(wb, PADDED, MODEL), block(wb, PADDED, MODEL), whole(vec), anywhere],
        out_specs=[block(wb, PADDED, 3 * MODEL), fixed(2, 64, 128), anywhere, anywhere, fixed(8, 3 * MODEL), fixed(8, MODEL), fixed(8, MODEL)],
        scratch_shapes=[pltpu.VMEM((wb, PADDED, MODEL), BF16), pltpu.VMEM((wb, PADDED, MODEL), BF16),
                        pltpu.VMEM((MODEL + 16, wb * PADDED), BF16), pltpu.VMEM((MODEL + 16, 4 * MODEL), F32),
                        pltpu.VMEM((2, MODEL, BLOCK), BF16), pltpu.VMEM((2, dp_size // 2, 2, row, BLOCK), BF16),
                        pltpu.SemaphoreType.DMA((2,)), pltpu.SemaphoreType.DMA((2, 2))]),
        out_shape=[jax.ShapeDtypeStruct((windows, PADDED, 3 * MODEL), BF16), jax.ShapeDtypeStruct((2, 64, 128), F32),
                   jax.ShapeDtypeStruct((BLOCKS, dp_size // 2, row, BLOCK), BF16),
                   jax.ShapeDtypeStruct((BLOCKS, dp_size // 2, row, BLOCK), BF16), jax.ShapeDtypeStruct((8, 3 * MODEL), F32),
                   jax.ShapeDtypeStruct((8, MODEL), F32), jax.ShapeDtypeStruct((8, MODEL), F32)],
        cost_estimate=cost(95),
        compiler_params=pltpu.CompilerParams(vmem_limit_bytes=VMEM_LIMIT, dimension_semantics=("arbitrary",)),
        name="attention_backward",
    )(core, da, ohm, oht, qkv, qaug, lse, wproj, relt, shift, xhat, o, vec, wqkv)


def input_kernel(live, x_ref, da_ref, dp_ref, vec_ref, wqkv_ref, *rest):
    gx_ref, wide, tall = rest[-3:]
    wide[0:live * PADDED, :] = mm(dp_ref[0:live].reshape(live * PADDED, 3 * MODEL), wqkv_ref[...], NT)
    for w in range(live):
        tall[AREA * w:AREA * (w + 1), :] = wide[PADDED * w:PADDED * w + AREA, :]
    rows = live * AREA
    for lo in range(0, rows, 112):
        hi = min(lo + 112, rows)
        c, r = norm(x_ref[lo:hi, :].astype(F32))
        xhat = c * r
        dx = tall[lo:hi, :] * vec_ref[LN1_GAIN]
        dx = r * (dx - jnp.mean(dx, axis=-1, keepdims=True) - xhat * jnp.mean(dx * xhat, axis=-1, keepdims=True))
        gx_ref[lo:hi, :] = (dx + da_ref[lo:hi, :].astype(F32)).astype(BF16)


def input_gradient(x, da, dp, vec, wqkv, at, count, x_at, live, held):
    windows = dp.shape[0]
    wb = block_windows(windows)
    part = lambda *shape: pl.BlockSpec(shape, lambda i: (i + at,) + (0,) * (len(shape) - 1))
    extra = [] if held is None else [held]
    return pl.pallas_call(
        functools.partial(input_kernel, live),
        grid=(count,),
        in_specs=[pl.BlockSpec((live * AREA, MODEL), lambda i: (i + x_at, 0)), part(wb * AREA, MODEL), part(wb, PADDED, 3 * MODEL),
                  once(vec), once(wqkv)] + [pl.BlockSpec(memory_space=pl.ANY)] * len(extra),
        out_specs=part(wb * AREA, MODEL),
        out_shape=jax.ShapeDtypeStruct((windows * AREA, MODEL), BF16),
        input_output_aliases={5: 0} if extra else {},
        scratch_shapes=[pltpu.VMEM((wb * PADDED, MODEL), F32), pltpu.VMEM((wb * AREA, MODEL), F32)],
        cost_estimate=cost(6 * count),
        compiler_params=pltpu.CompilerParams(vmem_limit_bytes=VMEM_LIMIT, dimension_semantics=("arbitrary",)),
        name="input_gradient",
    )(x, da, dp, vec, wqkv, *extra)


def constant_tables():
    place = np.arange(PADDED)
    real = place < AREA
    r, c = np.where(real, place // WIN, 0), np.where(real, place % WIN, 0)
    hot = [((WIN - 1 - v)[:, None] == np.arange(16)) & real[:, None] for v in (r, c)]
    keys = np.concatenate(hot + hot, axis=1).astype(np.float32)
    shift = np.stack([(v >> b) & 1 for v in (r, c) for b in (3, 2, 1, 0)]).astype(np.int32)
    return keys, np.concatenate(hot, axis=1).T.astype(np.float32), shift


def key_tables(window_extent):
    keys = constant_tables()[0]
    place = np.arange(PADDED)
    r, c = place // WIN, place % WIN
    valid = (r < window_extent[:, 0:1]) & (c < window_extent[:, 1:2]) & (place < AREA)
    keys = np.concatenate([keys, np.zeros((PADDED, 64), np.float32)], axis=1)
    flag = np.arange(128) == 14
    return jnp.where(flag[None, None, :], jnp.where(valid, 0.0, NEGATIVE)[:, :, None], keys[None]).astype(BF16)


def small_tables(rel_h, rel_w):
    _, oht, shift = constant_tables()
    both = jnp.pad(jnp.stack([rel_h, rel_w]), ((0, 0), (0, 5), (0, 0)))
    hi = both.astype(BF16).astype(F32)
    lo = both - hi
    parity = np.eye(2, dtype=np.float32)
    spread = lambda t: (t[:, None, :, None, :] * parity[None, :, None, :, None]).reshape(128, 128)
    mix = jnp.concatenate([spread(hi), spread(lo)], axis=1).astype(BF16)
    relt = jnp.concatenate([hi.reshape(64, HEAD_DIM), lo.reshape(64, HEAD_DIM)], axis=0).T.astype(BF16)
    return jnp.asarray(oht, BF16), jnp.asarray(shift), mix, relt


def gelu_parts(z):
    u = jnp.abs(z)
    t = 1.0 / (1.0 + 0.23164189 * u)
    e = jnp.exp2(z * (z * -0.72134752))
    poly = t * (0.127414796 + t * (-0.142248368 + t * (0.7107068705 + t * (-0.7265760135 + t * 0.5307027145))))
    q = poly * e
    phi = jnp.where(z >= 0.0, 1.0 - q, q)
    return z * phi, phi + z * e * 0.3989422804


ROWS = 512
CHUNK = 768
SLICES = 4


def mlp_kernel(rows, widths, offset_ref, x1_ref, dy_ref, mask_ref, par_ref, upb_ref, *rest):
    n = len(widths)
    ups, downs = rest[:n], rest[n:2 * n]
    out_ref, da_ref, dw_ref, dbu_ref, vec_ref, h2, dm, h2t, dmt, macc, dacc, accu, accd, zs, das, gs, dzs, stage, sems = rest[2 * n:]
    rb = h2.shape[0]
    ch = 512
    step = pl.program_id(0)

    @pl.when(step == 0)
    def _():
        accu[...] = jnp.zeros_like(accu)
        accd[...] = jnp.zeros_like(accd)
        h2t[MODEL:, :] = jnp.ones((16, h2t.shape[1]), BF16)
        vec_ref[...] = jnp.zeros_like(vec_ref)

    def live(i):
        row = step * rb + i * ch + lax.broadcasted_iota(jnp.int32, (ch, 1), 0)
        return row < rows

    @pl.loop(0, rb // ch)
    def _(i):
        rs = pl.ds(pl.multiple_of(i * ch, ch), ch)
        x1 = jnp.where(live(i), x1_ref[rs, :], 0.0)
        c, r = norm(x1)
        h2[rs, :] = (c * r * par_ref[LN2_GAIN] + par_ref[LN2_BIAS]).astype(BF16)
        d = jnp.where(live(i), dy_ref[rs, :].astype(F32), 0.0)
        dm[rs, :] = d.astype(BF16)
        vec_ref[0:8, :] += fold8(d)

    h2t[0:MODEL, :] = h2[...].T
    dmt[...] = dm[...].T

    chunks, at = [], 0
    for up_ref, down_ref, width in zip(ups, downs, widths):
        size = min(CHUNK, width)
        for lo in range(0, width, size):
            chunks.append((up_ref, down_ref, slice(lo, lo + size), slice(at, at + size)))
            at += size
    count, part = len(chunks), rb // SLICES

    def products(u):
        up_ref, down_ref, here, there = chunks[u // SLICES]
        rs = slice(u % SLICES * part, (u % SLICES + 1) * part)
        zs[u % 2] = mm(h2[rs, :], up_ref[:, here])
        das[u % 2] = mm(dm[rs, :], down_ref[:, here])

    def activate(u):
        there = chunks[u // SLICES][3]
        rs = slice(u % SLICES * part, (u % SLICES + 1) * part)
        g, gp = gelu_parts(zs[u % 2] + upb_ref[:, there])
        dz = (das[u % 2] * gp).astype(BF16)
        gs[u // SLICES % 2, rs, :] = g.astype(BF16)
        dzs[u // SLICES % 2, rs, :] = dz

    def consume(j, i):
        up_ref, down_ref, here, there = chunks[j]
        g, dz = gs.at[j % 2], dzs.at[j % 2]
        if i == 0:
            m = mm(g[...], down_ref[:, here], NT)
            macc[...] = m if j == 0 else macc[...] + m
        if i == 1:
            d = mm(dz[...], up_ref[:, here], NT)
            dacc[...] = d if j == 0 else dacc[...] + d
        if i == 2:
            accd[:, there] += mm(dmt[...], g[...])
        if i == 3:
            accu[:, there] += mm(h2t[...], dz[...])

    units = count * SLICES
    per = 4 // SLICES
    products(0)
    for u in range(units + SLICES):
        if u + 1 < units:
            products(u + 1)
        if u >= SLICES:
            for k in range(per):
                consume(u // SLICES - 1, u % SLICES * per + k)
        if u < units:
            activate(u)

    @pl.loop(0, rb // ch)
    def _(i):
        rs = pl.ds(pl.multiple_of(i * ch, ch), ch)
        x1 = jnp.where(live(i), x1_ref[rs, :], 0.0)
        c, r = norm(x1)
        xhat = c * r
        valid = live(i) & (mask_ref[rs, :] > 0.0)
        out_ref[rs, :] = jnp.where(valid, x1 + macc[rs, :] + par_ref[DOWN_BIAS], 0.0).astype(BF16)
        dh = dacc[rs, :]
        vec_ref[8:16, :] += fold8(dh * xhat)
        vec_ref[16:24, :] += fold8(dh)
        dx = dh * par_ref[LN2_GAIN]
        dx = r * (dx - jnp.mean(dx, axis=-1, keepdims=True) - xhat * jnp.mean(dx * xhat, axis=-1, keepdims=True))
        da = (dx + dm[rs, :].astype(F32)).astype(BF16)
        da_ref[rs, :] = da
        vec_ref[24:32, :] += fold8(da.astype(F32))

    @pl.when(step == pl.num_programs(0) - 1)
    def _():
        size = stage.shape[2]
        dbu_ref[...] = accu[MODEL:MODEL + 8, :]
        each = accu.shape[1] // size

        def copy(k):
            to = pl.multiple_of(offset_ref[k], 128)
            return pltpu.make_async_copy(stage.at[k % 2], dw_ref.at[:, pl.ds(to, size)], sems.at[k % 2])
        for k in range(2 * each):
            if k >= 2:
                copy(k - 2).wait()
            src = (accu, accd)[k // each]
            stage[k % 2] = src[0:MODEL, (k % each) * size:(k % each + 1) * size].astype(BF16)
            copy(k).start()
        copy(2 * each - 2).wait()
        copy(2 * each - 1).wait()


def mlp(x1, dy, mask, par, upb, ups, downs, offsets, live_rows):
    rows, d = x1.shape
    widths = tuple(u.shape[1] for u in ups)
    ff = sum(widths)
    size = 2 * ff // offsets.shape[0]
    rb = ROWS
    full = lambda a: pl.BlockSpec(a.shape, lambda i, _: (0, 0), pipeline_mode=pl.Buffered(1))
    rowspec = lambda w: pl.BlockSpec((rb, w), lambda i, _: (i, 0))
    return pl.pallas_call(
        functools.partial(mlp_kernel, live_rows, widths),
        grid_spec=pltpu.PrefetchScalarGridSpec(
            num_scalar_prefetch=1,
            grid=(pl.cdiv(live_rows, rb),),
            in_specs=[rowspec(d), rowspec(d), rowspec(1)] + [full(a) for a in (par, upb, *ups, *downs)],
            out_specs=[rowspec(d), rowspec(d), pl.BlockSpec(memory_space=pl.ANY),
                       pl.BlockSpec((8, ff), lambda i, _: (0, 0)), pl.BlockSpec((32, d), lambda i, _: (0, 0))],
            scratch_shapes=[pltpu.VMEM((rb, d), BF16), pltpu.VMEM((rb, d), BF16), pltpu.VMEM((d + 16, rb), BF16), pltpu.VMEM((d, rb), BF16),
                            pltpu.VMEM((rb, d), F32), pltpu.VMEM((rb, d), F32), pltpu.VMEM((d + 16, ff), F32), pltpu.VMEM((d, ff), F32),
                            pltpu.VMEM((2, rb // SLICES, CHUNK), F32), pltpu.VMEM((2, rb // SLICES, CHUNK), F32),
                            pltpu.VMEM((2, rb, CHUNK), BF16), pltpu.VMEM((2, rb, CHUNK), BF16), pltpu.VMEM((2, d, size), BF16), pltpu.SemaphoreType.DMA((2,))]),
        out_shape=[jax.ShapeDtypeStruct((rows, d), BF16), jax.ShapeDtypeStruct((rows, d), BF16),
                   jax.ShapeDtypeStruct((d, 2 * ff), BF16), jax.ShapeDtypeStruct((8, ff), F32), jax.ShapeDtypeStruct((32, d), F32)],
        cost_estimate=cost(170),
        compiler_params=pltpu.CompilerParams(vmem_limit_bytes=VMEM_LIMIT, dimension_semantics=("arbitrary",)),
        name="mlp",
    )(offsets, x1, dy, mask, par, upb, *ups, *downs)


GROUP_WIN = 40
SPARE = 2


def bits(n):
    return n.bit_length() - 1


def swap(value, axis, bit, sizes):
    return lax.ppermute(value, axis, [(i, i ^ (1 << bit)) for i in range(sizes[axis])])


def bit_of(axis, bit):
    return (lax.axis_index(axis) >> bit) & 1


def add(a, b):
    return (a.astype(F32) + b.astype(F32)).astype(BF16)


def split_dp(held, at, bit):
    mine = bit_of("dp", bit)
    return tuple(lax.dynamic_index_in_dim(held, m, at, keepdims=False) for m in (mine, 1 - mine))


def split_mlp(held, owners, bit):
    mine = bit_of("mlp", bit) == 1
    sides = []
    for side in range(2):
        runs = [n for n, o in enumerate(owners) if (o >> bit) & 1 == side]
        sides.append(jnp.concatenate([held[n:n + 1] for n in runs], axis=0))
    return jnp.where(mine, sides[1], sides[0]), jnp.where(mine, sides[0], sides[1])


def reduce_steps(keep, send, owners, sizes):
    nb, nm = bits(sizes["dp"]), bits(sizes["mlp"])
    apart = lambda v: v.reshape((v.shape[0],) + (2,) * (nb - 1) + v.shape[2:])
    got = yield [("dp", 0, send)]
    held = apart(add(keep, got[0]))
    orders = ([("mlp", b) for b in reversed(range(nm))] + [("dp", 1)], [("dp", 1)] + [("mlp", b) for b in reversed(range(nm))])
    halves = [held[:, 0], held[:, 1]]
    left = [list(owners), list(owners)]
    dims = [nb - 2, nb - 2]
    plan = list(zip(*orders)) + [(("dp", b), ("dp", b)) for b in range(2, nb - 1)]
    for both in plan:
        kept, sends = [], []
        for n, (axis, bit) in enumerate(both):
            if axis == "mlp":
                keep, send = split_mlp(halves[n], left[n], bit)
                mine = [o for o in left[n] if (o >> bit) & 1 == 0]
                left[n] = [o & ~(1 << bit) for o in mine]
            else:
                keep, send = split_dp(halves[n], dims[n], bit)
                dims[n] -= 1
            kept.append(keep)
            sends.append((axis, bit, send))
        got = yield sends
        halves = [add(k, g) for k, g in zip(kept, got)]
    mine = bit_of("dp", nb - 1) == 1
    got = yield [("dp", nb - 1, jnp.where(mine, halves[0], halves[1]))]
    yield add(jnp.where(mine, halves[1], halves[0]), got[0])


def sum_steps(v, sizes):
    for axis in ("dp", "mlp"):
        for b in range(bits(sizes[axis])):
            got = yield [(axis, b, v)]
            v = v + got[0]
    yield v


def pair_steps(v, width):
    mine = lax.axis_index("mlp") == 1
    low, high = v[:, :width], v[:, width:]
    got = yield [("mlp", 0, jnp.where(mine, low, high))]
    yield add(jnp.where(mine, high, low), got[0])


def run_steps(tasks, delays, work, sizes):
    states = [next(t) if not d else None for t, d in zip(tasks, delays)]
    results = [None] * len(tasks)
    turn = 0
    while any(r is None for r in results):
        turn += 1
        sends = [(n, s) for n, state in enumerate(states) if isinstance(state, list) for s in state]
        values = work(turn, [s[2] for _, s in sends], [swap_by(s[0], s[1], sizes) for _, s in sends])
        for n, task in enumerate(tasks):
            if isinstance(states[n], list):
                states[n] = task.send([v for v, (owner, _) in zip(values, sends) if owner == n])
                if not isinstance(states[n], list):
                    results[n] = states[n]
            elif results[n] is None and turn >= delays[n]:
                states[n] = next(task)
    return results


def swap_by(axis, bit, sizes):
    return lambda v: swap(v, axis, bit, sizes)


def feed_forward_weights(up, up_bias, down, sizes):
    width = up.shape[1]
    if sizes["mlp"] != 2:
        gather = lambda v: lax.all_gather(v, "mlp", axis=v.ndim - 1, tiled=True)
        count = sizes["mlp"]
        return [gather(up)], [gather(down)], gather(up_bias), jnp.arange(count, dtype=jnp.int32) * width, width
    half = width // 2
    core, me = bit_of("dp", 0), lax.axis_index("mlp")
    cut = lambda v: jnp.where(core == 1, v[:, half:], v[:, :half])
    far_up, far_down = swap(cut(up), "mlp", 0, sizes), swap(cut(down), "mlp", 0, sizes)
    far_bias = swap(up_bias, "mlp", 0, sizes)
    bias = jnp.concatenate([up_bias, jnp.roll(far_bias, -core * half)])
    places = jnp.stack([me * width, me * width + half, (1 - me) * width + core * half, (1 - me) * width + (1 - core) * half])
    return (up, far_up), (down, far_down), bias, places.astype(jnp.int32), half


def per_device(
    sizes,
    tokens,
    window_extent,
    ln1_gain,
    ln1_bias,
    qkv_weight,
    query_bias,
    value_bias,
    rel_h,
    rel_w,
    proj_weight,
    proj_bias,
    ln2_gain,
    ln2_bias,
    up_weight,
    up_bias,
    down_weight,
    down_bias,
    grad_out,
):
    owners = sizes["mlp"]
    line = lambda v: v.reshape(1, -1)
    ups, downs, up_bias_here, places, piece = feed_forward_weights(up_weight, up_bias, down_weight, sizes)
    windows = window_extent.shape[0]
    wb = block_windows(windows)
    blocks = windows // wb
    me = lax.axis_index("mlp")
    share = owners == 2 and 2 * windows == GROUP_WIN
    live = wb - SPARE if share else wb
    live_rows = (windows - wb + live) * AREA
    near, far = (windows - wb) * AREA, (windows - SPARE) * AREA
    oht, shift, mix, relt = small_tables(rel_h, rel_w)
    par = jnp.stack([ln1_gain, ln1_bias, query_bias, value_bias, proj_bias, ln2_gain, ln2_bias, down_bias])
    ohm = key_tables(window_extent)
    weights = (par, qkv_weight, mix, shift, proj_weight)
    if share:
        def taken(v, here, there):
            other = lax.ppermute(v[there:], "mlp", [(0, 1)])
            return jnp.where(me == 0, v[here:here + other.shape[0]], other)
        tail_x, tail_go = taken(tokens, near, far), taken(grad_out, near, far)
        tail_extent = taken(window_extent.astype(F32), windows - wb, windows - SPARE).astype(jnp.int32)
        tail_ohm = key_tables(tail_extent)
        held = attention_forward(tokens, grad_out, ohm, *weights, windows, 0, blocks - 1, wb, None)
        held = attention_forward(tail_x, tail_go, tail_ohm, *weights, windows, blocks - 1, 1, live, held)
        ohm = jnp.concatenate([ohm[:windows - wb], jnp.pad(tail_ohm, ((0, SPARE), (0, 0), (0, 0)))], axis=0)
    else:
        tail_x = tokens
        held = attention_forward(tokens, grad_out, ohm, *weights, windows, 0, blocks, wb, None)
    x1, xhat, qkv, qaug, o, lse, row_mask, dy = held
    if owners == 2:
        (ups, downs, x1) = lax.optimization_barrier((ups, downs, x1))
        ups, downs = list(ups) + [swap(ups[1], "dp", 0, sizes)], list(downs) + [swap(downs[1], "dp", 0, sizes)]
    width = up_weight.shape[1]
    ff = width * owners
    by_owner = (places // width) * (2 * width) + places % width
    output, da, dw_mlp, up_sums, mid_sums = mlp(
        x1, dy, row_mask, par, line(up_bias_here), ups, downs, jnp.concatenate([by_owner, by_owner + width]), live_rows)

    def give_back(v):
        return lax.ppermute(v[near:live_rows], "mlp", [(1, 0)])

    def completed(v, other):
        tail = jnp.where(me == 0, jnp.concatenate([v[near:live_rows], other], axis=0), 0)
        return lax.dynamic_update_slice(v, tail, (near, 0))

    if share:
        output_tail, da = lax.optimization_barrier((output[near:live_rows], da))
        output_back = lax.ppermute(output_tail, "mlp", [(1, 0)])
    dw_mlp = lax.psum_scatter(dw_mlp, "dp", scatter_dimension=0, tiled=True)
    if owners != 2:
        dw_mlp = lax.psum_scatter(dw_mlp, "mlp", scatter_dimension=1, tiled=True)
    dp_all, grel, dw_keep, dw_send, dp_sums, gain_sums, bias_sums = attention_backward(
        da, ohm, oht, qkv, qaug, lse, proj_weight, relt, shift, xhat, o, par, qkv_weight, bit_of("dp", 0).reshape(1).astype(jnp.int32), sizes["dp"], live)
    if share:
        output = completed(output, output_back)
    up_sum = up_sums[0].reshape(-1, piece)
    up_sum = sum(jnp.where(jnp.arange(ff) // piece == places[n] // piece, jnp.tile(up_sum[n], ff // piece), 0.0)
                 for n in range(ff // piece))
    block_owners = [0, 0, 0, 1, 1, 1, 0, 1]
    if owners != 2:
        def regroup(v):
            parts = [jnp.moveaxis(p, 0, 2) for p in (v[:6], v[6:])]
            parts = [p.reshape(p.shape[:2] + (owners, -1)) for p in parts]
            return jnp.moveaxis(jnp.concatenate(parts, axis=3), 2, 0)
        dw_keep, dw_send = regroup(dw_keep), regroup(dw_send)
        block_owners = list(range(owners))
    rel = grel[0, :, :HEAD_DIM] + grel[1, :, HEAD_DIM:]
    mid = jnp.sum(mid_sums.reshape(4, 8, MODEL), axis=1)
    sums = jnp.concatenate([gain_sums[0], bias_sums[0], dp_sums[0], rel.reshape(-1), mid.reshape(-1), up_sum])
    half = (blocks - 1) // 2
    order = [(blocks - 1, 1)] + [(at, n) for at, n in ((0, half), (half, blocks - 1 - half)) if n]
    held = {"gx": None, "da": da, "at": 0}

    def input_part():
        at, count = order[held["at"]]
        last = at == blocks - 1
        held["gx"] = input_gradient(tail_x if last else tokens, held["da"], dp_all, par, qkv_weight, at, count, 0 if share and last else at,
                                    live if last else wb, held["gx"])
        held["at"] += 1

    def work(turn, values, swaps):
        if held["at"] >= len(order):
            return [f(v) for f, v in zip(swaps, values)]
        values, held["da"] = lax.optimization_barrier((values, held["da"]))
        if share and turn == 3:
            held["back"] = give_back(held["gx"])
        got = [f(v) for f, v in zip(swaps, values)]
        input_part()
        got, held["gx"] = lax.optimization_barrier((got, held["gx"]))
        return got

    tasks = [reduce_steps(dw_keep, dw_send, block_owners, sizes), sum_steps(sums, sizes)]
    delays = [0, 0]
    if owners == 2:
        tasks.append(pair_steps(dw_mlp, 2 * width))
        delays.append(2)
    results = run_steps(tasks, delays, work, sizes)
    late, sums = results[0].astype(F32), results[1]
    late = jnp.concatenate([late[n] for n in range(late.shape[0])], axis=1)
    if owners == 2:
        dw_mlp = results[2]
    while held["at"] < len(order):
        input_part()
    grad_tokens = held["gx"]
    if share:
        grad_tokens = completed(grad_tokens, held["back"])
    d = MODEL
    table = 2 * WIN - 1
    n_rel = 64 * HEAD_DIM
    rel = sums[5 * d:5 * d + n_rel].reshape(64, HEAD_DIM)
    mid = sums[5 * d + n_rel:]
    cols = 3 * MODEL // owners
    dw_mlp = dw_mlp.astype(F32)
    return (
        output,
        grad_tokens,
        sums[0:d],
        sums[d:2 * d],
        late[:, :cols],
        sums[2 * d:3 * d],
        sums[4 * d:5 * d],
        rel[0:table],
        rel[32:32 + table],
        late[:, cols:],
        mid[3 * d:4 * d],
        mid[d:2 * d],
        mid[2 * d:3 * d],
        dw_mlp[:, :width],
        mid[4 * d:],
        dw_mlp[:, width:],
        mid[0:d],
    )


def solution(mesh):
    rows = P(("dp", "mlp"), None)
    in_specs = (rows, rows, P(), P(), P(), P(), P(), P(), P(), P(), P(), P(), P(),
                P(None, "mlp"), P("mlp"), P(None, "mlp"), P(), rows)
    block = P("dp", "mlp")
    out_specs = (rows, rows, P(), P(), block, P(), P(), P(), P(), block, P(), P(), P(), block, P(), block, P())
    sizes = {name: mesh.shape[name] for name in ("dp", "mlp")}
    return jax.shard_map(
        functools.partial(per_device, sizes), mesh=mesh, in_specs=in_specs, out_specs=out_specs, check_vma=False)
```

```python
import functools
import jax
import jax.numpy as jnp
import numpy as np
from jax import lax
from jax.experimental import pallas as pl
from jax.experimental.pallas import tpu as pltpu
from jax.sharding import PartitionSpec as P

HEADS = 12
HEAD_DIM = 64
WIN = 14
AREA = WIN * WIN
PADDED = 208
PAIRS = HEADS // 2
MODEL = HEADS * HEAD_DIM
EPSILON = 1e-6
NEGATIVE = -1e30
SCALE = HEAD_DIM ** -0.5
F32 = jnp.float32
BF16 = jnp.bfloat16
NN = (((1,), (0,)), ((), ()))
NT = (((1,), (1,)), ((), ()))
TN = (((0,), (0,)), ((), ()))
LN1_GAIN, LN1_BIAS, QUERY_BIAS, VALUE_BIAS, PROJ_BIAS, LN2_GAIN, LN2_BIAS, DOWN_BIAS = (slice(n, n + 1) for n in range(8))
VMEM_LIMIT = 60 * 1024 * 1024


def mm(a, b, dims=NN):
    return lax.dot_general(a, b, dims, preferred_element_type=F32)


def fold8(v):
    return jnp.sum(v.reshape(v.shape[0] // 8, 8, v.shape[1]), axis=0)


def norm(v):
    mu = jnp.mean(v, axis=-1, keepdims=True)
    c = v - mu
    return c, lax.rsqrt(jnp.mean(c * c, axis=-1, keepdims=True) + EPSILON)


def eye(n, value=1.0):
    r = lax.broadcasted_iota(jnp.int32, (n, n), 0)
    c = lax.broadcasted_iota(jnp.int32, (n, n), 1)
    return jnp.where(r == c, value, 0.0).astype(BF16)


def skew_bits(which):
    lane = lax.broadcasted_iota(jnp.int32, (1, PADDED), 1)
    r = lane // WIN
    return WIN - 1 - (jnp.minimum(r, WIN - 1) if which == 0 else lane - r * WIN)


def split(v):
    hi = v.astype(BF16)
    return hi, (v - hi.astype(F32)).astype(BF16)


def key_side(k, ohm):
    return jnp.concatenate([k, ohm], axis=1)


def query_side(qa, h):
    z = jnp.zeros((HEAD_DIM, PADDED), BF16)
    own = qa[h * 64:(h + 1) * 64]
    bias = qa[128 + 64 * h:192 + 64 * h]
    return jnp.concatenate(([own, z] if h == 0 else [z, own]) + [bias, z], axis=0)


def forward_kernel(live, x_ref, go_ref, ohm_ref, vec_ref, wqkv_ref, mix_ref, shift_ref, wproj_ref, *rest):
    x1_ref, xhat_ref, qkv_ref, qaug_ref, o_ref, lse_ref, mask_ref, dm_ref, h1_ref, wide = rest[-10:]
    rows = live * PADDED
    for w in range(live):
        here = slice(AREA * w, AREA * (w + 1))
        c, r = norm(x_ref[here, :].astype(F32))
        xhat = c * r
        valid = jnp.where(ohm_ref[w, 0:AREA, 14:15] < 0.0, 0.0, 1.0)
        h1_ref[w, PADDED - 16:, :] = jnp.zeros((16, MODEL), BF16)
        xhat_ref[w, PADDED - 16:, :] = jnp.zeros((16, MODEL), BF16)
        h1_ref[w, 0:AREA, :] = (xhat * vec_ref[LN1_GAIN] + vec_ref[LN1_BIAS]).astype(BF16)
        xhat_ref[w, 0:AREA, :] = xhat.astype(BF16)
        mask_ref[here, :] = valid
        dm_ref[here, :] = (go_ref[here, :].astype(F32) * valid).astype(BF16)
    for w in range(live, xhat_ref.shape[0]):
        xhat_ref[w] = jnp.zeros((PADDED, MODEL), BF16)
        o_ref[w] = jnp.zeros((PADDED, MODEL), BF16)

    for j, offset in enumerate((QUERY_BIAS, None, VALUE_BIAS)):
        cs = slice(j * MODEL, (j + 1) * MODEL)
        p = mm(h1_ref[0:live].reshape(rows, MODEL), wqkv_ref[:, cs])
        p = p if offset is None else p + vec_ref[offset]
        qkv_ref[0:live, :, cs] = p.astype(BF16).reshape(live, PADDED, MODEL)

    together = 4 if live % 4 == 0 else 1

    @pl.loop(0, live // together)
    def _(it):
        heads = [(it * together + n, p) for n in range(together) for p in range(PAIRS)]
        lanes = lambda part, p: slice(part * MODEL + p * 128, part * MODEL + (p + 1) * 128)
        qs = [qkv_ref[w, :, lanes(0, p)] for w, p in heads]
        us = [mm(mix_ref[...], jnp.concatenate([q, q], axis=1), NT) for q in qs]
        qts = [(q.T * SCALE).astype(BF16) for q in qs]
        vts = [qkv_ref[w, :, lanes(2, p)].T for w, p in heads]
        row = lax.broadcasted_iota(jnp.int32, (16, 1), 0)
        qas = []
        for (w, p), u, qt in zip(heads, us, qts):
            tabs = []
            for t in range(2):
                a = u[64 * t:64 * t + 64]
                for n, b in enumerate((8, 4, 2, 1)):
                    cond = shift_ref[4 * t + n:4 * t + n + 1, :] > 0
                    a = jnp.where(cond, pltpu.roll(a, 64 - b, 0), a)
                tabs.append(a)
            parts = [qt]
            for h in range(2):
                ah = jnp.where(row == 14, 1.0, tabs[0][32 * h:32 * h + 16])
                aw = tabs[1][32 * h:32 * h + 16]
                hh, hl = split(ah)
                wh, wl = split(aw)
                parts += [hh, wh, hl, wl]
            qa = jnp.concatenate(parts, axis=0)
            qaug_ref[w, p] = qa
            qas.append(qa)
        keys = [key_side(qkv_ref[w, :, lanes(1, p)], ohm_ref[w]) for w, p in heads]
        scores = [mm(key, query_side(qa, h)) for key, qa in zip(keys, qas) for h in range(2)]
        ots = []
        for n, s in enumerate(scores):
            (w, p), h = heads[n // 2], n % 2
            top = jnp.max(s, axis=0, keepdims=True)
            e = jnp.exp(s - top)
            total = jnp.sum(e, axis=0, keepdims=True)
            lse_ref[w, p, h:h + 1, :] = top + jnp.log(total)
            ots.append(mm(vts[n // 2][64 * h:64 * h + 64], e.astype(BF16)) * (1.0 / total))
        for n, (w, p) in enumerate(heads):
            ot = jnp.concatenate(ots[2 * n:2 * n + 2], axis=0).astype(BF16)
            o_ref[w, :, lanes(0, p)] = ot.T

    wide[0:rows, :] = mm(o_ref[0:live].reshape(rows, MODEL), wproj_ref[...]) + vec_ref[PROJ_BIAS]
    for w in range(live):
        here = slice(AREA * w, AREA * (w + 1))
        x1_ref[here, :] = x_ref[here, :].astype(F32) + wide[PADDED * w:PADDED * w + AREA, :]


def cost(us):
    return pl.CostEstimate(flops=int(us * 1.0e9), bytes_accessed=1 << 20, transcendentals=0)


def once(a):
    return pl.BlockSpec(a.shape, lambda i: (0,) * a.ndim, pipeline_mode=pl.Buffered(1))


def blocked(*shape):
    return pl.BlockSpec(shape, lambda i: (i,) + (0,) * (len(shape) - 1))


def block_windows(windows):
    return 4 if windows % 4 == 0 else windows


def attention_forward(x, go, ohm, vec, wqkv, mix, shift, wproj, windows, at, count, live, held):
    wb = block_windows(windows)
    outs = [((windows * AREA, MODEL), F32, (wb * AREA, MODEL)),
            ((windows, PADDED, MODEL), BF16, (wb, PADDED, MODEL)),
            ((windows, PADDED, 3 * MODEL), BF16, (wb, PADDED, 3 * MODEL)),
            ((windows, PAIRS, 256, PADDED), BF16, (wb, PAIRS, 256, PADDED)),
            ((windows, PADDED, MODEL), BF16, (wb, PADDED, MODEL)),
            ((windows, PAIRS, 2, PADDED), F32, (wb, PAIRS, 2, PADDED)),
            ((windows * AREA, 1), F32, (wb * AREA, 1)),
            ((windows * AREA, MODEL), BF16, (wb * AREA, MODEL))]
    part = lambda *shape: pl.BlockSpec(shape, lambda i: (i + at,) + (0,) * (len(shape) - 1))
    extra = list(held or [])
    return pl.pallas_call(
        functools.partial(forward_kernel, live),
        grid=(count,),
        in_specs=[blocked(live * AREA, MODEL), blocked(live * AREA, MODEL), blocked(live, PADDED, 128)]
        + [once(a) for a in (vec, wqkv, mix, shift, wproj)] + [pl.BlockSpec(memory_space=pl.ANY)] * len(extra),
        out_specs=[part(*b) for _, _, b in outs],
        out_shape=[jax.ShapeDtypeStruct(s, t) for s, t, _ in outs],
        input_output_aliases={8 + n: n for n in range(len(extra))},
        scratch_shapes=[pltpu.VMEM((wb, PADDED, MODEL), BF16), pltpu.VMEM((wb * PADDED, MODEL), F32)],
        cost_estimate=cost(14 * count * live // wb),
        compiler_params=pltpu.CompilerParams(vmem_limit_bytes=VMEM_LIMIT, dimension_semantics=("arbitrary",)),
        name="attention_forward",
    )(x, go, ohm, vec, wqkv, mix, shift, wproj, *extra)


BLOCK = 384
BLOCKS = 4 * MODEL // BLOCK


def backward_kernel(live, core_ref, da_ref, ohm_ref, oht_ref, qkv_ref, qaug_ref, lse_ref, wproj_ref, relt_ref, shift_ref, xhat_ref, o_ref, vec_ref,
                    wqkv_ref, dp_ref, grel_ref, keep_ref, send_ref, sum_ref, gvec_ref, bvec_ref,
                    do_ref, dap_ref, turned, acc, wstage, dstage, wsems, dsems):
    wb = ohm_ref.shape[0]
    rows = wb * PADDED
    step = pl.program_id(0)

    @pl.when(step == 0)
    def _():
        grel_ref[...] = jnp.zeros_like(grel_ref)
        acc[...] = jnp.zeros_like(acc)
        turned[MODEL:, :] = jnp.ones((16, rows), BF16)

    for w in range(wb):
        dap_ref[w, PADDED - 16:, :] = jnp.zeros((16, MODEL), BF16)
        dap_ref[w, 0:AREA, :] = da_ref[AREA * w:AREA * (w + 1), :]
    final = step == pl.num_programs(0) - 1
    if live < wb:
        @pl.when(final)
        def _():
            dap_ref[live:] = jnp.zeros((wb - live, PADDED, MODEL), BF16)
            dp_ref[live:] = jnp.zeros((wb - live, PADDED, 3 * MODEL), BF16)

    def outer(count):
        n = count * PADDED
        dap = dap_ref[0:count].reshape(n, MODEL)
        do_ref[0:count] = mm(dap, wproj_ref[...], NT).astype(BF16).reshape(count, PADDED, MODEL)
        turned[0:MODEL, 0:n] = o_ref[0:count].reshape(n, MODEL).T
        acc[0:MODEL, 3 * MODEL:] += mm(turned[0:MODEL, 0:n], dap)

    def inner(count):
        n = count * PADDED
        turned[0:MODEL, 0:n] = xhat_ref[0:count].reshape(n, MODEL).T
        for j in range(3):
            cs = slice(j * MODEL, (j + 1) * MODEL)
            acc[:, cs] += mm(turned[:, 0:n], dp_ref[0:count, :, cs].reshape(n, MODEL))

    def either(run):
        if live == wb:
            run(wb)
        else:
            pl.when(final)(lambda: run(live))
            pl.when(jnp.logical_not(final))(lambda: run(wb))

    either(outer)
    together = 1

    @pl.loop(0, jnp.where(final, live, wb) // together)
    def _(it):
        heads = [(it * together + n, p) for n in range(together) for p in range(PAIRS)]
        lanes = lambda part, p: slice(part * MODEL + p * 128, part * MODEL + (p + 1) * 128)
        both = [(n, w, p, h) for n, (w, p) in enumerate(heads) for h in range(2)]
        qs = [qkv_ref[w, :, lanes(0, p)] for w, p in heads]
        ks = [qkv_ref[w, :, lanes(1, p)] for w, p in heads]
        vs = [qkv_ref[w, :, lanes(2, p)] for w, p in heads]
        dos = [do_ref[w, :, lanes(0, p)] for w, p in heads]
        scores = [mm(key_side(ks[n], ohm_ref[w]), query_side(qaug_ref[w, p], h)) for n, w, p, h in both]
        dots = [do.T for do in dos]
        kts = [(k.T * SCALE).astype(BF16) for k in ks]
        z = jnp.zeros((HEAD_DIM, PADDED), BF16)
        dws = []
        for n, w, p, h in both:
            own = dots[n][64 * h:64 * h + 64]
            dws.append(mm(vs[n], jnp.concatenate([own, z] if h == 0 else [z, own], axis=0)))
        dvs, dks, dqs = [], [], []
        for s, dw, (n, w, p, h) in zip(scores, dws, both):
            a = jnp.exp(s - lse_ref[w, p, h:h + 1, :])
            t = a * dw
            dsb = (t - a * jnp.sum(t, axis=0, keepdims=True)).astype(BF16)
            dvs.append(mm(dots[n][64 * h:64 * h + 64], a.astype(BF16), NT))
            dks.append(mm(qaug_ref[w, p, 64 * h:64 * h + 64, :], dsb, NT))
            dqs.append(mm(jnp.concatenate([kts[n][64 * h:64 * h + 64], oht_ref[...]], axis=0), dsb))
        zz = jnp.zeros((16, PADDED), F32)
        dqts = []
        for n, (w, p) in enumerate(heads):
            tabs = []
            for t in range(2):
                lo = 64 + 16 * t
                a = jnp.concatenate([dqs[2 * n][lo:lo + 16], zz, dqs[2 * n + 1][lo:lo + 16], zz], axis=0)
                for i, b in enumerate((8, 4, 2, 1)):
                    cond = shift_ref[4 * t + i:4 * t + i + 1, :] > 0
                    a = jnp.where(cond, pltpu.roll(a, b, 0), a)
                tabs.append(a.astype(BF16))
            dqt = []
            for h in range(2):
                du = jnp.concatenate([tabs[0][32 * h:32 * h + 32], tabs[1][32 * h:32 * h + 32]], axis=0)
                dqt.append(dqs[2 * n + h][0:64] + mm(relt_ref[...], jnp.concatenate([du, du], axis=0)))
                grel_ref[h] += mm(du, qs[n])
            dqts.append(jnp.concatenate(dqt, axis=0).astype(BF16))
        for n, (w, p) in enumerate(heads):
            dp_ref[w, :, lanes(0, p)] = dqts[n].T
            dp_ref[w, :, lanes(1, p)] = jnp.concatenate(dks[2 * n:2 * n + 2], axis=0).astype(BF16).T
            dp_ref[w, :, lanes(2, p)] = jnp.concatenate(dvs[2 * n:2 * n + 2], axis=0).astype(BF16).T

    either(inner)

    @pl.when(final)
    def _():
        columns = jnp.concatenate([vec_ref[...]] * 16, axis=0).T
        gain, bias = columns[:, 0:1], columns[:, 1:2]
        nq = 3 * MODEL // BLOCK
        sum_ref[...] = acc[MODEL:MODEL + 8, 0:3 * MODEL]
        gsum, bsum = jnp.zeros((MODEL, 128), F32), jnp.zeros((MODEL, 128), F32)
        take = lambda n: pltpu.make_async_copy(wqkv_ref.at[:, pl.ds(n * BLOCK, BLOCK)], wstage.at[n % 2], wsems.at[n % 2])
        core = core_ref[0]

        def give(n, act):
            for k, to, c in ((0, keep_ref, core), (1, send_ref, 1 - core)):
                act(pltpu.make_async_copy(dstage.at[n % 2, :, c], to.at[n], dsems.at[n % 2, k]))
        start, wait = (lambda cp: cp.start()), (lambda cp: cp.wait())
        take(0).start()
        for n in range(BLOCKS):
            cs = slice(n * BLOCK, (n + 1) * BLOCK)
            if n + 1 < nq:
                take(n + 1).start()
            if n >= 2:
                give(n - 2, wait)
            m = acc[0:MODEL, cs]
            if n < nq:
                s = acc[MODEL:MODEL + 1, cs]
                take(n).wait()
                w = wstage[n % 2].astype(F32)
                g, b = w * m, w * s
                gsum += sum(g[:, 128 * i:128 * (i + 1)] for i in range(BLOCK // 128))
                bsum += sum(b[:, 128 * i:128 * (i + 1)] for i in range(BLOCK // 128))
                m = m * gain + bias * s
            dstage[n % 2] = m.astype(BF16).reshape(dstage.shape[1:])
            give(n, start)
        gvec_ref[...] = jnp.broadcast_to(jnp.sum(gsum.T, axis=0, keepdims=True), gvec_ref.shape)
        bvec_ref[...] = jnp.broadcast_to(jnp.sum(bsum.T, axis=0, keepdims=True), bvec_ref.shape)
        give(BLOCKS - 2, wait)
        give(BLOCKS - 1, wait)


def attention_backward(da, ohm, oht, qkv, qaug, lse, wproj, relt, shift, xhat, o, vec, wqkv, core, dp_size, live):
    windows = ohm.shape[0]
    wb = block_windows(windows)
    block = lambda *shape: pl.BlockSpec(shape, lambda i, _: (i,) + (0,) * (len(shape) - 1))
    whole = lambda a: pl.BlockSpec(a.shape, lambda i, _: (0,) * a.ndim, pipeline_mode=pl.Buffered(1))
    row = MODEL // dp_size
    fixed = lambda *shape: pl.BlockSpec(shape, lambda i, _: (0,) * len(shape))
    anywhere = pl.BlockSpec(memory_space=pl.ANY)
    return pl.pallas_call(
        functools.partial(backward_kernel, live),
        grid_spec=pltpu.PrefetchScalarGridSpec(
            num_scalar_prefetch=1,
            grid=(windows // wb,),
            in_specs=[block(wb * AREA, MODEL), block(wb, PADDED, 128), whole(oht), block(wb, PADDED, 3 * MODEL),
                  block(wb, PAIRS, 256, PADDED), block(wb, PAIRS, 2, PADDED), whole(wproj), whole(relt), whole(shift),
                  block(wb, PADDED, MODEL), block(wb, PADDED, MODEL), whole(vec), anywhere],
        out_specs=[block(wb, PADDED, 3 * MODEL), fixed(2, 64, 128), anywhere, anywhere, fixed(8, 3 * MODEL), fixed(8, MODEL), fixed(8, MODEL)],
        scratch_shapes=[pltpu.VMEM((wb, PADDED, MODEL), BF16), pltpu.VMEM((wb, PADDED, MODEL), BF16),
                        pltpu.VMEM((MODEL + 16, wb * PADDED), BF16), pltpu.VMEM((MODEL + 16, 4 * MODEL), F32),
                        pltpu.VMEM((2, MODEL, BLOCK), BF16), pltpu.VMEM((2, dp_size // 2, 2, row, BLOCK), BF16),
                        pltpu.SemaphoreType.DMA((2,)), pltpu.SemaphoreType.DMA((2, 2))]),
        out_shape=[jax.ShapeDtypeStruct((windows, PADDED, 3 * MODEL), BF16), jax.ShapeDtypeStruct((2, 64, 128), F32),
                   jax.ShapeDtypeStruct((BLOCKS, dp_size // 2, row, BLOCK), BF16),
                   jax.ShapeDtypeStruct((BLOCKS, dp_size // 2, row, BLOCK), BF16), jax.ShapeDtypeStruct((8, 3 * MODEL), F32),
                   jax.ShapeDtypeStruct((8, MODEL), F32), jax.ShapeDtypeStruct((8, MODEL), F32)],
        cost_estimate=cost(95),
        compiler_params=pltpu.CompilerParams(vmem_limit_bytes=VMEM_LIMIT, dimension_semantics=("arbitrary",)),
        name="attention_backward",
    )(core, da, ohm, oht, qkv, qaug, lse, wproj, relt, shift, xhat, o, vec, wqkv)


def input_kernel(live, x_ref, da_ref, dp_ref, vec_ref, wqkv_ref, *rest):
    gx_ref, wide, tall = rest[-3:]
    wide[0:live * PADDED, :] = mm(dp_ref[0:live].reshape(live * PADDED, 3 * MODEL), wqkv_ref[...], NT)
    for w in range(live):
        tall[AREA * w:AREA * (w + 1), :] = wide[PADDED * w:PADDED * w + AREA, :]
    rows = live * AREA
    for lo in range(0, rows, 112):
        hi = min(lo + 112, rows)
        c, r = norm(x_ref[lo:hi, :].astype(F32))
        xhat = c * r
        dx = tall[lo:hi, :] * vec_ref[LN1_GAIN]
        dx = r * (dx - jnp.mean(dx, axis=-1, keepdims=True) - xhat * jnp.mean(dx * xhat, axis=-1, keepdims=True))
        gx_ref[lo:hi, :] = (dx + da_ref[lo:hi, :].astype(F32)).astype(BF16)


def input_gradient(x, da, dp, vec, wqkv, at, count, x_at, live, held):
    windows = dp.shape[0]
    wb = block_windows(windows)
    part = lambda *shape: pl.BlockSpec(shape, lambda i: (i + at,) + (0,) * (len(shape) - 1))
    extra = [] if held is None else [held]
    return pl.pallas_call(
        functools.partial(input_kernel, live),
        grid=(count,),
        in_specs=[pl.BlockSpec((live * AREA, MODEL), lambda i: (i + x_at, 0)), part(wb * AREA, MODEL), part(wb, PADDED, 3 * MODEL),
                  once(vec), once(wqkv)] + [pl.BlockSpec(memory_space=pl.ANY)] * len(extra),
        out_specs=part(wb * AREA, MODEL),
        out_shape=jax.ShapeDtypeStruct((windows * AREA, MODEL), BF16),
        input_output_aliases={5: 0} if extra else {},
        scratch_shapes=[pltpu.VMEM((wb * PADDED, MODEL), F32), pltpu.VMEM((wb * AREA, MODEL), F32)],
        cost_estimate=cost(6 * count),
        compiler_params=pltpu.CompilerParams(vmem_limit_bytes=VMEM_LIMIT, dimension_semantics=("arbitrary",)),
        name="input_gradient",
    )(x, da, dp, vec, wqkv, *extra)


def constant_tables():
    place = np.arange(PADDED)
    real = place < AREA
    r, c = np.where(real, place // WIN, 0), np.where(real, place % WIN, 0)
    hot = [((WIN - 1 - v)[:, None] == np.arange(16)) & real[:, None] for v in (r, c)]
    keys = np.concatenate(hot + hot, axis=1).astype(np.float32)
    shift = np.stack([(v >> b) & 1 for v in (r, c) for b in (3, 2, 1, 0)]).astype(np.int32)
    return keys, np.concatenate(hot, axis=1).T.astype(np.float32), shift


def key_tables(window_extent):
    keys = constant_tables()[0]
    place = np.arange(PADDED)
    r, c = place // WIN, place % WIN
    valid = (r < window_extent[:, 0:1]) & (c < window_extent[:, 1:2]) & (place < AREA)
    keys = np.concatenate([keys, np.zeros((PADDED, 64), np.float32)], axis=1)
    flag = np.arange(128) == 14
    return jnp.where(flag[None, None, :], jnp.where(valid, 0.0, NEGATIVE)[:, :, None], keys[None]).astype(BF16)


def small_tables(rel_h, rel_w):
    _, oht, shift = constant_tables()
    both = jnp.pad(jnp.stack([rel_h, rel_w]), ((0, 0), (0, 5), (0, 0)))
    hi = both.astype(BF16).astype(F32)
    lo = both - hi
    parity = np.eye(2, dtype=np.float32)
    spread = lambda t: (t[:, None, :, None, :] * parity[None, :, None, :, None]).reshape(128, 128)
    mix = jnp.concatenate([spread(hi), spread(lo)], axis=1).astype(BF16)
    relt = jnp.concatenate([hi.reshape(64, HEAD_DIM), lo.reshape(64, HEAD_DIM)], axis=0).T.astype(BF16)
    return jnp.asarray(oht, BF16), jnp.asarray(shift), mix, relt


def gelu_parts(z):
    u = jnp.abs(z)
    t = 1.0 / (1.0 + 0.23164189 * u)
    e = jnp.exp2(z * (z * -0.72134752))
    poly = t * (0.127414796 + t * (-0.142248368 + t * (0.7107068705 + t * (-0.7265760135 + t * 0.5307027145))))
    q = poly * e
    phi = jnp.where(z >= 0.0, 1.0 - q, q)
    return z * phi, phi + z * e * 0.3989422804


ROWS = 512
CHUNK = 768
SLICES = 4


def mlp_kernel(rows, widths, offset_ref, x1_ref, dy_ref, mask_ref, par_ref, upb_ref, *rest):
    n = len(widths)
    ups, downs = rest[:n], rest[n:2 * n]
    out_ref, da_ref, dw_ref, dbu_ref, vec_ref, h2, dm, h2t, dmt, macc, dacc, accu, accd, zs, das, gs, dzs, stage, sems = rest[2 * n:]
    rb = h2.shape[0]
    ch = 512
    step = pl.program_id(0)

    @pl.when(step == 0)
    def _():
        accu[...] = jnp.zeros_like(accu)
        accd[...] = jnp.zeros_like(accd)
        h2t[MODEL:, :] = jnp.ones((16, h2t.shape[1]), BF16)
        vec_ref[...] = jnp.zeros_like(vec_ref)

    def live(i):
        row = step * rb + i * ch + lax.broadcasted_iota(jnp.int32, (ch, 1), 0)
        return row < rows

    @pl.loop(0, rb // ch)
    def _(i):
        rs = pl.ds(pl.multiple_of(i * ch, ch), ch)
        x1 = jnp.where(live(i), x1_ref[rs, :], 0.0)
        c, r = norm(x1)
        h2[rs, :] = (c * r * par_ref[LN2_GAIN] + par_ref[LN2_BIAS]).astype(BF16)
        d = jnp.where(live(i), dy_ref[rs, :].astype(F32), 0.0)
        dm[rs, :] = d.astype(BF16)
        vec_ref[0:8, :] += fold8(d)

    h2t[0:MODEL, :] = h2[...].T
    dmt[...] = dm[...].T

    chunks, at = [], 0
    for up_ref, down_ref, width in zip(ups, downs, widths):
        size = min(CHUNK, width)
        for lo in range(0, width, size):
            chunks.append((up_ref, down_ref, slice(lo, lo + size), slice(at, at + size)))
            at += size
    count, part = len(chunks), rb // SLICES

    def products(u):
        up_ref, down_ref, here, there = chunks[u // SLICES]
        rs = slice(u % SLICES * part, (u % SLICES + 1) * part)
        zs[u % 2] = mm(h2[rs, :], up_ref[:, here])
        das[u % 2] = mm(dm[rs, :], down_ref[:, here])

    def activate(u):
        there = chunks[u // SLICES][3]
        rs = slice(u % SLICES * part, (u % SLICES + 1) * part)
        g, gp = gelu_parts(zs[u % 2] + upb_ref[:, there])
        dz = (das[u % 2] * gp).astype(BF16)
        gs[u // SLICES % 2, rs, :] = g.astype(BF16)
        dzs[u // SLICES % 2, rs, :] = dz

    def consume(j, i):
        up_ref, down_ref, here, there = chunks[j]
        g, dz = gs.at[j % 2], dzs.at[j % 2]
        if i == 0:
            m = mm(g[...], down_ref[:, here], NT)
            macc[...] = m if j == 0 else macc[...] + m
        if i == 1:
            d = mm(dz[...], up_ref[:, here], NT)
            dacc[...] = d if j == 0 else dacc[...] + d
        if i == 2:
            accd[:, there] += mm(dmt[...], g[...])
        if i == 3:
            accu[:, there] += mm(h2t[...], dz[...])

    units = count * SLICES
    per = 4 // SLICES
    products(0)
    for u in range(units + SLICES):
        if u + 1 < units:
            products(u + 1)
        if u >= SLICES:
            for k in range(per):
                consume(u // SLICES - 1, u % SLICES * per + k)
        if u < units:
            activate(u)

    @pl.loop(0, rb // ch)
    def _(i):
        rs = pl.ds(pl.multiple_of(i * ch, ch), ch)
        x1 = jnp.where(live(i), x1_ref[rs, :], 0.0)
        c, r = norm(x1)
        xhat = c * r
        valid = live(i) & (mask_ref[rs, :] > 0.0)
        out_ref[rs, :] = jnp.where(valid, x1 + macc[rs, :] + par_ref[DOWN_BIAS], 0.0).astype(BF16)
        dh = dacc[rs, :]
        vec_ref[8:16, :] += fold8(dh * xhat)
        vec_ref[16:24, :] += fold8(dh)
        dx = dh * par_ref[LN2_GAIN]
        dx = r * (dx - jnp.mean(dx, axis=-1, keepdims=True) - xhat * jnp.mean(dx * xhat, axis=-1, keepdims=True))
        da = (dx + dm[rs, :].astype(F32)).astype(BF16)
        da_ref[rs, :] = da
        vec_ref[24:32, :] += fold8(da.astype(F32))

    @pl.when(step == pl.num_programs(0) - 1)
    def _():
        size = stage.shape[2]
        dbu_ref[...] = accu[MODEL:MODEL + 8, :]
        each = accu.shape[1] // size

        def copy(k):
            to = pl.multiple_of(offset_ref[k], 128)
            return pltpu.make_async_copy(stage.at[k % 2], dw_ref.at[:, pl.ds(to, size)], sems.at[k % 2])
        for k in range(2 * each):
            if k >= 2:
                copy(k - 2).wait()
            src = (accu, accd)[k // each]
            stage[k % 2] = src[0:MODEL, (k % each) * size:(k % each + 1) * size].astype(BF16)
            copy(k).start()
        copy(2 * each - 2).wait()
        copy(2 * each - 1).wait()


def mlp(x1, dy, mask, par, upb, ups, downs, offsets, live_rows):
    rows, d = x1.shape
    widths = tuple(u.shape[1] for u in ups)
    ff = sum(widths)
    size = 2 * ff // offsets.shape[0]
    rb = ROWS
    full = lambda a: pl.BlockSpec(a.shape, lambda i, _: (0, 0), pipeline_mode=pl.Buffered(1))
    rowspec = lambda w: pl.BlockSpec((rb, w), lambda i, _: (i, 0))
    return pl.pallas_call(
        functools.partial(mlp_kernel, live_rows, widths),
        grid_spec=pltpu.PrefetchScalarGridSpec(
            num_scalar_prefetch=1,
            grid=(pl.cdiv(live_rows, rb),),
            in_specs=[rowspec(d), rowspec(d), rowspec(1)] + [full(a) for a in (par, upb, *ups, *downs)],
            out_specs=[rowspec(d), rowspec(d), pl.BlockSpec(memory_space=pl.ANY),
                       pl.BlockSpec((8, ff), lambda i, _: (0, 0)), pl.BlockSpec((32, d), lambda i, _: (0, 0))],
            scratch_shapes=[pltpu.VMEM((rb, d), BF16), pltpu.VMEM((rb, d), BF16), pltpu.VMEM((d + 16, rb), BF16), pltpu.VMEM((d, rb), BF16),
                            pltpu.VMEM((rb, d), F32), pltpu.VMEM((rb, d), F32), pltpu.VMEM((d + 16, ff), F32), pltpu.VMEM((d, ff), F32),
                            pltpu.VMEM((2, rb // SLICES, CHUNK), F32), pltpu.VMEM((2, rb // SLICES, CHUNK), F32),
                            pltpu.VMEM((2, rb, CHUNK), BF16), pltpu.VMEM((2, rb, CHUNK), BF16), pltpu.VMEM((2, d, size), BF16), pltpu.SemaphoreType.DMA((2,))]),
        out_shape=[jax.ShapeDtypeStruct((rows, d), BF16), jax.ShapeDtypeStruct((rows, d), BF16),
                   jax.ShapeDtypeStruct((d, 2 * ff), BF16), jax.ShapeDtypeStruct((8, ff), F32), jax.ShapeDtypeStruct((32, d), F32)],
        cost_estimate=cost(170),
        compiler_params=pltpu.CompilerParams(vmem_limit_bytes=VMEM_LIMIT, dimension_semantics=("arbitrary",)),
        name="mlp",
    )(offsets, x1, dy, mask, par, upb, *ups, *downs)


GROUP_WIN = 40
SPARE = 2


def bits(n):
    return n.bit_length() - 1


def swap(value, axis, bit, sizes):
    return lax.ppermute(value, axis, [(i, i ^ (1 << bit)) for i in range(sizes[axis])])


def bit_of(axis, bit):
    return (lax.axis_index(axis) >> bit) & 1


def add(a, b):
    return (a.astype(F32) + b.astype(F32)).astype(BF16)


def split_dp(held, at, bit):
    mine = bit_of("dp", bit)
    return tuple(lax.dynamic_index_in_dim(held, m, at, keepdims=False) for m in (mine, 1 - mine))


def split_mlp(held, owners, bit):
    mine = bit_of("mlp", bit) == 1
    sides = []
    for side in range(2):
        runs = [n for n, o in enumerate(owners) if (o >> bit) & 1 == side]
        sides.append(jnp.concatenate([held[n:n + 1] for n in runs], axis=0))
    return jnp.where(mine, sides[1], sides[0]), jnp.where(mine, sides[0], sides[1])


def reduce_steps(keep, send, owners, sizes):
    nb, nm = bits(sizes["dp"]), bits(sizes["mlp"])
    apart = lambda v: v.reshape((v.shape[0],) + (2,) * (nb - 1) + v.shape[2:])
    got = yield [("dp", 0, send)]
    held = apart(add(keep, got[0]))
    orders = ([("mlp", b) for b in reversed(range(nm))] + [("dp", 1)], [("dp", 1)] + [("mlp", b) for b in reversed(range(nm))])
    halves = [held[:, 0], held[:, 1]]
    left = [list(owners), list(owners)]
    dims = [nb - 2, nb - 2]
    plan = list(zip(*orders)) + [(("dp", b), ("dp", b)) for b in range(2, nb - 1)]
    for both in plan:
        kept, sends = [], []
        for n, (axis, bit) in enumerate(both):
            if axis == "mlp":
                keep, send = split_mlp(halves[n], left[n], bit)
                mine = [o for o in left[n] if (o >> bit) & 1 == 0]
                left[n] = [o & ~(1 << bit) for o in mine]
            else:
                keep, send = split_dp(halves[n], dims[n], bit)
                dims[n] -= 1
            kept.append(keep)
            sends.append((axis, bit, send))
        got = yield sends
        halves = [add(k, g) for k, g in zip(kept, got)]
    mine = bit_of("dp", nb - 1) == 1
    got = yield [("dp", nb - 1, jnp.where(mine, halves[0], halves[1]))]
    yield add(jnp.where(mine, halves[1], halves[0]), got[0])


def sum_steps(v, sizes):
    for axis in ("dp", "mlp"):
        for b in range(bits(sizes[axis])):
            got = yield [(axis, b, v)]
            v = v + got[0]
    yield v


def run_steps(tasks, delays, work, sizes):
    states = [next(t) if not d else None for t, d in zip(tasks, delays)]
    results = [None] * len(tasks)
    turn = 0
    while any(r is None for r in results):
        turn += 1
        sends = [(n, s) for n, state in enumerate(states) if isinstance(state, list) for s in state]
        values = work(turn, [s[2] for _, s in sends], [swap_by(s[0], s[1], sizes) for _, s in sends])
        for n, task in enumerate(tasks):
            if isinstance(states[n], list):
                states[n] = task.send([v for v, (owner, _) in zip(values, sends) if owner == n])
                if not isinstance(states[n], list):
                    results[n] = states[n]
            elif results[n] is None and turn >= delays[n]:
                states[n] = next(task)
    return results


def swap_by(axis, bit, sizes):
    return lambda v: swap(v, axis, bit, sizes)


def feed_forward_weights(up, up_bias, down, sizes):
    width = up.shape[1]
    if sizes["mlp"] != 2:
        gather = lambda v: lax.all_gather(v, "mlp", axis=v.ndim - 1, tiled=True)
        count = sizes["mlp"]
        return [gather(up)], [gather(down)], gather(up_bias), jnp.arange(count, dtype=jnp.int32) * width, width
    half = width // 2
    core, me = bit_of("dp", 0), lax.axis_index("mlp")
    cut = lambda v: jnp.where(core == 1, v[:, half:], v[:, :half])
    far_up, far_down = swap(cut(up), "mlp", 0, sizes), swap(cut(down), "mlp", 0, sizes)
    far_bias = swap(up_bias, "mlp", 0, sizes)
    bias = jnp.concatenate([up_bias, jnp.roll(far_bias, -core * half)])
    places = jnp.stack([me * width, me * width + half, (1 - me) * width + core * half, (1 - me) * width + (1 - core) * half])
    return (up, far_up), (down, far_down), bias, places.astype(jnp.int32), half


def per_device(
    sizes,
    tokens,
    window_extent,
    ln1_gain,
    ln1_bias,
    qkv_weight,
    query_bias,
    value_bias,
    rel_h,
    rel_w,
    proj_weight,
    proj_bias,
    ln2_gain,
    ln2_bias,
    up_weight,
    up_bias,
    down_weight,
    down_bias,
    grad_out,
):
    owners = sizes["mlp"]
    line = lambda v: v.reshape(1, -1)
    ups, downs, up_bias_here, places, piece = feed_forward_weights(up_weight, up_bias, down_weight, sizes)
    windows = window_extent.shape[0]
    wb = block_windows(windows)
    blocks = windows // wb
    me = lax.axis_index("mlp")
    share = owners == 2 and 2 * windows == GROUP_WIN
    live = wb - SPARE if share else wb
    live_rows = (windows - wb + live) * AREA
    near, far = (windows - wb) * AREA, (windows - SPARE) * AREA
    oht, shift, mix, relt = small_tables(rel_h, rel_w)
    par = jnp.stack([ln1_gain, ln1_bias, query_bias, value_bias, proj_bias, ln2_gain, ln2_bias, down_bias])
    ohm = key_tables(window_extent)
    weights = (par, qkv_weight, mix, shift, proj_weight)
    if share:
        def taken(v, here, there):
            other = lax.ppermute(v[there:], "mlp", [(0, 1)])
            return jnp.where(me == 0, v[here:here + other.shape[0]], other)
        tail_x, tail_go = taken(tokens, near, far), taken(grad_out, near, far)
        tail_extent = taken(window_extent.astype(F32), windows - wb, windows - SPARE).astype(jnp.int32)
        tail_ohm = key_tables(tail_extent)
        held = attention_forward(tokens, grad_out, ohm, *weights, windows, 0, blocks - 1, wb, None)
        held = attention_forward(tail_x, tail_go, tail_ohm, *weights, windows, blocks - 1, 1, live, held)
        ohm = jnp.concatenate([ohm[:windows - wb], jnp.pad(tail_ohm, ((0, SPARE), (0, 0), (0, 0)))], axis=0)
    else:
        tail_x = tokens
        held = attention_forward(tokens, grad_out, ohm, *weights, windows, 0, blocks, wb, None)
    x1, xhat, qkv, qaug, o, lse, row_mask, dy = held
    if owners == 2:
        (ups, downs, x1) = lax.optimization_barrier((ups, downs, x1))
        ups, downs = list(ups) + [swap(ups[1], "dp", 0, sizes)], list(downs) + [swap(downs[1], "dp", 0, sizes)]
    width = up_weight.shape[1]
    ff = width * owners
    by_owner = (places // width) * (2 * width) + places % width
    output, da, dw_mlp, up_sums, mid_sums = mlp(
        x1, dy, row_mask, par, line(up_bias_here), ups, downs, jnp.concatenate([by_owner, by_owner + width]), live_rows)

    def give_back(v):
        return lax.ppermute(v[near:live_rows], "mlp", [(1, 0)])

    def completed(v, other):
        tail = jnp.where(me == 0, jnp.concatenate([v[near:live_rows], other], axis=0), 0)
        return lax.dynamic_update_slice(v, tail, (near, 0))

    if share:
        output_tail, da = lax.optimization_barrier((output[near:live_rows], da))
        output_back = lax.ppermute(output_tail, "mlp", [(1, 0)])
    dw_mlp = lax.psum_scatter(dw_mlp, "dp", scatter_dimension=0, tiled=True)
    dw_mlp = lax.psum_scatter(dw_mlp, "mlp", scatter_dimension=1, tiled=True)
    dp_all, grel, dw_keep, dw_send, dp_sums, gain_sums, bias_sums = attention_backward(
        da, ohm, oht, qkv, qaug, lse, proj_weight, relt, shift, xhat, o, par, qkv_weight, bit_of("dp", 0).reshape(1).astype(jnp.int32), sizes["dp"], live)
    if share:
        output = completed(output, output_back)
    up_sum = up_sums[0].reshape(-1, piece)
    up_sum = sum(jnp.where(jnp.arange(ff) // piece == places[n] // piece, jnp.tile(up_sum[n], ff // piece), 0.0)
                 for n in range(ff // piece))
    block_owners = [0, 0, 0, 1, 1, 1, 0, 1]
    if owners != 2:
        def regroup(v):
            parts = [jnp.moveaxis(p, 0, 2) for p in (v[:6], v[6:])]
            parts = [p.reshape(p.shape[:2] + (owners, -1)) for p in parts]
            return jnp.moveaxis(jnp.concatenate(parts, axis=3), 2, 0)
        dw_keep, dw_send = regroup(dw_keep), regroup(dw_send)
        block_owners = list(range(owners))
    rel = grel[0, :, :HEAD_DIM] + grel[1, :, HEAD_DIM:]
    mid = jnp.sum(mid_sums.reshape(4, 8, MODEL), axis=1)
    sums = jnp.concatenate([gain_sums[0], bias_sums[0], dp_sums[0], rel.reshape(-1), mid.reshape(-1), up_sum])
    half = (blocks - 1) // 2
    order = [(blocks - 1, 1)] + [(at, n) for at, n in ((0, half), (half, blocks - 1 - half)) if n]
    held = {"gx": None, "da": da, "at": 0}

    def input_part():
        at, count = order[held["at"]]
        last = at == blocks - 1
        held["gx"] = input_gradient(tail_x if last else tokens, held["da"], dp_all, par, qkv_weight, at, count, 0 if share and last else at,
                                    live if last else wb, held["gx"])
        held["at"] += 1

    def work(turn, values, swaps):
        if held["at"] >= len(order):
            return [f(v) for f, v in zip(swaps, values)]
        values, held["da"] = lax.optimization_barrier((values, held["da"]))
        if share and turn == 3:
            held["back"] = give_back(held["gx"])
        got = [f(v) for f, v in zip(swaps, values)]
        input_part()
        got, held["gx"] = lax.optimization_barrier((got, held["gx"]))
        return got

    tasks = [reduce_steps(dw_keep, dw_send, block_owners, sizes), sum_steps(sums, sizes)]
    delays = [0, 0]
    results = run_steps(tasks, delays, work, sizes)
    late, sums = results[0].astype(F32), results[1]
    late = jnp.concatenate([late[n] for n in range(late.shape[0])], axis=1)
    while held["at"] < len(order):
        input_part()
    grad_tokens = held["gx"]
    if share:
        grad_tokens = completed(grad_tokens, held["back"])
    d = MODEL
    table = 2 * WIN - 1
    n_rel = 64 * HEAD_DIM
    rel = sums[5 * d:5 * d + n_rel].reshape(64, HEAD_DIM)
    mid = sums[5 * d + n_rel:]
    cols = 3 * MODEL // owners
    dw_mlp = dw_mlp.astype(F32)
    return (
        output,
        grad_tokens,
        sums[0:d],
        sums[d:2 * d],
        late[:, :cols],
        sums[2 * d:3 * d],
        sums[4 * d:5 * d],
        rel[0:table],
        rel[32:32 + table],
        late[:, cols:],
        mid[3 * d:4 * d],
        mid[d:2 * d],
        mid[2 * d:3 * d],
        dw_mlp[:, :width],
        mid[4 * d:],
        dw_mlp[:, width:],
        mid[0:d],
    )


def solution(mesh):
    rows = P(("dp", "mlp"), None)
    in_specs = (rows, rows, P(), P(), P(), P(), P(), P(), P(), P(), P(), P(), P(),
                P(None, "mlp"), P("mlp"), P(None, "mlp"), P(), rows)
    block = P("dp", "mlp")
    out_specs = (rows, rows, P(), P(), block, P(), P(), P(), P(), block, P(), P(), P(), block, P(), block, P())
    sizes = {name: mesh.shape[name] for name in ("dp", "mlp")}
    return jax.shard_map(
        functools.partial(per_device, sizes), mesh=mesh, in_specs=in_specs, out_specs=out_specs, check_vma=False)
```

```python
import functools
import jax
import jax.numpy as jnp
import numpy as np
from jax import lax
from jax.experimental import pallas as pl
from jax.experimental.pallas import tpu as pltpu
from jax.sharding import PartitionSpec as P

HEADS = 12
HEAD_DIM = 64
WIN = 14
AREA = WIN * WIN
PADDED = 208
PAIRS = HEADS // 2
MODEL = HEADS * HEAD_DIM
EPSILON = 1e-6
NEGATIVE = -1e30
SCALE = HEAD_DIM ** -0.5
F32 = jnp.float32
BF16 = jnp.bfloat16
NN = (((1,), (0,)), ((), ()))
NT = (((1,), (1,)), ((), ()))
TN = (((0,), (0,)), ((), ()))
LN1_GAIN, LN1_BIAS, QUERY_BIAS, VALUE_BIAS, PROJ_BIAS, LN2_GAIN, LN2_BIAS, DOWN_BIAS = (slice(n, n + 1) for n in range(8))
VMEM_LIMIT = 60 * 1024 * 1024


def mm(a, b, dims=NN):
    return lax.dot_general(a, b, dims, preferred_element_type=F32)


def fold8(v):
    return jnp.sum(v.reshape(v.shape[0] // 8, 8, v.shape[1]), axis=0)


def norm(v):
    mu = jnp.mean(v, axis=-1, keepdims=True)
    c = v - mu
    return c, lax.rsqrt(jnp.mean(c * c, axis=-1, keepdims=True) + EPSILON)


def eye(n, value=1.0):
    r = lax.broadcasted_iota(jnp.int32, (n, n), 0)
    c = lax.broadcasted_iota(jnp.int32, (n, n), 1)
    return jnp.where(r == c, value, 0.0).astype(BF16)


def skew_bits(which):
    lane = lax.broadcasted_iota(jnp.int32, (1, PADDED), 1)
    r = lane // WIN
    return WIN - 1 - (jnp.minimum(r, WIN - 1) if which == 0 else lane - r * WIN)


def split(v):
    hi = v.astype(BF16)
    return hi, (v - hi.astype(F32)).astype(BF16)


def key_side(k, ohm):
    return jnp.concatenate([k, ohm], axis=1)


def query_side(qa, h):
    z = jnp.zeros((HEAD_DIM, PADDED), BF16)
    own = qa[h * 64:(h + 1) * 64]
    bias = qa[128 + 64 * h:192 + 64 * h]
    return jnp.concatenate(([own, z] if h == 0 else [z, own]) + [bias, z], axis=0)


def forward_kernel(live, x_ref, go_ref, ohm_ref, vec_ref, wqkv_ref, mix_ref, shift_ref, wproj_ref, *rest):
    x1_ref, xhat_ref, qkv_ref, qaug_ref, o_ref, lse_ref, mask_ref, dm_ref, h1_ref, wide = rest[-10:]
    rows = live * PADDED
    for w in range(live):
        here = slice(AREA * w, AREA * (w + 1))
        c, r = norm(x_ref[here, :].astype(F32))
        xhat = c * r
        valid = jnp.where(ohm_ref[w, 0:AREA, 14:15] < 0.0, 0.0, 1.0)
        h1_ref[w, PADDED - 16:, :] = jnp.zeros((16, MODEL), BF16)
        xhat_ref[w, PADDED - 16:, :] = jnp.zeros((16, MODEL), BF16)
        h1_ref[w, 0:AREA, :] = (xhat * vec_ref[LN1_GAIN] + vec_ref[LN1_BIAS]).astype(BF16)
        xhat_ref[w, 0:AREA, :] = xhat.astype(BF16)
        mask_ref[here, :] = valid
        dm_ref[here, :] = (go_ref[here, :].astype(F32) * valid).astype(BF16)
    for w in range(live, xhat_ref.shape[0]):
        xhat_ref[w] = jnp.zeros((PADDED, MODEL), BF16)
        o_ref[w] = jnp.zeros((PADDED, MODEL), BF16)

    for j, offset in enumerate((QUERY_BIAS, None, VALUE_BIAS)):
        cs = slice(j * MODEL, (j + 1) * MODEL)
        p = mm(h1_ref[0:live].reshape(rows, MODEL), wqkv_ref[:, cs])
        p = p if offset is None else p + vec_ref[offset]
        qkv_ref[0:live, :, cs] = p.astype(BF16).reshape(live, PADDED, MODEL)

    together = 4 if live % 4 == 0 else 1

    @pl.loop(0, live // together)
    def _(it):
        heads = [(it * together + n, p) for n in range(together) for p in range(PAIRS)]
        lanes = lambda part, p: slice(part * MODEL + p * 128, part * MODEL + (p + 1) * 128)
        qs = [qkv_ref[w, :, lanes(0, p)] for w, p in heads]
        us = [mm(mix_ref[...], jnp.concatenate([q, q], axis=1), NT) for q in qs]
        qts = [(q.T * SCALE).astype(BF16) for q in qs]
        vts = [qkv_ref[w, :, lanes(2, p)].T for w, p in heads]
        row = lax.broadcasted_iota(jnp.int32, (16, 1), 0)
        qas = []
        for (w, p), u, qt in zip(heads, us, qts):
            tabs = []
            for t in range(2):
                a = u[64 * t:64 * t + 64]
                for n, b in enumerate((8, 4, 2, 1)):
                    cond = shift_ref[4 * t + n:4 * t + n + 1, :] > 0
                    a = jnp.where(cond, pltpu.roll(a, 64 - b, 0), a)
                tabs.append(a)
            parts = [qt]
            for h in range(2):
                ah = jnp.where(row == 14, 1.0, tabs[0][32 * h:32 * h + 16])
                aw = tabs[1][32 * h:32 * h + 16]
                hh, hl = split(ah)
                wh, wl = split(aw)
                parts += [hh, wh, hl, wl]
            qa = jnp.concatenate(parts, axis=0)
            qaug_ref[w, p] = qa
            qas.append(qa)
        keys = [key_side(qkv_ref[w, :, lanes(1, p)], ohm_ref[w]) for w, p in heads]
        scores = [mm(key, query_side(qa, h)) for key, qa in zip(keys, qas) for h in range(2)]
        ots = []
        for n, s in enumerate(scores):
            (w, p), h = heads[n // 2], n % 2
            top = jnp.max(s, axis=0, keepdims=True)
            e = jnp.exp(s - top)
            total = jnp.sum(e, axis=0, keepdims=True)
            lse_ref[w, p, h:h + 1, :] = top + jnp.log(total)
            ots.append(mm(vts[n // 2][64 * h:64 * h + 64], e.astype(BF16)) * (1.0 / total))
        for n, (w, p) in enumerate(heads):
            ot = jnp.concatenate(ots[2 * n:2 * n + 2], axis=0).astype(BF16)
            o_ref[w, :, lanes(0, p)] = ot.T

    wide[0:rows, :] = mm(o_ref[0:live].reshape(rows, MODEL), wproj_ref[...]) + vec_ref[PROJ_BIAS]
    for w in range(live):
        here = slice(AREA * w, AREA * (w + 1))
        x1_ref[here, :] = x_ref[here, :].astype(F32) + wide[PADDED * w:PADDED * w + AREA, :]


def cost(us):
    return pl.CostEstimate(flops=int(us * 1.0e9), bytes_accessed=1 << 20, transcendentals=0)


def once(a):
    return pl.BlockSpec(a.shape, lambda i: (0,) * a.ndim, pipeline_mode=pl.Buffered(1))


def blocked(*shape):
    return pl.BlockSpec(shape, lambda i: (i,) + (0,) * (len(shape) - 1))


def block_windows(windows):
    return 4 if windows % 4 == 0 else windows


def attention_forward(x, go, ohm, vec, wqkv, mix, shift, wproj, windows, at, count, live, held):
    wb = block_windows(windows)
    outs = [((windows * AREA, MODEL), F32, (wb * AREA, MODEL)),
            ((windows, PADDED, MODEL), BF16, (wb, PADDED, MODEL)),
            ((windows, PADDED, 3 * MODEL), BF16, (wb, PADDED, 3 * MODEL)),
            ((windows, PAIRS, 256, PADDED), BF16, (wb, PAIRS, 256, PADDED)),
            ((windows, PADDED, MODEL), BF16, (wb, PADDED, MODEL)),
            ((windows, PAIRS, 2, PADDED), F32, (wb, PAIRS, 2, PADDED)),
            ((windows * AREA, 1), F32, (wb * AREA, 1)),
            ((windows * AREA, MODEL), BF16, (wb * AREA, MODEL))]
    part = lambda *shape: pl.BlockSpec(shape, lambda i: (i + at,) + (0,) * (len(shape) - 1))
    extra = list(held or [])
    return pl.pallas_call(
        functools.partial(forward_kernel, live),
        grid=(count,),
        in_specs=[blocked(live * AREA, MODEL), blocked(live * AREA, MODEL), blocked(live, PADDED, 128)]
        + [once(a) for a in (vec, wqkv, mix, shift, wproj)] + [pl.BlockSpec(memory_space=pl.ANY)] * len(extra),
        out_specs=[part(*b) for _, _, b in outs],
        out_shape=[jax.ShapeDtypeStruct(s, t) for s, t, _ in outs],
        input_output_aliases={8 + n: n for n in range(len(extra))},
        scratch_shapes=[pltpu.VMEM((wb, PADDED, MODEL), BF16), pltpu.VMEM((wb * PADDED, MODEL), F32)],
        cost_estimate=cost(14 * count * live // wb),
        compiler_params=pltpu.CompilerParams(vmem_limit_bytes=VMEM_LIMIT, dimension_semantics=("arbitrary",)),
        name="attention_forward",
    )(x, go, ohm, vec, wqkv, mix, shift, wproj, *extra)


BLOCK = 384
BLOCKS = 4 * MODEL // BLOCK


def backward_kernel(live, core_ref, da_ref, ohm_ref, oht_ref, qkv_ref, qaug_ref, lse_ref, wproj_ref, relt_ref, shift_ref, xhat_ref, o_ref, vec_ref,
                    wqkv_ref, dp_ref, grel_ref, keep_ref, send_ref, sum_ref, gvec_ref, bvec_ref,
                    do_ref, dap_ref, turned, acc, wstage, dstage, wsems, dsems):
    wb = ohm_ref.shape[0]
    rows = wb * PADDED
    step = pl.program_id(0)

    @pl.when(step == 0)
    def _():
        grel_ref[...] = jnp.zeros_like(grel_ref)
        acc[...] = jnp.zeros_like(acc)
        turned[MODEL:, :] = jnp.ones((16, rows), BF16)

    for w in range(wb):
        dap_ref[w, PADDED - 16:, :] = jnp.zeros((16, MODEL), BF16)
        dap_ref[w, 0:AREA, :] = da_ref[AREA * w:AREA * (w + 1), :]
    final = step == pl.num_programs(0) - 1
    if live < wb:
        @pl.when(final)
        def _():
            dap_ref[live:] = jnp.zeros((wb - live, PADDED, MODEL), BF16)
            dp_ref[live:] = jnp.zeros((wb - live, PADDED, 3 * MODEL), BF16)

    def outer(count):
        n = count * PADDED
        dap = dap_ref[0:count].reshape(n, MODEL)
        do_ref[0:count] = mm(dap, wproj_ref[...], NT).astype(BF16).reshape(count, PADDED, MODEL)
        turned[0:MODEL, 0:n] = o_ref[0:count].reshape(n, MODEL).T
        acc[0:MODEL, 3 * MODEL:] += mm(turned[0:MODEL, 0:n], dap)

    def inner(count):
        n = count * PADDED
        turned[0:MODEL, 0:n] = xhat_ref[0:count].reshape(n, MODEL).T
        for j in range(3):
            cs = slice(j * MODEL, (j + 1) * MODEL)
            acc[:, cs] += mm(turned[:, 0:n], dp_ref[0:count, :, cs].reshape(n, MODEL))

    def either(run):
        if live == wb:
            run(wb)
        else:
            pl.when(final)(lambda: run(live))
            pl.when(jnp.logical_not(final))(lambda: run(wb))

    either(outer)
    together = 1

    @pl.loop(0, jnp.where(final, live, wb) // together)
    def _(it):
        heads = [(it * together + n, p) for n in range(together) for p in range(PAIRS)]
        lanes = lambda part, p: slice(part * MODEL + p * 128, part * MODEL + (p + 1) * 128)
        both = [(n, w, p, h) for n, (w, p) in enumerate(heads) for h in range(2)]
        qs = [qkv_ref[w, :, lanes(0, p)] for w, p in heads]
        ks = [qkv_ref[w, :, lanes(1, p)] for w, p in heads]
        vs = [qkv_ref[w, :, lanes(2, p)] for w, p in heads]
        dos = [do_ref[w, :, lanes(0, p)] for w, p in heads]
        scores = [mm(key_side(ks[n], ohm_ref[w]), query_side(qaug_ref[w, p], h)) for n, w, p, h in both]
        dots = [do.T for do in dos]
        kts = [(k.T * SCALE).astype(BF16) for k in ks]
        z = jnp.zeros((HEAD_DIM, PADDED), BF16)
        dws = []
        for n, w, p, h in both:
            own = dots[n][64 * h:64 * h + 64]
            dws.append(mm(vs[n], jnp.concatenate([own, z] if h == 0 else [z, own], axis=0)))
        dvs, dks, dqs = [], [], []
        for s, dw, (n, w, p, h) in zip(scores, dws, both):
            a = jnp.exp(s - lse_ref[w, p, h:h + 1, :])
            t = a * dw
            dsb = (t - a * jnp.sum(t, axis=0, keepdims=True)).astype(BF16)
            dvs.append(mm(dots[n][64 * h:64 * h + 64], a.astype(BF16), NT))
            dks.append(mm(qaug_ref[w, p, 64 * h:64 * h + 64, :], dsb, NT))
            dqs.append(mm(jnp.concatenate([kts[n][64 * h:64 * h + 64], oht_ref[...]], axis=0), dsb))
        zz = jnp.zeros((16, PADDED), F32)
        dqts = []
        for n, (w, p) in enumerate(heads):
            tabs = []
            for t in range(2):
                lo = 64 + 16 * t
                a = jnp.concatenate([dqs[2 * n][lo:lo + 16], zz, dqs[2 * n + 1][lo:lo + 16], zz], axis=0)
                for i, b in enumerate((8, 4, 2, 1)):
                    cond = shift_ref[4 * t + i:4 * t + i + 1, :] > 0
                    a = jnp.where(cond, pltpu.roll(a, b, 0), a)
                tabs.append(a.astype(BF16))
            dqt = []
            for h in range(2):
                du = jnp.concatenate([tabs[0][32 * h:32 * h + 32], tabs[1][32 * h:32 * h + 32]], axis=0)
                dqt.append(dqs[2 * n + h][0:64] + mm(relt_ref[...], jnp.concatenate([du, du], axis=0)))
                grel_ref[h] += mm(du, qs[n])
            dqts.append(jnp.concatenate(dqt, axis=0).astype(BF16))
        for n, (w, p) in enumerate(heads):
            dp_ref[w, :, lanes(0, p)] = dqts[n].T
            dp_ref[w, :, lanes(1, p)] = jnp.concatenate(dks[2 * n:2 * n + 2], axis=0).astype(BF16).T
            dp_ref[w, :, lanes(2, p)] = jnp.concatenate(dvs[2 * n:2 * n + 2], axis=0).astype(BF16).T

    either(inner)

    @pl.when(final)
    def _():
        columns = jnp.concatenate([vec_ref[...]] * 16, axis=0).T
        gain, bias = columns[:, 0:1], columns[:, 1:2]
        nq = 3 * MODEL // BLOCK
        sum_ref[...] = acc[MODEL:MODEL + 8, 0:3 * MODEL]
        gsum, bsum = jnp.zeros((MODEL, 128), F32), jnp.zeros((MODEL, 128), F32)
        take = lambda n: pltpu.make_async_copy(wqkv_ref.at[:, pl.ds(n * BLOCK, BLOCK)], wstage.at[n % 2], wsems.at[n % 2])
        core = core_ref[0]

        def give(n, act):
            for k, to, c in ((0, keep_ref, core), (1, send_ref, 1 - core)):
                act(pltpu.make_async_copy(dstage.at[n % 2, :, c], to.at[n], dsems.at[n % 2, k]))
        start, wait = (lambda cp: cp.start()), (lambda cp: cp.wait())
        take(0).start()
        for n in range(BLOCKS):
            cs = slice(n * BLOCK, (n + 1) * BLOCK)
            if n + 1 < nq:
                take(n + 1).start()
            if n >= 2:
                give(n - 2, wait)
            m = acc[0:MODEL, cs]
            if n < nq:
                s = acc[MODEL:MODEL + 1, cs]
                take(n).wait()
                w = wstage[n % 2].astype(F32)
                g, b = w * m, w * s
                gsum += sum(g[:, 128 * i:128 * (i + 1)] for i in range(BLOCK // 128))
                bsum += sum(b[:, 128 * i:128 * (i + 1)] for i in range(BLOCK // 128))
                m = m * gain + bias * s
            dstage[n % 2] = m.astype(BF16).reshape(dstage.shape[1:])
            give(n, start)
        gvec_ref[...] = jnp.broadcast_to(jnp.sum(gsum.T, axis=0, keepdims=True), gvec_ref.shape)
        bvec_ref[...] = jnp.broadcast_to(jnp.sum(bsum.T, axis=0, keepdims=True), bvec_ref.shape)
        give(BLOCKS - 2, wait)
        give(BLOCKS - 1, wait)


def attention_backward(da, ohm, oht, qkv, qaug, lse, wproj, relt, shift, xhat, o, vec, wqkv, core, dp_size, live):
    windows = ohm.shape[0]
    wb = block_windows(windows)
    block = lambda *shape: pl.BlockSpec(shape, lambda i, _: (i,) + (0,) * (len(shape) - 1))
    whole = lambda a: pl.BlockSpec(a.shape, lambda i, _: (0,) * a.ndim, pipeline_mode=pl.Buffered(1))
    row = MODEL // dp_size
    fixed = lambda *shape: pl.BlockSpec(shape, lambda i, _: (0,) * len(shape))
    anywhere = pl.BlockSpec(memory_space=pl.ANY)
    return pl.pallas_call(
        functools.partial(backward_kernel, live),
        grid_spec=pltpu.PrefetchScalarGridSpec(
            num_scalar_prefetch=1,
            grid=(windows // wb,),
            in_specs=[block(wb * AREA, MODEL), block(wb, PADDED, 128), whole(oht), block(wb, PADDED, 3 * MODEL),
                  block(wb, PAIRS, 256, PADDED), block(wb, PAIRS, 2, PADDED), whole(wproj), whole(relt), whole(shift),
                  block(wb, PADDED, MODEL), block(wb, PADDED, MODEL), whole(vec), anywhere],
        out_specs=[block(wb, PADDED, 3 * MODEL), fixed(2, 64, 128), anywhere, anywhere, fixed(8, 3 * MODEL), fixed(8, MODEL), fixed(8, MODEL)],
        scratch_shapes=[pltpu.VMEM((wb, PADDED, MODEL), BF16), pltpu.VMEM((wb, PADDED, MODEL), BF16),
                        pltpu.VMEM((MODEL + 16, wb * PADDED), BF16), pltpu.VMEM((MODEL + 16, 4 * MODEL), F32),
                        pltpu.VMEM((2, MODEL, BLOCK), BF16), pltpu.VMEM((2, dp_size // 2, 2, row, BLOCK), BF16),
                        pltpu.SemaphoreType.DMA((2,)), pltpu.SemaphoreType.DMA((2, 2))]),
        out_shape=[jax.ShapeDtypeStruct((windows, PADDED, 3 * MODEL), BF16), jax.ShapeDtypeStruct((2, 64, 128), F32),
                   jax.ShapeDtypeStruct((BLOCKS, dp_size // 2, row, BLOCK), BF16),
                   jax.ShapeDtypeStruct((BLOCKS, dp_size // 2, row, BLOCK), BF16), jax.ShapeDtypeStruct((8, 3 * MODEL), F32),
                   jax.ShapeDtypeStruct((8, MODEL), F32), jax.ShapeDtypeStruct((8, MODEL), F32)],
        cost_estimate=cost(95),
        compiler_params=pltpu.CompilerParams(vmem_limit_bytes=VMEM_LIMIT, dimension_semantics=("arbitrary",)),
        name="attention_backward",
    )(core, da, ohm, oht, qkv, qaug, lse, wproj, relt, shift, xhat, o, vec, wqkv)


def input_kernel(live, x_ref, da_ref, dp_ref, vec_ref, wqkv_ref, *rest):
    gx_ref, wide, tall = rest[-3:]
    wide[0:live * PADDED, :] = mm(dp_ref[0:live].reshape(live * PADDED, 3 * MODEL), wqkv_ref[...], NT)
    for w in range(live):
        tall[AREA * w:AREA * (w + 1), :] = wide[PADDED * w:PADDED * w + AREA, :]
    rows = live * AREA
    for lo in range(0, rows, 112):
        hi = min(lo + 112, rows)
        c, r = norm(x_ref[lo:hi, :].astype(F32))
        xhat = c * r
        dx = tall[lo:hi, :] * vec_ref[LN1_GAIN]
        dx = r * (dx - jnp.mean(dx, axis=-1, keepdims=True) - xhat * jnp.mean(dx * xhat, axis=-1, keepdims=True))
        gx_ref[lo:hi, :] = (dx + da_ref[lo:hi, :].astype(F32)).astype(BF16)


def input_gradient(x, da, dp, vec, wqkv, at, count, x_at, live, held):
    windows = dp.shape[0]
    wb = block_windows(windows)
    part = lambda *shape: pl.BlockSpec(shape, lambda i: (i + at,) + (0,) * (len(shape) - 1))
    extra = [] if held is None else [held]
    return pl.pallas_call(
        functools.partial(input_kernel, live),
        grid=(count,),
        in_specs=[pl.BlockSpec((live * AREA, MODEL), lambda i: (i + x_at, 0)), part(wb * AREA, MODEL), part(wb, PADDED, 3 * MODEL),
                  once(vec), once(wqkv)] + [pl.BlockSpec(memory_space=pl.ANY)] * len(extra),
        out_specs=part(wb * AREA, MODEL),
        out_shape=jax.ShapeDtypeStruct((windows * AREA, MODEL), BF16),
        input_output_aliases={5: 0} if extra else {},
        scratch_shapes=[pltpu.VMEM((wb * PADDED, MODEL), F32), pltpu.VMEM((wb * AREA, MODEL), F32)],
        cost_estimate=cost(6 * count),
        compiler_params=pltpu.CompilerParams(vmem_limit_bytes=VMEM_LIMIT, dimension_semantics=("arbitrary",)),
        name="input_gradient",
    )(x, da, dp, vec, wqkv, *extra)


def constant_tables():
    place = np.arange(PADDED)
    real = place < AREA
    r, c = np.where(real, place // WIN, 0), np.where(real, place % WIN, 0)
    hot = [((WIN - 1 - v)[:, None] == np.arange(16)) & real[:, None] for v in (r, c)]
    keys = np.concatenate(hot + hot, axis=1).astype(np.float32)
    shift = np.stack([(v >> b) & 1 for v in (r, c) for b in (3, 2, 1, 0)]).astype(np.int32)
    return keys, np.concatenate(hot, axis=1).T.astype(np.float32), shift


def key_tables(window_extent):
    keys = constant_tables()[0]
    place = np.arange(PADDED)
    r, c = place // WIN, place % WIN
    valid = (r < window_extent[:, 0:1]) & (c < window_extent[:, 1:2]) & (place < AREA)
    keys = np.concatenate([keys, np.zeros((PADDED, 64), np.float32)], axis=1)
    flag = np.arange(128) == 14
    return jnp.where(flag[None, None, :], jnp.where(valid, 0.0, NEGATIVE)[:, :, None], keys[None]).astype(BF16)


def small_tables(rel_h, rel_w):
    _, oht, shift = constant_tables()
    both = jnp.pad(jnp.stack([rel_h, rel_w]), ((0, 0), (0, 5), (0, 0)))
    hi = both.astype(BF16).astype(F32)
    lo = both - hi
    parity = np.eye(2, dtype=np.float32)
    spread = lambda t: (t[:, None, :, None, :] * parity[None, :, None, :, None]).reshape(128, 128)
    mix = jnp.concatenate([spread(hi), spread(lo)], axis=1).astype(BF16)
    relt = jnp.concatenate([hi.reshape(64, HEAD_DIM), lo.reshape(64, HEAD_DIM)], axis=0).T.astype(BF16)
    return jnp.asarray(oht, BF16), jnp.asarray(shift), mix, relt


def gelu_parts(z):
    u = jnp.abs(z)
    t = 1.0 / (1.0 + 0.23164189 * u)
    e = jnp.exp2(z * (z * -0.72134752))
    poly = t * (0.127414796 + t * (-0.142248368 + t * (0.7107068705 + t * (-0.7265760135 + t * 0.5307027145))))
    q = poly * e
    phi = jnp.where(z >= 0.0, 1.0 - q, q)
    return z * phi, phi + z * e * 0.3989422804


ROWS = 512
CHUNK = 768
SLICES = 4


def mlp_kernel(rows, widths, offset_ref, x1_ref, dy_ref, mask_ref, par_ref, upb_ref, *rest):
    n = len(widths)
    ups, downs = rest[:n], rest[n:2 * n]
    out_ref, da_ref, dw_ref, dbu_ref, vec_ref, h2, dm, h2t, dmt, macc, dacc, accu, accd, zs, das, gs, dzs, stage, sems = rest[2 * n:]
    rb = h2.shape[0]
    ch = 512
    step = pl.program_id(0)

    @pl.when(step == 0)
    def _():
        accu[...] = jnp.zeros_like(accu)
        accd[...] = jnp.zeros_like(accd)
        h2t[MODEL:, :] = jnp.ones((16, h2t.shape[1]), BF16)
        vec_ref[...] = jnp.zeros_like(vec_ref)

    def live(i):
        row = step * rb + i * ch + lax.broadcasted_iota(jnp.int32, (ch, 1), 0)
        return row < rows

    @pl.loop(0, rb // ch)
    def _(i):
        rs = pl.ds(pl.multiple_of(i * ch, ch), ch)
        x1 = jnp.where(live(i), x1_ref[rs, :], 0.0)
        c, r = norm(x1)
        h2[rs, :] = (c * r * par_ref[LN2_GAIN] + par_ref[LN2_BIAS]).astype(BF16)
        d = jnp.where(live(i), dy_ref[rs, :].astype(F32), 0.0)
        dm[rs, :] = d.astype(BF16)
        vec_ref[0:8, :] += fold8(d)

    h2t[0:MODEL, :] = h2[...].T
    dmt[...] = dm[...].T

    chunks, at = [], 0
    for up_ref, down_ref, width in zip(ups, downs, widths):
        size = min(CHUNK, width)
        for lo in range(0, width, size):
            chunks.append((up_ref, down_ref, slice(lo, lo + size), slice(at, at + size)))
            at += size
    count, part = len(chunks), rb // SLICES

    def products(u):
        up_ref, down_ref, here, there = chunks[u // SLICES]
        rs = slice(u % SLICES * part, (u % SLICES + 1) * part)
        zs[u % 2] = mm(h2[rs, :], up_ref[:, here])
        das[u % 2] = mm(dm[rs, :], down_ref[:, here])

    def activate(u):
        there = chunks[u // SLICES][3]
        rs = slice(u % SLICES * part, (u % SLICES + 1) * part)
        g, gp = gelu_parts(zs[u % 2] + upb_ref[:, there])
        dz = (das[u % 2] * gp).astype(BF16)
        gs[u // SLICES % 2, rs, :] = g.astype(BF16)
        dzs[u // SLICES % 2, rs, :] = dz

    def consume(j, i):
        up_ref, down_ref, here, there = chunks[j]
        g, dz = gs.at[j % 2], dzs.at[j % 2]
        if i == 0:
            m = mm(g[...], down_ref[:, here], NT)
            macc[...] = m if j == 0 else macc[...] + m
        if i == 1:
            d = mm(dz[...], up_ref[:, here], NT)
            dacc[...] = d if j == 0 else dacc[...] + d
        if i == 2:
            accd[:, there] += mm(dmt[...], g[...])
        if i == 3:
            accu[:, there] += mm(h2t[...], dz[...])

    units = count * SLICES
    per = 4 // SLICES
    products(0)
    for u in range(units + SLICES):
        if u + 1 < units:
            products(u + 1)
        if u >= SLICES:
            for k in range(per):
                consume(u // SLICES - 1, u % SLICES * per + k)
        if u < units:
            activate(u)

    @pl.loop(0, rb // ch)
    def _(i):
        rs = pl.ds(pl.multiple_of(i * ch, ch), ch)
        x1 = jnp.where(live(i), x1_ref[rs, :], 0.0)
        c, r = norm(x1)
        xhat = c * r
        valid = live(i) & (mask_ref[rs, :] > 0.0)
        out_ref[rs, :] = jnp.where(valid, x1 + macc[rs, :] + par_ref[DOWN_BIAS], 0.0).astype(BF16)
        dh = dacc[rs, :]
        vec_ref[8:16, :] += fold8(dh * xhat)
        vec_ref[16:24, :] += fold8(dh)
        dx = dh * par_ref[LN2_GAIN]
        dx = r * (dx - jnp.mean(dx, axis=-1, keepdims=True) - xhat * jnp.mean(dx * xhat, axis=-1, keepdims=True))
        da = (dx + dm[rs, :].astype(F32)).astype(BF16)
        da_ref[rs, :] = da
        vec_ref[24:32, :] += fold8(da.astype(F32))

    @pl.when(step == pl.num_programs(0) - 1)
    def _():
        size = stage.shape[2]
        dbu_ref[...] = accu[MODEL:MODEL + 8, :]
        each = accu.shape[1] // size

        def copy(k):
            to = pl.multiple_of(offset_ref[k], 128)
            return pltpu.make_async_copy(stage.at[k % 2], dw_ref.at[:, pl.ds(to, size)], sems.at[k % 2])
        for k in range(2 * each):
            if k >= 2:
                copy(k - 2).wait()
            src = (accu, accd)[k // each]
            stage[k % 2] = src[0:MODEL, (k % each) * size:(k % each + 1) * size].astype(BF16)
            copy(k).start()
        copy(2 * each - 2).wait()
        copy(2 * each - 1).wait()


def mlp(x1, dy, mask, par, upb, ups, downs, offsets, live_rows):
    rows, d = x1.shape
    widths = tuple(u.shape[1] for u in ups)
    ff = sum(widths)
    size = 2 * ff // offsets.shape[0]
    rb = ROWS
    full = lambda a: pl.BlockSpec(a.shape, lambda i, _: (0, 0), pipeline_mode=pl.Buffered(1))
    rowspec = lambda w: pl.BlockSpec((rb, w), lambda i, _: (i, 0))
    return pl.pallas_call(
        functools.partial(mlp_kernel, live_rows, widths),
        grid_spec=pltpu.PrefetchScalarGridSpec(
            num_scalar_prefetch=1,
            grid=(pl.cdiv(live_rows, rb),),
            in_specs=[rowspec(d), rowspec(d), rowspec(1)] + [full(a) for a in (par, upb, *ups, *downs)],
            out_specs=[rowspec(d), rowspec(d), pl.BlockSpec(memory_space=pl.ANY),
                       pl.BlockSpec((8, ff), lambda i, _: (0, 0)), pl.BlockSpec((32, d), lambda i, _: (0, 0))],
            scratch_shapes=[pltpu.VMEM((rb, d), BF16), pltpu.VMEM((rb, d), BF16), pltpu.VMEM((d + 16, rb), BF16), pltpu.VMEM((d, rb), BF16),
                            pltpu.VMEM((rb, d), F32), pltpu.VMEM((rb, d), F32), pltpu.VMEM((d + 16, ff), F32), pltpu.VMEM((d, ff), F32),
                            pltpu.VMEM((2, rb // SLICES, CHUNK), F32), pltpu.VMEM((2, rb // SLICES, CHUNK), F32),
                            pltpu.VMEM((2, rb, CHUNK), BF16), pltpu.VMEM((2, rb, CHUNK), BF16), pltpu.VMEM((2, d, size), BF16), pltpu.SemaphoreType.DMA((2,))]),
        out_shape=[jax.ShapeDtypeStruct((rows, d), BF16), jax.ShapeDtypeStruct((rows, d), BF16),
                   jax.ShapeDtypeStruct((d, 2 * ff), BF16), jax.ShapeDtypeStruct((8, ff), F32), jax.ShapeDtypeStruct((32, d), F32)],
        cost_estimate=cost(170),
        compiler_params=pltpu.CompilerParams(vmem_limit_bytes=VMEM_LIMIT, dimension_semantics=("arbitrary",)),
        name="mlp",
    )(offsets, x1, dy, mask, par, upb, *ups, *downs)


GROUP_WIN = 40
SPARE = 2


def bits(n):
    return n.bit_length() - 1


def swap(value, axis, bit, sizes):
    return lax.ppermute(value, axis, [(i, i ^ (1 << bit)) for i in range(sizes[axis])])


def bit_of(axis, bit):
    return (lax.axis_index(axis) >> bit) & 1


def add(a, b):
    return (a.astype(F32) + b.astype(F32)).astype(BF16)


def split_dp(held, at, bit):
    mine = bit_of("dp", bit)
    return tuple(lax.dynamic_index_in_dim(held, m, at, keepdims=False) for m in (mine, 1 - mine))


def split_mlp(held, owners, bit):
    mine = bit_of("mlp", bit) == 1
    sides = []
    for side in range(2):
        runs = [n for n, o in enumerate(owners) if (o >> bit) & 1 == side]
        sides.append(jnp.concatenate([held[n:n + 1] for n in runs], axis=0))
    return jnp.where(mine, sides[1], sides[0]), jnp.where(mine, sides[0], sides[1])


def reduce_steps(keep, send, owners, sizes):
    nb, nm = bits(sizes["dp"]), bits(sizes["mlp"])
    apart = lambda v: v.reshape((v.shape[0],) + (2,) * (nb - 1) + v.shape[2:])
    got = yield [("dp", 0, send)]
    held = apart(add(keep, got[0]))
    orders = ([("mlp", b) for b in reversed(range(nm))] + [("dp", 1)], [("dp", 1)] + [("mlp", b) for b in reversed(range(nm))])
    halves = [held[:, 0], held[:, 1]]
    left = [list(owners), list(owners)]
    dims = [nb - 2, nb - 2]
    plan = list(zip(*orders)) + [(("dp", b), ("dp", b)) for b in range(2, nb - 1)]
    for both in plan:
        kept, sends = [], []
        for n, (axis, bit) in enumerate(both):
            if axis == "mlp":
                keep, send = split_mlp(halves[n], left[n], bit)
                mine = [o for o in left[n] if (o >> bit) & 1 == 0]
                left[n] = [o & ~(1 << bit) for o in mine]
            else:
                keep, send = split_dp(halves[n], dims[n], bit)
                dims[n] -= 1
            kept.append(keep)
            sends.append((axis, bit, send))
        got = yield sends
        halves = [add(k, g) for k, g in zip(kept, got)]
    mine = bit_of("dp", nb - 1) == 1
    got = yield [("dp", nb - 1, jnp.where(mine, halves[0], halves[1]))]
    yield add(jnp.where(mine, halves[1], halves[0]), got[0])


def sum_steps(v, sizes):
    for axis in ("dp", "mlp"):
        for b in range(bits(sizes[axis])):
            got = yield [(axis, b, v)]
            v = v + got[0]
    yield v


def run_steps(tasks, delays, work, sizes):
    states = [next(t) if not d else None for t, d in zip(tasks, delays)]
    results = [None] * len(tasks)
    turn = 0
    while any(r is None for r in results):
        turn += 1
        sends = [(n, s) for n, state in enumerate(states) if isinstance(state, list) for s in state]
        values = work(turn, [s[2] for _, s in sends], [swap_by(s[0], s[1], sizes) for _, s in sends])
        for n, task in enumerate(tasks):
            if isinstance(states[n], list):
                states[n] = task.send([v for v, (owner, _) in zip(values, sends) if owner == n])
                if not isinstance(states[n], list):
                    results[n] = states[n]
            elif results[n] is None and turn >= delays[n]:
                states[n] = next(task)
    return results


def swap_by(axis, bit, sizes):
    return lambda v: swap(v, axis, bit, sizes)


def feed_forward_weights(up, up_bias, down, sizes):
    width = up.shape[1]
    if sizes["mlp"] != 2:
        gather = lambda v: lax.all_gather(v, "mlp", axis=v.ndim - 1, tiled=True)
        count = sizes["mlp"]
        return [gather(up)], [gather(down)], gather(up_bias), jnp.arange(count, dtype=jnp.int32) * width, width
    half = width // 2
    core, me = bit_of("dp", 0), lax.axis_index("mlp")
    cut = lambda v: jnp.where(core == 1, v[:, half:], v[:, :half])
    far_up, far_down = swap(cut(up), "mlp", 0, sizes), swap(cut(down), "mlp", 0, sizes)
    far_bias = swap(up_bias, "mlp", 0, sizes)
    bias = jnp.concatenate([up_bias, jnp.roll(far_bias, -core * half)])
    places = jnp.stack([me * width, me * width + half, (1 - me) * width + core * half, (1 - me) * width + (1 - core) * half])
    return (up, far_up), (down, far_down), bias, places.astype(jnp.int32), half


def per_device(
    sizes,
    tokens,
    window_extent,
    ln1_gain,
    ln1_bias,
    qkv_weight,
    query_bias,
    value_bias,
    rel_h,
    rel_w,
    proj_weight,
    proj_bias,
    ln2_gain,
    ln2_bias,
    up_weight,
    up_bias,
    down_weight,
    down_bias,
    grad_out,
):
    owners = sizes["mlp"]
    line = lambda v: v.reshape(1, -1)
    ups, downs, up_bias_here, places, piece = feed_forward_weights(up_weight, up_bias, down_weight, sizes)
    windows = window_extent.shape[0]
    wb = block_windows(windows)
    blocks = windows // wb
    me = lax.axis_index("mlp")
    share = owners == 2 and 2 * windows == GROUP_WIN
    live = wb - SPARE if share else wb
    live_rows = (windows - wb + live) * AREA
    near, far = (windows - wb) * AREA, (windows - SPARE) * AREA
    oht, shift, mix, relt = small_tables(rel_h, rel_w)
    par = jnp.stack([ln1_gain, ln1_bias, query_bias, value_bias, proj_bias, ln2_gain, ln2_bias, down_bias])
    ohm = key_tables(window_extent)
    weights = (par, qkv_weight, mix, shift, proj_weight)
    if share:
        def taken(v, here, there):
            other = lax.ppermute(v[there:], "mlp", [(0, 1)])
            return jnp.where(me == 0, v[here:here + other.shape[0]], other)
        tail_x, tail_go = taken(tokens, near, far), taken(grad_out, near, far)
        tail_extent = taken(window_extent.astype(F32), windows - wb, windows - SPARE).astype(jnp.int32)
        tail_ohm = key_tables(tail_extent)
        held = attention_forward(tokens, grad_out, ohm, *weights, windows, 0, blocks - 1, wb, None)
        held = attention_forward(tail_x, tail_go, tail_ohm, *weights, windows, blocks - 1, 1, live, held)
        ohm = jnp.concatenate([ohm[:windows - wb], jnp.pad(tail_ohm, ((0, SPARE), (0, 0), (0, 0)))], axis=0)
    else:
        tail_x = tokens
        held = attention_forward(tokens, grad_out, ohm, *weights, windows, 0, blocks, wb, None)
    x1, xhat, qkv, qaug, o, lse, row_mask, dy = held
    if owners == 2:
        (ups, downs, x1) = lax.optimization_barrier((ups, downs, x1))
        ups, downs = list(ups) + [swap(ups[1], "dp", 0, sizes)], list(downs) + [swap(downs[1], "dp", 0, sizes)]
    width = up_weight.shape[1]
    ff = width * owners
    by_owner = (places // width) * (2 * width) + places % width
    output, da, dw_mlp, up_sums, mid_sums = mlp(
        x1, dy, row_mask, par, line(up_bias_here), ups, downs, jnp.concatenate([by_owner, by_owner + width]), live_rows)

    def give_back(v):
        return lax.ppermute(v[near:live_rows], "mlp", [(1, 0)])

    def completed(v, other):
        tail = jnp.where(me == 0, jnp.concatenate([v[near:live_rows], other], axis=0), 0)
        return lax.dynamic_update_slice(v, tail, (near, 0))

    if share:
        output_tail, da = lax.optimization_barrier((output[near:live_rows], da))
        output_back = lax.ppermute(output_tail, "mlp", [(1, 0)])
    dw_mlp = lax.psum_scatter(dw_mlp, "dp", scatter_dimension=0, tiled=True)
    dw_mlp = lax.psum_scatter(dw_mlp, "mlp", scatter_dimension=1, tiled=True)
    dp_all, grel, dw_keep, dw_send, dp_sums, gain_sums, bias_sums = attention_backward(
        da, ohm, oht, qkv, qaug, lse, proj_weight, relt, shift, xhat, o, par, qkv_weight, bit_of("dp", 0).reshape(1).astype(jnp.int32), sizes["dp"], live)
    if share:
        output = completed(output, output_back)
    up_sum = up_sums[0].reshape(-1, piece)
    up_sum = sum(jnp.where(jnp.arange(ff) // piece == places[n] // piece, jnp.tile(up_sum[n], ff // piece), 0.0)
                 for n in range(ff // piece))
    block_owners = [0, 0, 0, 1, 1, 1, 0, 1]
    if owners != 2:
        def regroup(v):
            parts = [jnp.moveaxis(p, 0, 2) for p in (v[:6], v[6:])]
            parts = [p.reshape(p.shape[:2] + (owners, -1)) for p in parts]
            return jnp.moveaxis(jnp.concatenate(parts, axis=3), 2, 0)
        dw_keep, dw_send = regroup(dw_keep), regroup(dw_send)
        block_owners = list(range(owners))
    rel = grel[0, :, :HEAD_DIM] + grel[1, :, HEAD_DIM:]
    mid = jnp.sum(mid_sums.reshape(4, 8, MODEL), axis=1)
    sums = jnp.concatenate([gain_sums[0], bias_sums[0], dp_sums[0], rel.reshape(-1), mid.reshape(-1), up_sum])
    half = (blocks - 1) // 2
    order = [(at, n) for at, n in ((0, half), (half, blocks - 1 - half)) if n] + [(blocks - 1, 1)]
    held = {"gx": None, "da": da, "at": 0}

    def input_part():
        at, count = order[held["at"]]
        last = at == blocks - 1
        held["gx"] = input_gradient(tail_x if last else tokens, held["da"], dp_all, par, qkv_weight, at, count, 0 if share and last else at,
                                    live if last else wb, held["gx"])
        held["at"] += 1

    def work(turn, values, swaps):
        if held["at"] >= len(order):
            return [f(v) for f, v in zip(swaps, values)]
        values, held["da"] = lax.optimization_barrier((values, held["da"]))
        got = [f(v) for f, v in zip(swaps, values)]
        input_part()
        got, held["gx"] = lax.optimization_barrier((got, held["gx"]))
        if share and held["at"] == len(order):
            held["back"] = give_back(held["gx"])
        return got

    tasks = [reduce_steps(dw_keep, dw_send, block_owners, sizes), sum_steps(sums, sizes)]
    delays = [0, 0]
    results = run_steps(tasks, delays, work, sizes)
    late, sums = results[0].astype(F32), results[1]
    late = jnp.concatenate([late[n] for n in range(late.shape[0])], axis=1)
    while held["at"] < len(order):
        input_part()
    grad_tokens = held["gx"]
    if share:
        grad_tokens = completed(grad_tokens, held["back"])
    d = MODEL
    table = 2 * WIN - 1
    n_rel = 64 * HEAD_DIM
    rel = sums[5 * d:5 * d + n_rel].reshape(64, HEAD_DIM)
    mid = sums[5 * d + n_rel:]
    cols = 3 * MODEL // owners
    dw_mlp = dw_mlp.astype(F32)
    return (
        output,
        grad_tokens,
        sums[0:d],
        sums[d:2 * d],
        late[:, :cols],
        sums[2 * d:3 * d],
        sums[4 * d:5 * d],
        rel[0:table],
        rel[32:32 + table],
        late[:, cols:],
        mid[3 * d:4 * d],
        mid[d:2 * d],
        mid[2 * d:3 * d],
        dw_mlp[:, :width],
        mid[4 * d:],
        dw_mlp[:, width:],
        mid[0:d],
    )


def solution(mesh):
    rows = P(("dp", "mlp"), None)
    in_specs = (rows, rows, P(), P(), P(), P(), P(), P(), P(), P(), P(), P(), P(),
                P(None, "mlp"), P("mlp"), P(None, "mlp"), P(), rows)
    block = P("dp", "mlp")
    out_specs = (rows, rows, P(), P(), block, P(), P(), P(), P(), block, P(), P(), P(), block, P(), block, P())
    sizes = {name: mesh.shape[name] for name in ("dp", "mlp")}
    return jax.shard_map(
        functools.partial(per_device, sizes), mesh=mesh, in_specs=in_specs, out_specs=out_specs, check_vma=False)
```
